32 devices in a mesh: dp: 4 (over y, core), fsdp: 8 (over z, x).
Axes of the slice: x: 2, y: 2, z: 4, core: 2. Of those that a mesh axis runs over, the one named last changes fastest.
Arguments:
- tokens: bfloat16 [8192, 768], P(('dp', 'fsdp')), may hold values from -6 to 6
- segment_ids: int32 [32, 256], P(('dp', 'fsdp')), may hold values from 0 to 3, never falling along the last dimension, each value on 1 to 128 neighbouring positions
- neighbours: bfloat16 [256, 128, 768], P(('dp', 'fsdp')), may hold values from -6 to 6
- neighbour_ids: int32 [32, 4, 2], P(('dp', 'fsdp')), may hold values from 0 to 255, as said below
- neighbour_tokens: int32 [256, 128], P(('dp', 'fsdp')), may hold values from 0 to 50256, as said below
- gains_one: bfloat16 [3, 768], P(None, ('dp', 'fsdp')), may hold values from 0.5 to 1.5
- biases_one: bfloat16 [10, 768], P(None, ('dp', 'fsdp')), may hold values from -1 to 1
- w_qkv_one: bfloat16 [768, 2304], P(('dp', 'fsdp')), may hold values from -0.21875 to 0.21875
- w_out_one: bfloat16 [768, 768], P(('dp', 'fsdp')), may hold values from -0.625 to 0.625
- w_cross_q: bfloat16 [768, 768], P(('dp', 'fsdp')), may hold values from -0.21875 to 0.21875
- w_cross_kv: bfloat16 [768, 1536], P(('dp', 'fsdp')), may hold values from -0.21875 to 0.21875
- w_cross_out: bfloat16 [768, 768], P(('dp', 'fsdp')), may hold values from -0.625 to 0.625
- w_up_one: bfloat16 [768, 3072], P(('dp', 'fsdp')), may hold values from -0.21875 to 0.21875
- bias_up_one: bfloat16 [3072], P(('dp', 'fsdp')), may hold values from -1 to 1
- w_down_one: bfloat16 [3072, 768], P(('dp', 'fsdp')), may hold values from -0.109375 to 0.109375
- gains_two: bfloat16 [2, 768], P(None, ('dp', 'fsdp')), may hold values from 0.5 to 1.5
- biases_two: bfloat16 [6, 768], P(None, ('dp', 'fsdp')), may hold values from -1 to 1
- w_qkv_two: bfloat16 [768, 2304], P(('dp', 'fsdp')), may hold values from -0.21875 to 0.21875
- w_out_two: bfloat16 [768, 768], P(('dp', 'fsdp')), may hold values from -0.625 to 0.625
- w_up_two: bfloat16 [768, 3072], P(('dp', 'fsdp')), may hold values from -0.21875 to 0.21875
- bias_up_two: bfloat16 [3072], P(('dp', 'fsdp')), may hold values from -1 to 1
- w_down_two: bfloat16 [3072, 768], P(('dp', 'fsdp')), may hold values from -0.109375 to 0.109375
- cotangent: bfloat16 [8192, 768], P(('dp', 'fsdp')), may hold values from -6 to 6
Outputs:
- out: bfloat16 [8192, 768], P(('dp', 'fsdp'))
- grad_tokens: float32 [8192, 768], P(('dp', 'fsdp'))
- grad_neighbours: float32 [256, 128, 768], P(('dp', 'fsdp'))
- grad_gains_one: float32 [3, 768], P(None, ('dp', 'fsdp'))
- grad_biases_one: float32 [10, 768], P(None, ('dp', 'fsdp'))
- grad_w_qkv_one: float32 [768, 2304], P(('dp', 'fsdp'))
- grad_w_out_one: float32 [768, 768], P(('dp', 'fsdp'))
- grad_w_cross_q: float32 [768, 768], P(('dp', 'fsdp'))
- grad_w_cross_kv: float32 [768, 1536], P(('dp', 'fsdp'))
- grad_w_cross_out: float32 [768, 768], P(('dp', 'fsdp'))
- grad_w_up_one: float32 [768, 3072], P(('dp', 'fsdp'))
- grad_bias_up_one: float32 [3072], P(('dp', 'fsdp'))
- grad_w_down_one: float32 [3072, 768], P(('dp', 'fsdp'))
- grad_gains_two: float32 [2, 768], P(None, ('dp', 'fsdp'))
- grad_biases_two: float32 [6, 768], P(None, ('dp', 'fsdp'))
- grad_w_qkv_two: float32 [768, 2304], P(('dp', 'fsdp'))
- grad_w_out_two: float32 [768, 768], P(('dp', 'fsdp'))
- grad_w_up_two: float32 [768, 3072], P(('dp', 'fsdp'))
- grad_bias_up_two: float32 [3072], P(('dp', 'fsdp'))
- grad_w_down_two: float32 [3072, 768], P(('dp', 'fsdp'))
The draws below stay inside these ranges and needn't reach their ends.
Inputs may be any that keep to these rules, and one draw needn't show every extreme that they name: `segment_ids`: within each row the ids never fall. `neighbour_ids`: the spans of sequence s name, each once, the 8 neighbours stored with that sequence, numbers s * 2 * 4 onward. `neighbour_tokens`: in each neighbour the nonzero ids come first, a quarter of 128 of them or more; zeros after them are padding.
All inputs are finite; a program needn't handle non-finite values.
Results may differ from the reference program's by a relative error of at most 0.023.
Values may be sent and summed in bfloat16 or wider, within the bound.
A program may use at most 256 MiB of HBM per device.

```python
import math
import jax
import jax.numpy as jnp
import numpy as np
from jax import lax

D = 768
HEADS = 12
HEAD_DIM = 64
FF = 3072
VOCAB = 50257
SEQ = 256
SPAN = 64
NLEN = 128
NEAR = 2
SEQS = 32
TOKENS = 8192
SPANS = 4
NEIGH = 256


def draw_neighbour_ids(key, part):
    key = jax.random.fold_in(key, 11)
    block = NEAR * SPANS
    ordered = jnp.tile(jnp.arange(block, dtype=jnp.int32)[None, :], (SEQS, 1))
    shuffled = jax.random.permutation(key, ordered, axis=1, independent=True)
    offsets = (jnp.arange(SEQS, dtype=jnp.int32) * block)[:, None]
    return (shuffled + offsets).astype(jnp.int32).reshape(SEQS, SPANS, NEAR)


def draw_neighbour_tokens(key, part):
    key = jax.random.fold_in(key, 23)
    length_key, token_key = jax.random.split(key)
    lengths = jax.random.randint(length_key, (NEIGH, 1), NLEN // 4, NLEN + 1)
    lengths = lengths.at[0, 0].set(NLEN).at[1, 0].set(NLEN // 4)
    token_ids = jax.random.randint(token_key, (NEIGH, NLEN), 1, VOCAB)
    token_ids = token_ids.at[0, 0].set(VOCAB - 1)
    place = jnp.arange(NLEN, dtype=jnp.int32)[None, :]
    return jnp.where(place < lengths, token_ids, 0).astype(jnp.int32)


def block_scale(key, shape, cuts, least, high):
    gain, own = 1.0, jax.random.fold_in(key, 6)
    for dim, blocks in cuts:
        heights = jnp.exp(jax.random.uniform(jax.random.fold_in(own, dim), (blocks,), jnp.float32, least / len(cuts), high / len(cuts)))
        gain = gain * jnp.repeat(heights, shape[dim] // blocks).reshape([-1 if axis == dim else 1 for axis in range(len(shape))])
    return gain


def profile(count, total, reach, skew):
    weights = [(1 << 20) // math.isqrt(grade ** skew) + 1 for grade in range(2, count + 1)]
    surplus, given = total - reach - (count - 1), [1] * (count - 1)
    while surplus > 0:
        free = [i for i in range(count - 1) if given[i] < reach]
        mass, remaining = sum([weights[i] for i in free]), surplus
        for i in free:
            extra = min(reach - given[i], max(1, remaining * weights[i] // mass), surplus)
            given[i] = given[i] + extra
            surplus = surplus - extra
    return np.array([reach] + given)


def uneven(stream_key, number_of, total, limit, lean):
    if number_of == 2:
        one = jax.random.randint(stream_key, (), max(1, total - limit), min(limit, total - 1) + 1)
        return jnp.stack([one, total - one])
    tallies = jnp.asarray(profile(number_of, total, limit, lean), jnp.int32)
    twos = (number_of - 1) // 2
    source_of, receiver = tallies[1:1 + 2 * twos:2], tallies[2:2 + 2 * twos:2]
    slack = jnp.minimum(source_of - 1, limit - receiver)
    moved = jax.random.randint(jax.random.fold_in(stream_key, 1), (twos,), 0, 1 << 20) % (slack + 1)
    tallies = tallies.at[1:1 + 2 * twos:2].set(source_of - moved).at[2:2 + 2 * twos:2].set(receiver + moved)
    return tallies[jax.random.permutation(jax.random.fold_in(stream_key, 2), number_of)]


def gaussian(stream_key, extent, scale, bound, cuts=(), held_as=jnp.bfloat16):
    factor_of = block_scale(stream_key, extent, cuts, -0.22, 0.18) if cuts else 1.0
    values = jax.random.normal(stream_key, extent, jnp.float32) * scale * factor_of
    return jnp.minimum(jnp.maximum(values, -bound), bound).astype(held_as)


def setup_inputs(seed: int = 0) -> dict:
    streams_of = jax.random.split(jax.random.key(seed), 24)
    tokens = gaussian(streams_of[0], (TOKENS, D), 1.0, 6.0, ((0, 32),))
    segment_ids = jax.vmap(lambda own: jnp.searchsorted(jnp.cumsum(uneven(own, 4, SEQ, SEQ // 2, 1)), jnp.arange(SEQ), side="right"))(jax.random.split(streams_of[1], SEQS)).reshape((SEQS, SEQ)).astype(jnp.int32)
    neighbours = gaussian(streams_of[2], (NEIGH, NLEN, D), 1.0, 6.0, ((0, 32),))
    neighbour_ids = draw_neighbour_ids(jax.random.fold_in(streams_of[23], 71), 0)
    neighbour_tokens = draw_neighbour_tokens(jax.random.fold_in(streams_of[23], 71), 0)
    gains_one = jnp.clip(1.0 + 0.1 * jax.random.normal(streams_of[5], (3, D), jnp.float32), 0.5, 1.5).astype(jnp.bfloat16)
    biases_one = gaussian(streams_of[6], (10, D), 0.2, 1.0, ((1, 32),))
    w_qkv_one = gaussian(streams_of[7], (D, 3 * D), D ** -0.5, 0.21875, ((0, 32),))
    w_out_one = gaussian(streams_of[8], (D, D), (D // 8) ** -0.5, 0.625, ((0, 32),))
    w_cross_q = gaussian(streams_of[9], (D, D), D ** -0.5, 0.21875, ((0, 32),))
    w_cross_kv = gaussian(streams_of[10], (D, 2 * D), D ** -0.5, 0.21875, ((0, 32),))
    w_cross_out = gaussian(streams_of[11], (D, D), (D // 8) ** -0.5, 0.625, ((0, 32),))
    w_up_one = gaussian(streams_of[12], (D, FF), D ** -0.5, 0.21875, ((0, 32),))
    bias_up_one = gaussian(streams_of[13], (FF,), 0.2, 1.0, ((0, 32),))
    w_down_one = gaussian(streams_of[14], (FF, D), FF ** -0.5, 0.109375, ((0, 32),))
    gains_two = jnp.clip(1.0 + 0.1 * jax.random.normal(streams_of[15], (2, D), jnp.float32), 0.5, 1.5).astype(jnp.bfloat16)
    biases_two = gaussian(streams_of[16], (6, D), 0.2, 1.0, ((1, 32),))
    w_qkv_two = gaussian(streams_of[17], (D, 3 * D), D ** -0.5, 0.21875, ((0, 32),))
    w_out_two = gaussian(streams_of[18], (D, D), (D // 8) ** -0.5, 0.625, ((0, 32),))
    w_up_two = gaussian(streams_of[19], (D, FF), D ** -0.5, 0.21875, ((0, 32),))
    bias_up_two = gaussian(streams_of[20], (FF,), 0.2, 1.0, ((0, 32),))
    w_down_two = gaussian(streams_of[21], (FF, D), FF ** -0.5, 0.109375, ((0, 32),))
    cotangent = gaussian(streams_of[22], (TOKENS, D), 1.0, 6.0, ((0, 32),))
    return {"tokens": tokens, "segment_ids": segment_ids, "neighbours": neighbours, "neighbour_ids": neighbour_ids, "neighbour_tokens": neighbour_tokens, "gains_one": gains_one, "biases_one": biases_one, "w_qkv_one": w_qkv_one, "w_out_one": w_out_one, "w_cross_q": w_cross_q, "w_cross_kv": w_cross_kv, "w_cross_out": w_cross_out, "w_up_one": w_up_one, "bias_up_one": bias_up_one, "w_down_one": w_down_one, "gains_two": gains_two, "biases_two": biases_two, "w_qkv_two": w_qkv_two, "w_out_two": w_out_two, "w_up_two": w_up_two, "bias_up_two": bias_up_two, "w_down_two": w_down_two, "cotangent": cotangent}


@jax.custom_vjp
def low(v):
    return lax.optimization_barrier(v.astype(jnp.bfloat16)).astype(jnp.float32)

@jax.custom_vjp
def low_back(v):
    return v

def low_keep(v):
    return (low(v), None)

def low_pass(kept, grad):
    return (grad,)

def back_keep(v):
    return (v, None)

def back_low(kept, grad):
    return (low(grad),)
low.defvjp(low_keep, low_pass)
low_back.defvjp(back_keep, back_low)

def matmul(left, right):
    return jnp.dot(left, right, precision=lax.Precision.HIGHEST)

def layer_norm(hidden, norm_gain, norm_bias):
    centred = hidden - lax.optimization_barrier(jnp.mean(hidden, axis=-1, keepdims=True))
    spread = lax.optimization_barrier(jnp.mean(centred * centred, axis=-1, keepdims=True))
    return centred * lax.rsqrt(spread + 1e-05) * norm_gain + norm_bias

def self_attention(normed, w_packed, bias_query, bias_value, w_output, bias_output, allowed):
    score_scale = HEAD_DIM ** (-0.5)
    packed_bias = jnp.concatenate([bias_query, jnp.zeros_like(bias_query), bias_value])
    packed = low(low_back(matmul(normed, w_packed) + packed_bias)).reshape(SEQ, 3, HEADS, HEAD_DIM)
    scores = low_back(jnp.einsum('qhe,khe->hqk', packed[:, 0], packed[:, 1], precision=lax.Precision.HIGHEST) * score_scale)
    scores = jnp.where(allowed[None], scores, -1e+30)
    attn_probs = low(jax.nn.softmax(scores, axis=-1))
    mixed_heads = jnp.einsum('hqk,khe->qhe', attn_probs, packed[:, 2], precision=lax.Precision.HIGHEST)
    mixed_heads = low(low_back(mixed_heads)).reshape(SEQ, D)
    return low_back(matmul(mixed_heads, w_output) + bias_output)

def cross_attention(normed, near_rows, near_valid, w_query, bias_query, w_pair, bias_value, w_output, bias_output):
    score_scale = HEAD_DIM ** (-0.5)
    queries = low(low_back(matmul(normed, w_query) + bias_query)).reshape(SPANS, SPAN, HEADS, HEAD_DIM)
    pair_bias = jnp.concatenate([jnp.zeros_like(bias_value), bias_value])
    key_value = matmul(near_rows.reshape(SPANS * NEAR * NLEN, D), w_pair) + pair_bias
    key_value = low(low_back(key_value)).reshape(SPANS, NEAR * NLEN, 2, HEADS, HEAD_DIM)
    scores = low_back(jnp.einsum('cqhe,ckhe->chqk', queries, key_value[:, :, 0], precision=lax.Precision.HIGHEST) * score_scale)
    scores = jnp.where(near_valid[:, None, None, :], scores, -1e+30)
    attn_probs = low(jax.nn.softmax(scores, axis=-1))
    mixed_heads = jnp.einsum('chqk,ckhe->cqhe', attn_probs, key_value[:, :, 1], precision=lax.Precision.HIGHEST)
    mixed_heads = low(low_back(mixed_heads)).reshape(SEQ, D)
    return low_back(matmul(mixed_heads, w_output) + bias_output)

def feed_forward(normed, w_up, bias_up, w_down, bias_down):
    hidden = low_back(matmul(normed, w_up) + bias_up)
    active = low(jax.nn.gelu(hidden, approximate=True))
    return low_back(matmul(active, w_down) + bias_down)

def layer_pair(state, near_store, weights, segments, near_ids, near_tokens):
    gains_a, biases_a, w_qkv_a, w_out_a, w_query_c, w_pair_c, w_out_c, w_up_a, bias_up_a, w_down_a, gains_b, biases_b, w_qkv_b, w_out_b, w_up_b, bias_up_b, w_down_b = weights
    near_index = near_ids.reshape(-1)
    near_rows = jnp.take(near_store, near_index, axis=0).reshape(SPANS, NEAR * NLEN, D)
    near_valid = (jnp.take(near_tokens, near_index, axis=0) != 0).reshape(SPANS, NEAR * NLEN)
    position = jnp.arange(SEQ)
    allowed = (position[:, None] >= position[None, :]) & (segments[:, None] == segments[None, :])
    state = state + self_attention(low(layer_norm(state, gains_a[0], biases_a[0])), w_qkv_a, biases_a[3], biases_a[4], w_out_a, biases_a[5], allowed)
    state = state + cross_attention(low(layer_norm(state, gains_a[1], biases_a[1])), near_rows, near_valid, w_query_c, biases_a[6], w_pair_c, biases_a[7], w_out_c, biases_a[8])
    state = state + feed_forward(low(layer_norm(state, gains_a[2], biases_a[2])), w_up_a, bias_up_a, w_down_a, biases_a[9])
    state = state + self_attention(low(layer_norm(state, gains_b[0], biases_b[0])), w_qkv_b, biases_b[2], biases_b[3], w_out_b, biases_b[4], allowed)
    state = state + feed_forward(low(layer_norm(state, gains_b[1], biases_b[1])), w_up_b, bias_up_b, w_down_b, biases_b[5])
    return state

def reference(tokens, segment_ids, neighbours, neighbour_ids, neighbour_tokens, gains_one, biases_one, w_qkv_one, w_out_one, w_cross_q, w_cross_kv, w_cross_out, w_up_one, bias_up_one, w_down_one, gains_two, biases_two, w_qkv_two, w_out_two, w_up_two, bias_up_two, w_down_two, cotangent):
    params = tuple((value.astype(jnp.float32) for value in (gains_one, biases_one, w_qkv_one, w_out_one, w_cross_q, w_cross_kv, w_cross_out, w_up_one, bias_up_one, w_down_one, gains_two, biases_two, w_qkv_two, w_out_two, w_up_two, bias_up_two, w_down_two)))
    group = max((count for count in (1, 2, 4, 8) if SEQS % count == 0 and count * SEQ <= 4096))
    rounds = SEQS // group
    per_seq = NEAR * SPANS
    inputs = (tokens.astype(jnp.float32).reshape(rounds, group, SEQ, D), segment_ids.reshape(rounds, group, SEQ), neighbours.astype(jnp.float32).reshape(rounds, group, per_seq, NLEN, D), (neighbour_ids % per_seq).astype(jnp.int32).reshape(rounds, group, SPANS, NEAR), neighbour_tokens.reshape(rounds, group, per_seq, NLEN), cotangent.astype(jnp.float32).reshape(rounds, group, SEQ, D))

    def step(totals, batch):
        states, segments, near_store, near_ids, near_tokens, grad_out = batch

        def run(state_in, near_in, weights):

            def single(state_one, near_one, segment_one, ids_one, tokens_one):
                return layer_pair(state_one, near_one, weights, segment_one, ids_one, tokens_one)
            return jax.vmap(single)(state_in, near_in, segments, near_ids, near_tokens)
        result, pullback = jax.vjp(run, states, near_store, params)
        grad_states, grad_near, grad_params = pullback(grad_out)
        return (jax.tree.map(jnp.add, totals, grad_params), (result.astype(jnp.bfloat16), grad_states, grad_near))
    zeros = jax.tree.map(jnp.zeros_like, params)
    sums, (outputs, grad_states, grad_near) = lax.scan(step, zeros, inputs)
    return (outputs.reshape(TOKENS, D), grad_states.reshape(TOKENS, D), grad_near.reshape(NEIGH, NLEN, D), sums[0], sums[1], sums[2], sums[3], sums[4], sums[5], sums[6], sums[7], sums[8], sums[9], sums[10], sums[11], sums[12], sums[13], sums[14], sums[15], sums[16])
```

```python
import functools
import itertools
import math
import types
import jax
import jax.numpy as jnp
from jax import lax
from jax.experimental import pallas as pl
from jax.experimental.pallas import tpu as pltpu
from jax.sharding import PartitionSpec as P

HEADS = 12
HEAD_DIM = 64
MESH = pl.DeviceIdType.MESH
ROUTES = ((("z", "x", "y"), 1), (("z", "y", "x"), 1), (("x", "z", "y"), 2), (("y", "z", "x"), 2))
NAMES = ("y", "c", "z", "x")
GATHER_STEPS = (0, 1, 2, 3, 4, 6, 8)
VMEM_MOST = 63 * 2 ** 20
COMPUTE_SHARE, CHAIN_SHARE = 3.5, 3.0
SCATTER_STEPS = (0, 2, 4, 5, 6, 7, 8)
LANDINGS, WINDOW = 6, 8


class Place:
    def __init__(self, dp_size, fsdp_size):
        dp, fsdp = lax.axis_index("dp"), lax.axis_index("fsdp")
        self.size = {"y": dp_size // 2, "c": 2, "z": fsdp_size // 2, "x": 2}
        self.at = {"y": dp // 2, "c": lax.rem(dp, 2), "z": fsdp // 2, "x": lax.rem(fsdp, 2)}

    def device(self, axis, index):
        at = dict(self.at)
        at[axis] = index
        return (at["y"] * 2 + at["c"], at["z"] * 2 + at["x"])

    def partners(self):
        found = []
        for axis in ("c", "x", "y", "z"):
            n, p = self.size[axis], self.at[axis]
            if n == 2:
                found.append((self.device(axis, 1 - p), None))
            elif n > 2:
                found.append((self.device(axis, p + 1), p + 1 < n))
                found.append((self.device(axis, p - 1), p > 0))
        return found


def greet(place):
    barrier = pltpu.get_barrier_semaphore()
    expected = 0
    for device, condition in place.partners():
        if condition is None:
            pl.semaphore_signal(barrier, inc=1, device_id=device, device_id_type=MESH)
            expected = expected + 1
        else:
            @pl.when(condition)
            def _(device=device):
                pl.semaphore_signal(barrier, inc=1, device_id=device, device_id_type=MESH)
            expected = expected + condition.astype(jnp.int32)
    pl.semaphore_wait(barrier, expected)


def when(condition, action):
    if condition is None:
        action()
    else:
        pl.when(condition)(action)


class Sems:
    def __init__(self, send, recv):
        self.send, self.recv, self.used, self.sent = send, recv, 0, []

    def take(self):
        self.used += 1
        return self.used - 1

    def copy(self, slot, src, dst, device):
        return pltpu.make_async_remote_copy(
            src_ref=src, dst_ref=dst, send_sem=self.send.at[slot], recv_sem=self.recv.at[slot],
            device_id=device, device_id_type=MESH)

    def start(self, slot, src, dst, device, condition=None):
        copy = self.copy(slot, src, dst, device)
        when(condition, copy.start)
        self.sent.append((copy, condition))

    def arrived(self, slot, dst, device, condition=None):
        when(condition, self.copy(slot, dst, dst, device).wait_recv)

    def drain(self):
        for copy, condition in self.sent:
            when(condition, copy.wait_send)


def run_schedule(groups, offsets, after=None):
    for tick in range(len(groups) + offsets[-1]):
        for k, group in enumerate(groups):
            if tick - k in offsets:
                for flow in group:
                    next(flow, None)
        if after is not None:
            after(tick)


def routes(width):
    if width % 768:
        return [(ROUTES[0][0], 0, width)]
    found, start = [], 0
    for order, share in ROUTES:
        found.append((order, start, share * width // 6))
        start += share * width // 6
    return found


def copies_of(order, size):
    return 1 + sum(1 if size[d] == 2 else 2 * (size[d] - 1) for d in order)


def gather_flow(place, sems, ref, order, row, height, col, width):
    part = (pl.ds(row, height), pl.ds(col, width))

    def block(done, **fixed):
        where = []
        for name in NAMES:
            if name in fixed:
                where.append(fixed[name])
            elif name in done:
                where.append(pl.ds(0, place.size[name]))
            else:
                where.append(place.at[name])
        return ref.at[(*where, *part)]

    c = place.at["c"]
    sibling = place.device("c", 1 - c)
    done, crossed = set(), []

    def cross(**fixed):
        slot, mine = sems.take(), block(done, c=c, **fixed)
        sems.start(slot, mine, mine, sibling)
        crossed.append((slot, block(done, c=1 - c, **fixed)))

    for axis in order:
        n, p = place.size[axis], place.at[axis]
        final = axis == order[-1]
        if n == 2:
            slot, other = sems.take(), place.device(axis, 1 - p)
            mine = block(done, **{axis: p})
            sems.start(slot, mine, mine, other)
            if final:
                cross(**{axis: p})
            yield
            sems.arrived(slot, block(done, **{axis: 1 - p}), other)
            if final:
                cross(**{axis: 1 - p})
        else:
            for step in range(n - 1):
                up, down = sems.take(), sems.take()
                above, below = place.device(axis, p + 1), place.device(axis, p - 1)
                sent = block(done, **{axis: jnp.maximum(p - step, 0)})
                sems.start(up, sent, sent, above, (p - step >= 0) & (p + 1 < n))
                sent = block(done, **{axis: jnp.minimum(p + step, n - 1)})
                sems.start(down, sent, sent, below, (p + step < n) & (p > 0))
                yield
                sems.arrived(up, block(done, **{axis: jnp.maximum(p - 1 - step, 0)}), above, p - 1 - step >= 0)
                sems.arrived(down, block(done, **{axis: jnp.minimum(p + 1 + step, n - 1)}), below, p + 1 + step < n)
            done.add(axis)
            if final:
                cross()
            continue
        done.add(axis)
    yield
    for slot, theirs in crossed:
        sems.arrived(slot, theirs, sibling)


def pack_small(parts, ups):
    rows = [jnp.pad(ref[...].astype(jnp.float32), ((0, 0), (0, 128 - ref.shape[1]))) for ref in (*parts, *ups)]
    rows = jnp.concatenate(rows, axis=0)
    return jnp.pad(rows, ((0, -rows.shape[0] % 32), (0, 0))).astype(jnp.bfloat16)


def add_blocks(lead, result, *terms):
    def body(where):
        kind = F32 if isinstance(result, list) else result.dtype
        total = terms[0][where].astype(kind)
        for term in terms[1:]:
            total = total + term[where].astype(kind)
        if isinstance(result, list):
            result[where[0]][...] = total
        else:
            result[where] = total

    for index in itertools.product(*map(range, lead)):
        body((*index, slice(None), slice(None)))


def scatter_buffers(size, order, block):
    dims, found = [name for name in NAMES if name != "c"], []
    for axis in order:
        dims = [name for name in dims if name != axis]
        lead = tuple(size[name] for name in dims)
        found.append((() if size[axis] == 2 else (2 * size[axis] - 2,)) + lead + block)
    return found


def scatter_flow(place, sems, sums, buffers, order, out, parts):
    dims = [name for name in NAMES if name != "c"]
    leaving = []

    def leave(slot, src, dst, device, condition=None):
        copy = sems.copy(slot, src, dst, device)
        when(condition, copy.start)
        leaving.append((copy, condition))

    def settle():
        while leaving:
            copy, condition = leaving.pop()
            when(condition, copy.wait_send)

    for axis, buffer in zip(order, buffers):
        n, p = place.size[axis], place.at[axis]
        spot = dims.index(axis)
        rest = [name for name in dims if name != axis]
        lead = tuple(place.size[name] for name in rest) + parts
        last = not rest

        def at(index, sums=sums, spot=spot, count=len(dims)):
            where = [slice(None)] * (count + 3)
            where[spot] = index
            return sums.at[tuple(where)]

        if n == 2:
            slot, other = sems.take(), place.device(axis, 1 - p)
            leave(slot, at(1 - p), buffer, other)
            yield
            sems.arrived(slot, buffer, other)
            settle()
            add_blocks(lead, out if last else buffer, buffer, at(p))
            sums = buffer
        else:
            above, below = place.device(axis, p + 1), place.device(axis, p - 1)
            q = n - 1 - p
            ups = [sems.take() for _ in range(n - 1)]
            downs = [sems.take() for _ in range(n - 1)]

            def from_below(block):
                return buffer.at[jnp.maximum(block - 1, 0)]

            def from_above(block):
                return buffer.at[jnp.minimum(n - 1 + block, 2 * n - 3)]
            for step in range(n - 1):
                up = jnp.minimum(n - 1 - step + p, n - 1)
                down = jnp.maximum(step - q, 0)
                if step:
                    def pass_up(up=up, step=step):
                        sems.copy(ups[step - 1], from_below(up), from_below(up), above).wait_recv()
                        add_blocks(lead, at(up), at(up), from_below(up))
                    def pass_down(down=down, step=step):
                        sems.copy(downs[step - 1], from_above(down), from_above(down), below).wait_recv()
                        add_blocks(lead, at(down), at(down), from_above(down))
                    pl.when((step >= p) & (p > 0) & (p < n - 1))(pass_up)
                    pl.when((step >= q) & (q > 0) & (q < n - 1))(pass_down)
                leave(ups[step], at(up), from_below(up), above, (step >= p) & (p < n - 1))
                leave(downs[step], at(down), from_above(down), below, (step >= q) & (p > 0))
                yield
            sems.arrived(ups[n - 2], from_below(p), above, p > 0)
            sems.arrived(downs[n - 2], from_above(p), below, p < n - 1)
            settle()
            result = out if last else at(p)
            pl.when(p == 0)(lambda: add_blocks(lead, result, at(p), from_above(p)))
            pl.when(p == n - 1)(lambda: add_blocks(lead, result, at(p), from_below(p)))
            pl.when((p > 0) & (p < n - 1))(
                lambda: add_blocks(lead, result, at(p), from_below(p), from_above(p)))
            sums = at(p)
        dims = rest


def split_kernel(D, *refs):
    one, up_one, down_one, two, up_two, down_two, small, near_in, ids = refs[:9]
    (gains_a, biases_a, qkv_a, out_a, cross_q, cross_kv, cross_out, g_up_a, bias_up_a, g_down_a,
     gains_b, biases_b, qkv_b, out_b, g_up_b, bias_up_b, g_down_b, near, sems) = refs[9:]
    copies = [pltpu.make_async_copy(near_in.at[j], near.at[ids[j]], sems.at[j]) for j in range(near.shape[0])]
    for copy in copies:
        copy.start()
    for src, dst in (
            (one[:, 0:3 * D], qkv_a), (one[:, 3 * D:4 * D], out_a), (one[:, 4 * D:5 * D], cross_q),
            (one[:, 5 * D:7 * D], cross_kv), (one[:, 7 * D:8 * D], cross_out), (up_one[...], g_up_a), (down_one[...], g_down_a),
            (two[:, 0:3 * D], qkv_b), (two[:, 3 * D:4 * D], out_b), (up_two[...], g_up_b), (down_two[...], g_down_b)):
        dst[...] = src
    start = 0
    for ref in (gains_a, biases_a, gains_b, biases_b, bias_up_a, bias_up_b):
        ref[...] = small[start:start + ref.shape[0], :ref.shape[1]]
        start += ref.shape[0]
    for copy in copies:
        copy.wait()


def split_gradients(owned, near, near_index, D, quarter, part):
    rows = owned[2].shape[0]
    shapes = [(3, part), (10, part), (part, 3 * D), (part, D), (part, D), (part, 2 * D), (part, D), (part, quarter * D),
              (1, quarter * part), (rows, D), (2, part), (6, part), (part, 3 * D), (part, D), (part, quarter * D),
              (1, quarter * part), (rows, D), near.shape]
    vmem, hbm = pl.BlockSpec(memory_space=pltpu.VMEM), pl.BlockSpec(memory_space=pl.ANY)
    return pl.pallas_call(
        functools.partial(split_kernel, D),
        out_shape=[jax.ShapeDtypeStruct(shape, jnp.float32) for shape in shapes],
        in_specs=[vmem] * 8 + [pl.BlockSpec(memory_space=pltpu.SMEM)],
        out_specs=[vmem] * 17 + [hbm],
        scratch_shapes=[pltpu.SemaphoreType.DMA((near.shape[0],))],
        compiler_params=pltpu.CompilerParams(vmem_limit_bytes=VMEM_MOST),
        name="split_gradients",
    )(*owned, near, near_index)


F32, BF16 = jnp.float32, jnp.bfloat16
SCALE = HEAD_DIM ** (-0.5)
NN, NT = (((1,), (0,)), ((), ())), (((1,), (1,)), ((), ()))
GELU_ONE, GELU_TWO = (2.0 / 3.141592653589793) ** 0.5, 0.044715


def dot(left, right, dims=NN):
    return lax.dot_general(left, right, dims, preferred_element_type=F32)


def span_of(index, width):
    return pl.ds(pl.multiple_of(index * width, width), width)


def row_blocks(count, action, block=64):
    pl.loop(0, count // block)(lambda i: action(span_of(i, block)))


def normalise(h):
    centred = h - jnp.mean(h, axis=-1, keepdims=True)
    inverse = lax.rsqrt(jnp.mean(centred * centred, axis=-1, keepdims=True) + 1e-05)
    return centred * inverse, inverse


def fill_allowed(allowed, segments):
    shape = allowed.shape
    of_key = jnp.broadcast_to(segments[...].astype(F32), shape)
    above = lax.broadcasted_iota(jnp.int32, shape, 0) >= lax.broadcasted_iota(jnp.int32, shape, 1)
    allowed[...] = (above & (of_key.T == of_key)).astype(jnp.int32)


def norm_forward(h_ref, n_ref, gain, shift):
    def block(rows):
        xhat, _ = normalise(h_ref[rows, :].astype(F32))
        n_ref[rows, :] = (xhat * gain + shift).astype(BF16)
    row_blocks(h_ref.shape[0], block)


def norm_backward(h_ref, gain, gn_ref, g_ref, vec_ref, gain_row, shift_row):
    width = h_ref.shape[1]

    def block(i, sums):
        rows = span_of(i, 64)
        xhat, inverse = normalise(h_ref[rows, :].astype(F32))
        gn = gn_ref[rows, :]
        product = gn * xhat
        scaled = gn * gain
        inner = jnp.mean(scaled * xhat, axis=-1, keepdims=True)
        g_ref[rows, :] += inverse * (scaled - jnp.mean(scaled, axis=-1, keepdims=True) - xhat * inner)
        return sums[0] + jnp.sum(product, axis=0, keepdims=True), sums[1] + jnp.sum(gn, axis=0, keepdims=True)
    zero = jnp.zeros((1, width), F32)
    of_gain, of_shift = lax.fori_loop(0, h_ref.shape[0] // 64, block, (zero, zero))
    vec_ref[gain_row:gain_row + 1, :] = of_gain
    vec_ref[shift_row:shift_row + 1, :] = of_shift


def column_sum(values):
    return jnp.sum(values.astype(F32), axis=0, keepdims=True)


def weight_gradient(dst_ref, left_ref, right_ref, tile):
    wide = right_ref.shape[1]

    def block(i):
        rows = span_of(i, 256)
        turned = left_ref[:, rows].T
        for start in range(0, wide, tile):
            dst_ref[rows, start:start + tile] = dot(turned, right_ref[:, start:start + tile]).astype(BF16)
    pl.loop(0, left_ref.shape[1] // 256)(block)


def both_heads(pair, low_half):
    none = jnp.zeros_like(pair)
    return jnp.concatenate([jnp.where(low_half, pair, none), jnp.where(low_half, none, pair)], axis=0)


def of_both(stacked, low_half):
    rows = stacked.shape[0] // 2
    return jnp.where(low_half, stacked[:rows], stacked[rows:])


def lane_half(rows):
    return lax.broadcasted_iota(jnp.int32, (rows, 2 * HEAD_DIM), 1) < HEAD_DIM


def attend(q, k, v, seen):
    low = lane_half(q.shape[0])
    scores = jnp.where(seen, dot(both_heads(q, low), k, NT) * SCALE, -1e30)
    top = jnp.max(scores, axis=-1, keepdims=True)
    raised = jnp.exp(scores - top)
    total = jnp.sum(raised, axis=-1, keepdims=True)
    mixed = dot((raised / total).astype(BF16), v)
    return of_both(mixed, low), top + jnp.log(total)


def attend_back(q, k, v, seen, logsum, gm):
    low = lane_half(q.shape[0])
    q2, gm2 = both_heads(q, low), both_heads(gm, low)
    scores = jnp.where(seen, dot(q2, k, NT) * SCALE, -1e30)
    probs = jnp.exp(scores - logsum)
    grad_probs = dot(gm2, v, NT)
    grad_v = dot(probs.astype(BF16).T, gm2)
    inner = jnp.sum(probs * grad_probs, axis=-1, keepdims=True)
    grad_scores = (probs * (grad_probs - inner)).astype(BF16)
    grad_q = of_both(dot(grad_scores, k), low) * SCALE
    grad_k = dot(grad_scores.T, q2) * SCALE
    return grad_q, grad_k, grad_v


def gelu_both(x):
    square = x * x
    bent = jnp.tanh(GELU_ONE * x * (1.0 + GELU_TWO * square))
    half = 0.5 * (1.0 + bent)
    slope = half + 0.5 * x * (1.0 - bent * bent) * (GELU_ONE * (1.0 + 3.0 * GELU_TWO * square))
    return x * half, slope


def linear(out_ref, left_ref, w_ref, first, count, tile, bias=None):
    def block(j):
        value = dot(left_ref[...], w_ref[:, pl.ds(pl.multiple_of(first + j * tile, 128), tile)])
        if bias is not None:
            value = value + bias(j)
        out_ref[:, span_of(j, tile)] = value.astype(out_ref.dtype)
    pl.loop(0, count // tile)(block)


def self_forward(e, i, h_in, h_out, w, gain, shift, bq, bv, bo, norm):
    D = h_in.shape[1]
    n, packed, mixed, logsum = e.n.at[norm], e.packed.at[i], e.mixed.at[i], e.logsum.at[i]
    norm_forward(h_in, n, gain, shift)
    zero = jnp.zeros_like(bq)

    def bias(j):
        return jnp.where(j == 0, bq, jnp.where(j == 2, bv, zero))
    linear(packed, n, w, 0, 3 * D, D, bias)
    seen = e.allowed[...] != 0
    seen = jnp.concatenate([seen, seen], axis=0)
    for p in range(D // 128):
        a = p * 128
        value, sums = attend(packed[:, a:a + 128], packed[:, D + a:D + a + 128], packed[:, 2 * D + a:2 * D + a + 128], seen)
        mixed[:, a:a + 128] = value.astype(BF16)
        logsum[:, p:p + 1] = sums
    h_out[...] = h_in[...].astype(F32) + dot(mixed[...], w[:, 3 * D:4 * D]) + bo


def cross_pairs(e):
    neighbours, keys = e.near.shape[0], e.near.shape[1]
    spans = e.spans
    return spans, neighbours // spans * keys, e.queries.shape[0] // spans


def cross_seen(e, span):
    near = e.near.shape[0] // e.spans
    return jnp.concatenate([e.near_tokens[pl.ds(span * near + j, 1), :] for j in range(near)], axis=1) != 0


def cross_keys(e, w, bv):
    D = e.near.shape[2]
    near = e.near

    def rows(i):
        for j in range(2):
            value = dot(near[2 * i:2 * i + 2].reshape(-1, D) if isinstance(i, int) else near[pl.ds(2 * i, 2)].reshape(-1, D),
                        w[:, D + j * D:2 * D + j * D])
            if j == 1:
                value = value + bv
            e.kv[span_of(i, 2 * near.shape[1]), j * D:(j + 1) * D] = value.astype(BF16)
    pl.loop(0, near.shape[0] // 2)(rows)


def cross_forward(e, h_in, h_out, w, gain, shift, bq, bo):
    D = h_in.shape[1]
    n, queries, kv, mixed, logsum = e.n.at[1], e.queries, e.kv, e.mixed.at[2], e.logsum.at[2]
    norm_forward(h_in, n, gain, shift)
    linear(queries, n, w, 0, D, D, lambda j: bq)
    spans, keys, size = cross_pairs(e)

    def span(c):
        rows, krows = span_of(c, size), span_of(c, keys)
        seen = cross_seen(e, c)
        for p in range(D // 128):
            a = p * 128
            value, sums = attend(queries[rows, a:a + 128], kv[krows, a:a + 128], kv[krows, D + a:D + a + 128], seen)
            mixed[rows, a:a + 128] = value.astype(BF16)
            logsum[span_of(c, 2 * size), p:p + 1] = sums
    pl.loop(0, spans)(span)
    h_out[...] = h_in[...] + dot(mixed[...], w[:, 3 * D:4 * D]) + bo


def ffn_forward(e, i, h_in, w_up, w_down, gain, shift, b_up, bd, norm, write):
    D, FF = h_in.shape[1], w_up.shape[1]
    n, slope, active, total = e.n.at[norm], e.slope.at[i], e.active.at[i], e.gn
    norm_forward(h_in, n, gain, shift)

    def up(j):
        cols = span_of(j, D)
        value = dot(n[...], w_up[:, cols]) + b_up[:, cols]
        raised, bent = gelu_both(value)
        active[:, cols] = raised.astype(BF16)
        slope[:, cols] = bent
    pl.loop(0, FF // D)(up)
    total[...] = h_in[...] + bd

    def down(j):
        rows = span_of(j, D)
        total[...] += dot(active[:, rows], w_down[rows, :])
    pl.loop(0, FF // D)(down)
    write(total)


def ffn_backward(e, i, h_in, w_up, w_down, gain, norm, rows, b_row):
    D, FF = h_in.shape[1], w_up.shape[1]
    n, slope, active = e.n.at[norm], e.slope.at[i], e.active.at[i]
    g, gb, gh, gn, vec = e.g, e.gb, e.gh, e.gn, e.vec
    gb[...] = g[...].astype(BF16)
    vec[rows[2]:rows[2] + 1, :] = column_sum(gb[...])

    def hidden(j):
        cols = span_of(j, D)
        value = (dot(gb[...], w_down[cols, :], NT) * slope[:, cols].astype(F32)).astype(BF16)
        gh[:, cols] = value
        e.vec_up[i:i + 1, cols] = column_sum(value)
    pl.loop(0, FF // D)(hidden)
    gn[...] = jnp.zeros_like(gn)

    def back(j):
        cols = span_of(j, D)
        gn[...] += dot(gh[:, cols], w_up[:, cols], NT)
    pl.loop(0, FF // D)(back)
    weight_gradient(w_down, active, gb, D)
    e.ship(b_row)
    weight_gradient(w_up, n, gh, D)
    e.ship(b_row + 1)
    norm_backward(h_in, gain, gn, g, vec, rows[0], rows[1])


def self_backward(e, i, h_in, w, gain, norm, rows, ship):
    D = h_in.shape[1]
    n, packed, mixed, logsum = e.n.at[norm], e.packed.at[i], e.mixed.at[i], e.logsum.at[i]
    g, gb, gmix, gpacked, gn, vec = e.g, e.gb, e.gmix, e.gpacked, e.gn, e.vec
    gb[...] = g[...].astype(BF16)
    vec[rows[4]:rows[4] + 1, :] = column_sum(gb[...])
    gmix[...] = dot(gb[...], w[:, 3 * D:4 * D], NT).astype(BF16)
    seen = e.allowed[...] != 0
    seen = jnp.concatenate([seen, seen], axis=0)
    for p in range(D // 128):
        a = p * 128
        q, k, v = (slice(t * D + a, t * D + a + 128) for t in range(3))
        of_q, of_k, of_v = attend_back(
            packed[:, q], packed[:, k], packed[:, v], seen, logsum[:, p:p + 1], gmix[:, a:a + 128])
        gpacked[:, q], gpacked[:, k], gpacked[:, v] = of_q.astype(BF16), of_k.astype(BF16), of_v.astype(BF16)
    vec[rows[2]:rows[2] + 1, :] = column_sum(gpacked[:, :D])
    vec[rows[3]:rows[3] + 1, :] = column_sum(gpacked[:, 2 * D:])
    gn[...] = jnp.zeros_like(gn)

    def back(j):
        cols = span_of(j, D)
        gn[...] += dot(gpacked[:, cols], w[:, cols], NT)
    pl.loop(0, 3)(back)
    weight_gradient(w.at[:, 0:3 * D], n, gpacked, D)
    weight_gradient(w.at[:, 3 * D:4 * D], mixed, gb, D)
    e.ship(ship)
    norm_backward(h_in, gain, gn, g, vec, rows[0], rows[1])


def cross_backward(e, h_in, w, gain, rows, ship):
    D = h_in.shape[1]
    n, queries, kv, mixed, logsum = e.n.at[1], e.queries, e.kv, e.mixed.at[2], e.logsum.at[2]
    g, gb, gmix, gq, gkv, gn, vec = e.g, e.gb, e.gmix, e.gpacked, e.gkv, e.gn, e.vec
    near = e.near
    gb[...] = g[...].astype(BF16)
    vec[rows[4]:rows[4] + 1, :] = column_sum(gb[...])
    gmix[...] = dot(gb[...], w[:, 3 * D:4 * D], NT).astype(BF16)
    spans, keys, size = cross_pairs(e)

    def span(c):
        srows, krows = span_of(c, size), span_of(c, keys)
        seen = cross_seen(e, c)
        for p in range(D // 128):
            a, b = p * 128, D + p * 128
            of_q, of_k, of_v = attend_back(
                queries[srows, a:a + 128], kv[krows, a:a + 128], kv[krows, b:b + 128], seen,
                logsum[span_of(c, 2 * size), p:p + 1], gmix[srows, a:a + 128])
            gq[srows, a:a + 128] = of_q.astype(BF16)
            gkv[krows, a:a + 128], gkv[krows, b:b + 128] = of_k.astype(BF16), of_v.astype(BF16)
    pl.loop(0, spans)(span)
    vec[rows[2]:rows[2] + 1, :] = column_sum(gq[:, :D])
    vec[rows[3]:rows[3] + 1, :] = column_sum(gkv[:, D:])
    gn[...] = dot(gq[:, :D], w[:, 0:D], NT)
    length = near.shape[1]

    def near_rows(i):
        krows = span_of(i, 2 * length)
        value = dot(gkv[krows, :D], w[:, D:2 * D], NT) + dot(gkv[krows, D:], w[:, 2 * D:3 * D], NT)
        e.near_out(i, value.reshape(2, length, D))
    pl.loop(0, near.shape[0] // 2)(near_rows)
    weight_gradient(w.at[:, 0:D], n, gq.at[:, 0:D], D)

    def pair(i):
        cols = span_of(i, 256)
        turned = near[:, :, cols].reshape(-1, 256).T
        for j in range(2):
            w[cols, D + j * D:2 * D + j * D] = dot(turned, gkv[:, j * D:(j + 1) * D]).astype(BF16)
    pl.loop(0, D // 256)(pair)
    weight_gradient(w.at[:, 3 * D:4 * D], mixed, gb, D)
    e.ship(ship)
    norm_backward(h_in, gain, gn, g, vec, rows[0], rows[1])


def block_kernel(spans, *refs):
    (ids, tokens, cotangent, segments, neighbours, stored_tokens, rows, bias_up,
     first, up_a, down_a, second, up_b, down_b,
     out, grad_tokens, grad_near, g_first, g_up_a, g_down_a, g_second, g_up_b, g_down_b, vec, vec_up,
     h, n, packed, mixed, logsum, queries, kv, near, near_tokens, slope, active, allowed,
     gb, gmix, gpacked, gkv, gh, gn, wide, tall, near_stage, loads, ships, nears, near_sems) = refs
    D = tokens.shape[1]
    FF = 4 * D

    def load(number):
        src, dst = (
            (first.at[:, 0:FF], wide.at[0]), (first.at[:, FF:2 * FF], wide.at[1]), (up_a, wide.at[2]), (down_a, tall.at[0]),
            (second, wide.at[0]), (up_b, wide.at[1]), (down_b, tall.at[1]),
            (first.at[:, FF:2 * FF], wide.at[1]), (first.at[:, 0:FF], wide.at[0]))[number]
        return pltpu.make_async_copy(src, dst, loads.at[number])

    def ship_copy(number):
        src, dst = (
            (tall.at[1], g_down_b), (wide.at[1], g_up_b), (wide.at[0], g_second), (tall.at[0], g_down_a),
            (wide.at[2], g_up_a), (wide.at[1], g_first.at[:, FF:2 * FF]), (wide.at[0], g_first.at[:, 0:FF]))[number]
        return pltpu.make_async_copy(src, dst, ships.at[number])

    def near_copy(j):
        return pltpu.make_async_copy(neighbours.at[ids[j]], near.at[j], nears.at[j])

    count = near.shape[0]
    for number in (0, 1, 2, 3, 6):
        load(number).start()
    for j in range(count):
        near_copy(j).start()
    for j in range(count):
        near_tokens[j:j + 1, :] = stored_tokens[pl.ds(ids[j], 1), :]
    grad_near_stage = near_stage

    def near_write(i, half):
        return pltpu.make_async_copy(grad_near_stage.at[i % 2, half], grad_near.at[ids[2 * i + half]], near_sems.at[i % 2, half])

    def near_out(i, value):
        @pl.when(i >= 2)
        def _():
            for half in range(2):
                near_write(i, half).wait()
        grad_near_stage[i % 2] = value
        for half in range(2):
            near_write(i, half).start()

    fill_allowed(allowed, segments)
    e = types.SimpleNamespace(n=n, packed=packed, mixed=mixed, logsum=logsum, queries=queries, kv=kv, near=near, near_tokens=near_tokens,
             slope=slope, active=active, allowed=allowed, g=grad_tokens, gb=gb, gmix=gmix, gpacked=gpacked, gkv=gkv, gh=gh,
             gn=gn, vec=vec, vec_up=vec_up, spans=spans, ship=lambda number: ship_copy(number).start(), near_out=near_out)

    def row(i):
        return rows[i:i + 1, :]
    load(0).wait()
    self_forward(e, 0, tokens, h.at[0], wide.at[0], row(0), row(3), row(6), row(7), row(8), 0)
    load(4).start()
    load(1).wait()
    for j in range(count):
        near_copy(j).wait()
    cross_keys(e, wide.at[1], row(10))
    cross_forward(e, h.at[0], h.at[1], wide.at[1], row(1), row(4), row(9), row(11))
    load(5).start()
    load(2).wait()
    load(3).wait()

    def keep(total):
        h[2] = total[...]
    ffn_forward(e, 0, h.at[1], wide.at[2], tall.at[0], row(2), row(5), bias_up.at[0:1], row(12), 2, keep)
    load(4).wait()
    self_forward(e, 1, h.at[2], h.at[3], wide.at[0], row(13), row(15), row(17), row(18), row(19), 3)
    load(5).wait()
    load(6).wait()

    def finish(total):
        out[...] = total[...].astype(BF16)
    ffn_forward(e, 1, h.at[3], wide.at[1], tall.at[1], row(14), row(16), bias_up.at[1:2], row(20), 4, finish)
    grad_tokens[...] = cotangent[...].astype(F32)
    ffn_backward(e, 1, h.at[3], wide.at[1], tall.at[1], row(14), 4, (14, 16, 20), 0)
    ship_copy(1).wait()
    load(7).start()
    self_backward(e, 1, h.at[2], wide.at[0], row(13), 3, (13, 15, 17, 18, 19), 2)
    ship_copy(2).wait()
    load(8).start()
    ffn_backward(e, 0, h.at[1], wide.at[2], tall.at[0], row(2), 2, (2, 5, 12), 3)
    load(7).wait()
    cross_backward(e, h.at[0], wide.at[1], row(1), (1, 4, 9, 10, 11), 5)
    load(8).wait()
    self_backward(e, 0, tokens, wide.at[0], row(0), 0, (0, 3, 6, 7, 8), 6)
    for number in (0, 3, 4, 5, 6):
        ship_copy(number).wait()
    for i in (count // 2 - 2, count // 2 - 1):
        for half in range(2):
            near_write(i, half).wait()


def run_blocks(tokens, cotangent, segment_ids, neighbours, near_index, neighbour_tokens, spans, rows, bias_up, weights):
    T, D = tokens.shape
    FF = 4 * D
    count, length, _ = neighbours.shape
    vmem, hbm = pl.BlockSpec(memory_space=pltpu.VMEM), pl.BlockSpec(memory_space=pl.ANY)
    shape = jax.ShapeDtypeStruct
    return pl.pallas_call(
        functools.partial(block_kernel, spans),
        out_shape=[shape((T, D), BF16), shape((T, D), F32), shape(neighbours.shape, F32)]
        + [shape(w.shape, BF16) for w in weights] + [shape((24, D), F32), shape((8, FF), F32)],
        in_specs=[pl.BlockSpec(memory_space=pltpu.SMEM), vmem, vmem, vmem, hbm, vmem, vmem, vmem] + [hbm] * 6,
        out_specs=[vmem, vmem, hbm] + [hbm] * 6 + [vmem, vmem],
        scratch_shapes=[
            pltpu.VMEM((4, T, D), F32), pltpu.VMEM((5, T, D), BF16), pltpu.VMEM((2, T, 3 * D), BF16),
            pltpu.VMEM((3, T, D), BF16), pltpu.VMEM((3, 2 * T, 128), F32), pltpu.VMEM((T, D), BF16),
            pltpu.VMEM((count * length, 2 * D), BF16), pltpu.VMEM(neighbours.shape, BF16),
            pltpu.VMEM((count, length), jnp.int32), pltpu.VMEM((2, T, FF), F32), pltpu.VMEM((2, T, FF), BF16),
            pltpu.VMEM((T, T), jnp.int32), pltpu.VMEM((T, D), BF16), pltpu.VMEM((T, D), BF16),
            pltpu.VMEM((T, 3 * D), BF16), pltpu.VMEM((count * length, 2 * D), BF16), pltpu.VMEM((T, FF), BF16),
            pltpu.VMEM((T, D), F32), pltpu.VMEM((3, D, FF), BF16), pltpu.VMEM((2, FF, D), BF16),
            pltpu.VMEM((2, 2, length, D), F32),
            pltpu.SemaphoreType.DMA((9,)), pltpu.SemaphoreType.DMA((7,)), pltpu.SemaphoreType.DMA((count,)),
            pltpu.SemaphoreType.DMA((2, 2)),
        ],
        compiler_params=pltpu.CompilerParams(vmem_limit_bytes=63 * 2 ** 20, has_side_effects=True),
        name="blocks",
    )(near_index, tokens, cotangent, segment_ids, neighbours, neighbour_tokens, rows, bias_up,
      *weights)


def parameter_tile(ref, start, width):
    tile = ref[(slice(None),) * 5 + (pl.ds(start, width),)]
    rows = math.prod(tile.shape[:5])
    if tile.shape[4] % 16:
        return tile.astype(F32).reshape(rows, width).astype(BF16)
    return tile.reshape(rows, width)


def project(out_ref, out_col, lefts, w_ref, w_col, count, bias=None, action=None):
    tile = 256

    def block(j):
        for start in range(0, group, tile):
            here = j * group + start
            weights = parameter_tile(w_ref, pl.multiple_of(w_col + here, tile), tile)
            cols = pl.ds(pl.multiple_of(out_col + here, tile), tile)
            row = 0
            for left in lefts():
                value = dot(left, weights)
                if bias is not None:
                    value = value + bias[:, pl.ds(pl.multiple_of(here, tile), tile)]
                if action is not None:
                    action(cols, value)
                else:
                    out_ref[row:row + left.shape[0], cols] = value.astype(out_ref.dtype)
                row += left.shape[0]
    group = 3 * tile if count % (3 * tile) == 0 else tile
    pl.loop(0, count // group)(block)


def self_pieces(e, i, norm, h_in, h_out, w, chunk, gain, bias_rows):
    D = h_in.shape[1]
    n, packed, mixed, logsum, rows = e.n, e.packed, e.mixed, e.logsum, e.rows
    shift, bq, bv, bo = bias_rows

    def bias(row):
        return rows.at[row:row + 1, :]
    yield chunk, 3.0
    e.free("n")
    norm_forward(h_in, n, rows[gain:gain + 1, :], rows[shift:shift + 1, :])
    e.save("n", norm)
    e.free("packed")
    project(packed, 0, lambda: [n[...]], w, 0, D, bias(bq))
    project(packed, D, lambda: [n[...]], w, D, D)
    yield chunk + 1, 1.0
    project(packed, 2 * D, lambda: [n[...]], w, 2 * D, D, bias(bv))
    e.save("packed", i)
    e.free("mixed")
    e.free("logsum")
    for p in range(D // 128):
        if p % 3 == 0:
            yield chunk + 1, 2.0
        seen = e.allowed[...] != 0
        seen = jnp.concatenate([seen, seen], axis=0)
        a = p * 128
        value, sums = attend(packed[:, a:a + 128], packed[:, D + a:D + a + 128], packed[:, 2 * D + a:2 * D + a + 128], seen)
        mixed[:, a:a + 128] = value.astype(BF16)
        logsum[:, p:p + 1] = sums
    e.save("mixed", i)
    e.save("logsum", i)
    yield chunk + 1, 1.0

    def add(cols, value):
        h_out[:, cols] = h_in[:, cols].astype(F32) + value
    project(None, 0, lambda: [mixed[...]], w, 3 * D, D, bias(bo), add)
    e.save("h", 3 * i)


def cross_pieces(e, norm, h_in, h_out, w, chunk, gain, bias_rows):
    D = h_in.shape[1]
    n, queries, kv, mixed, logsum, rows = e.n, e.queries, e.kv, e.mixed, e.logsum, e.rows
    near, near_tokens, spans = e.near, e.near_tokens, e.spans
    count, length = near.shape[0], near.shape[1]
    shift, bq, bv, bo = bias_rows
    yield chunk, 2.0
    e.free("n")
    norm_forward(h_in, n, rows[gain:gain + 1, :], rows[shift:shift + 1, :])
    e.save("n", norm)
    project(queries, 0, lambda: [n[...]], w, 4 * D, D, rows.at[bq:bq + 1, :])
    e.save("queries", 0)
    flat = lambda: [near[j:j + 2].reshape(2 * length, D) for j in range(0, count, 2)]
    yield chunk, 3.0
    project(kv, 0, flat, w, 5 * D, D)
    yield chunk + 1, 3.0
    project(kv, D, flat, w, 6 * D, D, rows.at[bv:bv + 1, :])
    e.save("kv", 0)
    e.free("mixed")
    e.free("logsum")
    size, each = n.shape[0] // spans, count // spans
    for c in range(spans):
        yield chunk + 1, 1.3
        seen = jnp.concatenate([near_tokens[c * each + j:c * each + j + 1, :] for j in range(each)], axis=1) != 0

        def read(col):
            return kv[c * each * length:(c + 1) * each * length, col:col + 128]
        for p in range(D // 128):
            a = p * 128
            value, sums = attend(queries[c * size:(c + 1) * size, a:a + 128], read(a), read(D + a), seen)
            mixed[c * size:(c + 1) * size, a:a + 128] = value.astype(BF16)
            logsum[2 * c * size:2 * (c + 1) * size, p:p + 1] = sums
    e.save("mixed", 2)
    e.save("logsum", 2)
    yield chunk + 1, 1.0

    def add(cols, value):
        h_out[:, cols] = h_in[:, cols] + value
    project(None, 0, lambda: [mixed[...]], w, 7 * D, D, rows.at[bo:bo + 1, :], add)
    e.save("h", 1)


def ffn_pieces(e, i, norm, h_in, w_up, w_down, chunk, gain, bias_rows, finish):
    D = h_in.shape[1]
    n, slope, active, rows, total = e.n, e.slope, e.active, e.rows, e.total
    shift, bd = bias_rows
    FF = active.shape[1]
    yield chunk, 1.0
    e.free("n")
    norm_forward(h_in, n, rows[gain:gain + 1, :], rows[shift:shift + 1, :])
    e.save("n", norm)
    e.free("slope")
    e.free("active")

    def action(cols, value):
        raised, bent = gelu_both(value)
        active[:, cols] = raised.astype(BF16)
        slope[:, cols] = bent.astype(BF16)
    for j in range(FF // D):
        yield chunk + (2 * j * D) // FF, 1.3
        project(None, j * D, lambda: [n[...]], w_up, j * D, D, e.bias_up.at[i:i + 1, j * D:(j + 1) * D], action)
    e.save("slope", i)
    e.save("active", i)

    def add(cols, value):
        total[:, cols] = h_in[:, cols] + value
    yield chunk + 3, 3.0
    project(None, 0, lambda: [active[...]], w_down, 0, D, rows.at[bd:bd + 1, :], add)
    finish()


def forward_pieces(e, h, tokens, first, up_a, down_a, second, up_b, down_b, small):
    yield 0, 1.5
    lines = [small[index] for index in itertools.product(*map(range, small.shape[:4]))]
    part = e.rows.shape[1] // len(lines)
    wide = e.bias_up.shape[1] // len(lines)
    e.rows[...] = jnp.concatenate([line[:24, :part].astype(F32) for line in lines], axis=1)
    both = jnp.concatenate([line[16:24, :wide].astype(F32) for line in lines], axis=1)
    e.bias_up[...] = both[5:7]
    yield from self_pieces(e, 0, 0, tokens, h.at[0], first, 0, 0, (3, 6, 7, 8))
    yield from cross_pieces(e, 1, h.at[0], h.at[1], first, 2, 1, (4, 9, 10, 11))

    def keep():
        h[2] = e.total[...]
        e.save("h", 2)
    yield from ffn_pieces(e, 0, 2, h.at[1], up_a, down_a, 4, 2, (5, 12), keep)
    yield from self_pieces(e, 1, 3, h.at[2], h.at[3], second, 8, 13, (15, 17, 18, 19))

    def finish():
        e.out[...] = e.total[...].astype(BF16)
    yield from ffn_pieces(e, 1, 4, h.at[3], up_b, down_b, 10, 14, (16, 20), finish)


SAVED = ("n", "packed", "queries", "kv", "mixed", "logsum", "slope", "active")


def forward_kernel(dp_size, fsdp_size, chunks, places, count, spans, *refs):
    n = len(places)
    shards, vectors, (tokens, segments, near, near_tokens) = refs[:n], refs[n:n + 6], refs[n + 6:n + 10]
    refs = refs[n + 10:]
    wholes, (out, h_out, rows), saved = refs[:count - 1], refs[count - 1:count + 2], dict(zip(SAVED, refs[count + 2:count + 10]))
    refs = refs[count + 10:]
    landing, held, (h, allowed, total, bias_up) = refs[:count], dict(zip(SAVED, refs[count:count + 8])), refs[count + 8:count + 12]
    kept, saves, send, recv = refs[count + 12:]
    place = Place(dp_size, fsdp_size)
    here = tuple(place.at[name] for name in NAMES)
    for shard, (which, col) in zip(shards, places):
        landing[which][(*here, slice(None), slice(col, col + shard.shape[1]))] = shard[...]
    landing[count - 1][here] = pack_small(vectors[:4], vectors[4:])
    greet(place)
    sems = Sems(send, recv)
    copies, pending, used = [], {}, [0]

    def keep(slot, which, row, height, col, width):
        where = (slice(None),) * 4 + (pl.ds(row, height), pl.ds(col, width))
        copy = pltpu.make_async_copy(landing[which].at[where], wholes[which].at[where], kept.at[slot])
        copy.start()
        copies.append(copy)

    def chunk_flow(slots, group):
        flows = [
            gather_flow(place, sems, landing[which], order, row, height, start + col, width)
            for which, row, height, start, total in group
            for order, col, width in routes(total)
        ]
        while flows:
            flows = [flow for flow in flows if next(flow, 0) is None]
            if flows:
                yield
        for slot, member in zip(slots, group):
            if member[0] < count - 1:
                keep(slot, *member)

    def save(name, index):
        src, dst = (h.at[index], h_out.at[index]) if name == "h" else (held[name], saved[name].at[index])
        copy = pltpu.make_async_copy(src, dst, saves.at[used[0]])
        copy.start()
        used[0] += 1
        pending[(name, index) if name == "h" else name] = copy

    def free(name):
        if name in pending:
            pending.pop(name).wait()

    fill_allowed(allowed, segments)
    e = types.SimpleNamespace(**held, rows=rows, bias_up=bias_up, allowed=allowed, near=near, near_tokens=near_tokens, spans=spans,
             total=total, out=out, save=save, free=free)
    work = forward_pieces(e, h, tokens, *landing)
    ahead = next(work, None)
    groups, slot = [], 0
    for group in chunks:
        groups.append([chunk_flow(range(slot, slot + len(group)), group)])
        slot += len(group)

    def compute(tick, ahead=[ahead]):
        left = COMPUTE_SHARE
        last = tick == len(groups) + GATHER_STEPS[-1] - 1
        while ahead[0] is not None and ahead[0][0] + GATHER_STEPS[-1] <= tick and (left > 0 or last):
            left -= ahead[0][1]
            ahead[0] = next(work, None)
    run_schedule(groups, GATHER_STEPS, compute)
    sems.drain()
    for copy in copies + list(pending.values()):
        copy.wait()


def arrange_kernel(ids, neighbours, stored_tokens, near, near_tokens, sems):
    copies = [pltpu.make_async_copy(neighbours.at[ids[j]], near.at[j], sems.at[j]) for j in range(near.shape[0])]
    for copy in copies:
        copy.start()
    for j in range(near.shape[0]):
        near_tokens[j:j + 1, :] = stored_tokens[pl.ds(ids[j], 1), :]
    for copy in copies:
        copy.wait()


def arrange(near_index, neighbours, neighbour_tokens):
    vmem, hbm = pl.BlockSpec(memory_space=pltpu.VMEM), pl.BlockSpec(memory_space=pl.ANY)
    return pl.pallas_call(
        arrange_kernel,
        out_shape=[jax.ShapeDtypeStruct(x.shape, x.dtype) for x in (neighbours, neighbour_tokens)],
        in_specs=[pl.BlockSpec(memory_space=pltpu.SMEM), hbm, vmem],
        out_specs=[vmem, vmem],
        scratch_shapes=[pltpu.SemaphoreType.DMA((neighbours.shape[0],))],
        name="arrange_neighbours",
    )(near_index, neighbours, neighbour_tokens)


def gather_and_run(mesh_shape, shards, places, vectors, chunks, tokens, segment_ids, neighbours, neighbour_tokens,
                   spans, collective_id):
    dp_size, fsdp_size = mesh_shape
    size = {"y": dp_size // 2, "c": 2, "z": fsdp_size // 2, "x": 2}
    count = sum(copies_of(order, size) for group in chunks for *_, total in group for order, _, _ in routes(total))
    count += sum(1 for group in chunks for *_, total in group for _ in routes(total))
    lead = tuple(size[name] for name in NAMES)
    shapes = {}
    for shard, (which, col) in zip(shards, places):
        rows, width = shapes.get(which, (shard.shape[0], 0))
        shapes[which] = (rows, max(width, col + shard.shape[1]))
    shapes = [shapes[which] for which in sorted(shapes)] + [(32, 128)]
    T, D = tokens.shape
    FF = 4 * D
    near, length, _ = neighbours.shape
    shape = jax.ShapeDtypeStruct
    held = {"n": ((T, D), BF16, 5), "packed": ((T, 3 * D), BF16, 2), "queries": ((T, D), BF16, 1),
            "kv": ((near * length, 2 * D), BF16, 1), "mixed": ((T, D), BF16, 3), "logsum": ((2 * T, 128), F32, 3),
            "slope": ((T, FF), BF16, 2), "active": ((T, FF), BF16, 2)}
    n, vmem, hbm = len(shards), pl.BlockSpec(memory_space=pltpu.VMEM), pl.BlockSpec(memory_space=pl.ANY)
    results = pl.pallas_call(
        functools.partial(forward_kernel, dp_size, fsdp_size, chunks, places, len(shapes), spans),
        out_shape=[shape(lead + s, BF16) for s in shapes[:-1]]
        + [shape((T, D), BF16), shape((4, T, D), F32), shape((24, D), F32)]
        + [shape((times,) + s, kind) for s, kind, times in held.values()],
        in_specs=[vmem] * (n + 10),
        out_specs=[hbm] * (len(shapes) - 1) + [vmem, hbm, vmem] + [hbm] * 8,
        scratch_shapes=[pltpu.VMEM(lead + s, BF16) for s in shapes]
        + [pltpu.VMEM(s, kind) for s, kind, _ in held.values()]
        + [pltpu.VMEM((4, T, D), F32), pltpu.VMEM((T, T), jnp.int32), pltpu.VMEM((T, D), F32), pltpu.VMEM((2, FF), F32)]
        + [
            pltpu.SemaphoreType.DMA((sum(map(len, chunks)),)),
            pltpu.SemaphoreType.DMA((24,)),
            pltpu.SemaphoreType.DMA((count,)),
            pltpu.SemaphoreType.DMA((count,)),
        ],
        compiler_params=pltpu.CompilerParams(
            collective_id=collective_id, has_side_effects=True, vmem_limit_bytes=63 * 2 ** 20),
        name="gather_and_forward",
    )(*shards, *vectors, tokens, segment_ids, neighbours, neighbour_tokens)
    return results[:len(shapes) - 1], results[len(shapes) - 1:len(shapes) + 2], dict(zip(SAVED, results[len(shapes) + 2:]))


def ffn_chain(e, i, h_in, w_up, w_down, gain, norm, rows):
    D, FF = h_in.shape[1], w_up.shape[1]
    slope, gb, gh, g, gn, vec = e.slope.at[i], e.gb.at[norm], e.gh.at[i], e.g, e.gn, e.vec
    gb[...] = g[...].astype(BF16)
    vec[rows[2]:rows[2] + 1, :] = column_sum(gb[...])
    gn[...] = jnp.zeros_like(gn)

    def hidden(j):
        cols = span_of(j, D)
        value = (dot(gb[...], w_down[cols, :], NT) * slope[:, cols].astype(F32)).astype(BF16)
        gh[:, cols] = value
        e.vec_up[i:i + 1, cols] = column_sum(value)
        gn[...] += dot(value, w_up[:, cols], NT)
    pl.loop(0, FF // D)(hidden)
    e.save("gb", norm)
    e.save("gh", i)
    norm_backward(h_in, gain, gn, g, vec, rows[0], rows[1])


def self_chain(e, i, h_in, w, gain, norm, rows):
    D = h_in.shape[1]
    packed, logsum, gb, gpacked = e.packed.at[i], e.logsum.at[i], e.gb.at[norm], e.gpacked.at[i]
    g, gmix, gn, vec = e.g, e.gmix, e.gn, e.vec
    gb[...] = g[...].astype(BF16)
    vec[rows[4]:rows[4] + 1, :] = column_sum(gb[...])
    e.save("gb", norm)
    gmix[...] = dot(gb[...], w[:, 3 * D:4 * D], NT).astype(BF16)
    seen = e.allowed[...] != 0
    seen = jnp.concatenate([seen, seen], axis=0)
    for p in range(D // 128):
        a = p * 128
        q, k, v = (slice(t * D + a, t * D + a + 128) for t in range(3))
        of_q, of_k, of_v = attend_back(
            packed[:, q], packed[:, k], packed[:, v], seen, logsum[:, p:p + 1], gmix[:, a:a + 128])
        gpacked[:, q], gpacked[:, k], gpacked[:, v] = of_q.astype(BF16), of_k.astype(BF16), of_v.astype(BF16)
    e.save("gpacked", i)
    vec[rows[2]:rows[2] + 1, :] = column_sum(gpacked[:, :D])
    vec[rows[3]:rows[3] + 1, :] = column_sum(gpacked[:, 2 * D:])
    gn[...] = jnp.zeros_like(gn)

    def back(j):
        cols = span_of(j, D)
        gn[...] += dot(gpacked[:, cols], w[:, cols], NT)
    pl.loop(0, 3)(back)
    norm_backward(h_in, gain, gn, g, vec, rows[0], rows[1])


KEPT = ("packed", "logsum", "slope")
MADE = ("gb", "gh", "gpacked")


def backward_kernel(*refs):
    (cotangent, segments, rows, h_in, up_a, down_a, second, up_b, down_b) = refs[:9]
    stored = dict(zip(KEPT, refs[9:12]))
    g, vec, vec_up = refs[12:15]
    given, held, made = dict(zip(MADE, refs[15:18])), dict(zip(KEPT, refs[18:21])), dict(zip(MADE, refs[21:24]))
    (h, allowed, gmix, gn, wide, tall, loads, brought, saves) = refs[24:]

    def load(number):
        src, dst = (
            (down_b, tall.at[1]), (up_b, wide.at[1]), (second, wide.at[0]), (down_a, tall.at[0]), (up_a, wide.at[2]))[number]
        return pltpu.make_async_copy(src, dst, loads.at[number])

    wanted = ((2, 1), (3, 3), (0, 1), (1, 1), (3, 2), (2, 0), (3, 1))

    def bring(number):
        which, index = wanted[number]
        src, dst = (h_in, h) if which == 3 else (stored[KEPT[which]], held[KEPT[which]])
        return pltpu.make_async_copy(src.at[index], dst.at[index], brought.at[number])

    saved = []

    def save(name, index):
        copy = pltpu.make_async_copy(made[name].at[index], given[name].at[index], saves.at[len(saved)])
        copy.start()
        saved.append(copy)

    load(0).start()
    bring(0).start()
    load(1).start()
    bring(1).start()
    load(2).start()
    for number in range(2, len(wanted)):
        bring(number).start()
    load(3).start()
    load(4).start()
    fill_allowed(allowed, segments)
    e = types.SimpleNamespace(**held, **made, allowed=allowed, g=g, gmix=gmix, gn=gn, vec=vec, vec_up=vec_up, save=save)

    def row(i):
        return rows[i:i + 1, :]

    def ready(*numbers):
        for number in numbers:
            bring(number).wait()
    g[...] = cotangent[...].astype(F32)
    load(0).wait()
    load(1).wait()
    ready(0, 1)
    ffn_chain(e, 1, h.at[3], wide.at[1], tall.at[1], row(14), 4, (14, 16, 20))
    load(2).wait()
    ready(2, 3, 4)
    self_chain(e, 1, h.at[2], wide.at[0], row(13), 3, (13, 15, 17, 18, 19))
    load(3).wait()
    load(4).wait()
    ready(5, 6)
    ffn_chain(e, 0, h.at[1], wide.at[2], tall.at[0], row(2), 2, (2, 5, 12))
    for copy in saved:
        copy.wait()


def run_backward(cotangent, segment_ids, rows, h, saved, weights):
    T, D = cotangent.shape
    FF = 4 * D
    vmem, hbm = pl.BlockSpec(memory_space=pltpu.VMEM), pl.BlockSpec(memory_space=pl.ANY)
    shape = jax.ShapeDtypeStruct
    made = ((5, T, D), (2, T, FF), (2, T, 3 * D))
    results = pl.pallas_call(
        backward_kernel,
        out_shape=[shape((T, D), F32), shape((24, D), F32), shape((8, FF), F32)] + [shape(s, BF16) for s in made],
        in_specs=[vmem] * 3 + [hbm] * 9,
        out_specs=[vmem] * 3 + [hbm] * 3,
        scratch_shapes=[pltpu.VMEM(saved[name].shape, saved[name].dtype) for name in KEPT]
        + [pltpu.VMEM(s, BF16) for s in made] + [
            pltpu.VMEM((4, T, D), F32), pltpu.VMEM((T, T), jnp.int32), pltpu.VMEM((T, D), BF16),
            pltpu.VMEM((T, D), F32), pltpu.VMEM((3, D, FF), BF16), pltpu.VMEM((2, FF, D), BF16),
            pltpu.SemaphoreType.DMA((5,)), pltpu.SemaphoreType.DMA((7,)), pltpu.SemaphoreType.DMA((6,)),
        ],
        compiler_params=pltpu.CompilerParams(vmem_limit_bytes=VMEM_MOST, has_side_effects=True),
        name="backward",
    )(cotangent, segment_ids, rows, h, *weights, *[saved[name] for name in KEPT])
    return results[:3], dict(zip(MADE, results[3:]))


def gradient_columns(dst, j, left, right, right_col):
    size = dst.shape
    rows = math.prod(size[1:4]) * size[5]

    def block(y):
        turned = left(pl.ds(pl.multiple_of(y * rows, 128), rows)).T
        for start in range(0, size[6], 256):
            value = dot(turned, right[:, right_col + start:right_col + start + 256])
            dst[y, :, :, :, j, :, start:start + 256] = value.reshape(size[1:4] + (size[5], 256)).astype(BF16)
    pl.loop(0, size[0])(block)


def gradient_rows(dsts, left, right):
    Y, C, Z, X, parts, rows, width = dsts[0].shape
    each = 2 * X * rows * parts * len(dsts)

    def block(i):
        y, c, z = i // (C * Z // 2), (i // (Z // 2)) % C, i % (Z // 2)
        turned = left[:, pl.ds(pl.multiple_of(i * each, 128), each)].T
        for start in range(0, width, 256):
            value = dot(turned, right[:, start:start + 256]).reshape(2, X, len(dsts), parts, rows, 256).astype(BF16)
            for half, dst in enumerate(dsts):
                dst[y, c, pl.ds(2 * z, 2), :, :, :, start:start + 256] = value[:, :, half]
    pl.loop(0, left.shape[1] // each)(block)


FACTORS = ("n", "active", "mixed", "gb", "gh", "gpacked", "packed", "logsum", "kv", "queries", "h")
ORDER = (("active", 1, 0), ("gb", 4, 4), ("n", 4, 4), ("gh", 1, 0), ("kv", 0, 0), ("queries", 0, 0), ("logsum", 2, 2), ("h", 0, 0),
         ("n", 3, 3), ("gpacked", 1, 0), ("mixed", 1, 1), ("gb", 3, 3), ("packed", 0, 0), ("logsum", 0, 0), ("gb", 2, 2),
         ("n", 2, 2), ("n", 1, 1), ("mixed", 2, 2), ("n", 0, 0), ("mixed", 0, 0))
LATER = (("active", 0, 0), ("gh", 0, 0))


def chunk_makers(f, need, later, require):
    near = f.near
    D = near.shape[2]

    def rows_of(i, norm):
        def make(dsts):
            need(("active", i), ("gb", norm))
            gradient_rows(dsts, f.active.at[0], f.gb.at[norm])
            if i:
                later(0)
        return make

    def columns(dst, j, name, index, right, right_col):
        left = getattr(f, name)
        gradient_columns(dst, j, lambda rows: left[index, :, rows], right, right_col)

    def up(i, norm, half):
        def make(dsts):
            need(("n", norm), ("gh", i))
            for j in range(2):
                columns(dsts[0], j, "n", norm, f.gh.at[0], (2 * half + j) * D)
            if i and not half:
                later(1)
        return make

    def query_key(i, norm):
        def make(dsts):
            require(2 - 2 * i)
            need(("n", norm), ("gpacked", i))
            for j in range(2):
                columns(dsts[0], j, "n", norm, f.gpacked.at[0], j * D)
        return make

    def value_out(i, norm):
        def make(dsts):
            require(2 - 2 * i)
            need(("n", norm), ("gpacked", i), ("mixed", i), ("gb", norm))
            columns(dsts[0], 0, "n", norm, f.gpacked.at[0], 2 * D)
            columns(dsts[0], 1, "mixed", i, f.gb.at[norm], 0)
        return make

    def near_rows(rows):
        return near[:, :, rows].reshape(-1, rows.size)

    def cross_one(dsts):
        require(1)
        need(("n", 1))
        columns(dsts[0], 0, "n", 1, f.gq, 0)
        gradient_columns(dsts[0], 1, near_rows, f.gkv, 0)

    def cross_two(dsts):
        require(1)
        need(("mixed", 2))
        gradient_columns(dsts[0], 0, near_rows, f.gkv, D)
        columns(dsts[0], 1, "mixed", 2, f.gb.at[1], 0)
    return (rows_of(1, 4), None, up(1, 4, 1), up(1, 4, 0), value_out(1, 3), query_key(1, 3), rows_of(0, 2), None,
            up(0, 2, 1), up(0, 2, 0), cross_two, cross_one, value_out(0, 0), query_key(0, 0))


def chain_pieces(f, need, near_out, spans):
    g, gn, gmix, vec, rows, gq, gkv, gpacked = f.g, f.gn, f.gmix, f.vec, f.rows, f.gq, f.gkv, f.gpacked.at[0]
    D = g.shape[1]
    tiles = f.tiles
    yield 1.5
    need(("tiles", 0))
    gb = f.gb.at[1]
    gb[...] = g[...].astype(BF16)
    vec[11:12, :] = column_sum(gb[...])
    gmix[...] = dot(gb[...], tiles[3], NT).astype(BF16)
    near, length = f.near_tokens.shape
    each = near // spans
    keys, size = each * length, g.shape[0] // spans
    need(("kv", 0), ("queries", 0), ("logsum", 2), ("h", 0))
    queries, kv, logsum = f.queries.at[0], f.kv.at[0], f.logsum.at[2]
    for c in range(spans):
        yield 2.5
        srows, krows = slice(c * size, (c + 1) * size), slice(c * keys, (c + 1) * keys)
        seen = jnp.concatenate([f.near_tokens[c * each + j:c * each + j + 1, :] for j in range(each)], axis=1) != 0
        for p in range(D // 128):
            a, b = p * 128, D + p * 128
            of_q, of_k, of_v = attend_back(
                queries[srows, a:a + 128], kv[krows, a:a + 128], kv[krows, b:b + 128], seen,
                logsum[2 * c * size:2 * (c + 1) * size, p:p + 1], gmix[srows, a:a + 128])
            gq[srows, a:a + 128] = of_q.astype(BF16)
            gkv[krows, a:a + 128], gkv[krows, b:b + 128] = of_k.astype(BF16), of_v.astype(BF16)
    yield 1.0
    vec[9:10, :] = column_sum(gq[...])
    vec[10:11, :] = column_sum(gkv[:, D:])
    gn[...] = dot(gq[...], tiles[0], NT)
    yield 1.5
    norm_backward(f.h.at[0], rows[1:2, :], gn, g, vec, 1, 4)
    f.stage = 1
    yield 1.0
    gb = f.gb.at[0]
    gb[...] = g[...].astype(BF16)
    vec[8:9, :] = column_sum(gb[...])
    gmix[...] = dot(gb[...], tiles[7], NT).astype(BF16)
    need(("packed", 0), ("logsum", 0))
    packed, logsum = f.packed.at[0], f.logsum.at[0]
    for p in range(D // 128):
        if p % 3 == 0:
            yield 3.0
        seen = f.allowed[...] != 0
        seen = jnp.concatenate([seen, seen], axis=0)
        a = p * 128
        q, k, v = (slice(t * D + a, t * D + a + 128) for t in range(3))
        of_q, of_k, of_v = attend_back(
            packed[:, q], packed[:, k], packed[:, v], seen, logsum[:, p:p + 1], gmix[:, a:a + 128])
        gpacked[:, q], gpacked[:, k], gpacked[:, v] = of_q.astype(BF16), of_k.astype(BF16), of_v.astype(BF16)
    yield 2.0
    vec[6:7, :] = column_sum(gpacked[:, :D])
    vec[7:8, :] = column_sum(gpacked[:, 2 * D:])
    gn[...] = dot(gpacked[:, :D], tiles[4], NT) + dot(gpacked[:, D:2 * D], tiles[5], NT) + dot(gpacked[:, 2 * D:], tiles[6], NT)
    yield 1.5
    norm_backward(f.tokens, rows[0:1, :], gn, g, vec, 0, 3)
    f.stage = 2
    for i in range(near // 2):
        yield 1.5
        krows = slice(2 * i * length, 2 * (i + 1) * length)
        value = dot(gkv[krows, :D], tiles[1], NT) + dot(gkv[krows, D:], tiles[2], NT)
        near_out(i, value.reshape(2, length, D))
    f.stage = 3


def scatter_routes(parts, width):
    if parts == 1:
        return [(ROUTES[0][0][::-1], 0, 1, 0, width)]
    third = width // 3
    cut = ((0, 1, 0), (1, 1, 0), (0, 2, third), (0, 2, 2 * third))
    return [(order[::-1], *where, third) for (order, _), where in zip(ROUTES, cut)]


def scatter_kernel(dp_size, fsdp_size, chunks, count, plan, spans, *refs):
    factors = dict(zip(FACTORS, refs[:11]))
    (first, near, near_tokens, rows, tokens, segments, g_in, vec_in, vec_up) = refs[11:20]
    outs, grad_tokens, grad_near = refs[20:20 + count], refs[20 + count], refs[21 + count]
    refs = refs[22 + count:]
    f = types.SimpleNamespace(**dict(zip(FACTORS, refs[:11])))
    (f.gq, f.gkv, f.tiles, f.gmix, f.gn, f.vec, f.allowed, small, near_stage), scratch = refs[11:20], refs[20:-5]
    brought, loads, near_sem, send, recv = refs[-5:]
    f.near, f.near_tokens, f.rows, f.tokens, f.g, f.stage = near, near_tokens, rows, tokens, grad_tokens, 0
    D = tokens.shape[1]
    place = Place(dp_size, fsdp_size)
    sems = Sems(send, recv)
    c = place.at["c"]
    sibling = place.device("c", 1 - c)
    arriving = {}

    def bring(number):
        name, index, slot = (ORDER + LATER)[number]
        copy = pltpu.make_async_copy(factors[name].at[index], getattr(f, name).at[slot], brought.at[number])
        copy.start()
        arriving[name, index] = [copy]

    def load(j):
        copy = pltpu.make_async_copy(first.at[:, (j + 4) % 8 * D:((j + 4) % 8 + 1) * D], f.tiles.at[j], loads.at[j])
        copy.start()
        return copy
    for number in range(4):
        bring(number)
    arriving["tiles", 0] = [load(j) for j in range(8)]
    for number in range(4, len(ORDER)):
        bring(number)

    def need(*wanted):
        for key in wanted:
            for copy in arriving.pop(key, ()):
                copy.wait()
    near_copies = []

    def near_out(i, value):
        if near_copies:
            near_copies.pop().wait()
        near_stage[...] = value
        near_copies.append(pltpu.make_async_copy(near_stage, grad_near.at[2 * i:2 * i + 2], near_sem))
        near_copies[-1].start()
    chain = chain_pieces(f, need, near_out, spans)

    def require(stage):
        while f.stage < stage:
            next(chain)
    makers = chunk_makers(f, need, lambda number: bring(len(ORDER) + number), require)
    everything = pl.ds(0, place.size["y"])
    lead = tuple(place.size[name] for name in NAMES if name != "c")

    def pack():
        require(2)
        part, wide = outs[-1].shape[0], vec_up.shape[1]
        for index in itertools.product(*(range(place.size[name]) for name in NAMES)):
            i = ((index[0] * 2 + index[1]) * place.size["z"] + index[2]) * 2 + index[3]
            devices = dp_size * fsdp_size
            one, many = D // devices, wide // devices
            values = jnp.pad(f.vec[0:21, i * one:(i + 1) * one], ((0, 0), (0, 128 - one)))
            ups = jnp.pad(vec_up[0:2, i * many:(i + 1) * many], ((0, 0), (0, 128 - many)))
            blank = jnp.zeros((part - 23, 128), F32)
            small[(*index, 0)] = jnp.concatenate([values, ups, blank], axis=0).astype(BF16)

    def chunk_flow(make, grad, landing, buffers, routed, targets):
        if make is not None:
            make()
        crossing = []
        for _, j, nj, col, width in routed:
            slot, part = sems.take(), (pl.ds(j, nj), slice(None), pl.ds(col, width))
            copy = sems.copy(slot, grad.at[(everything, 1 - c, slice(None), slice(None), *part)],
                             landing.at[(slice(None), slice(None), slice(None), *part)], sibling)
            copy.start()
            crossing.append(copy)
        yield
        for copy in crossing:
            copy.wait()
        add_blocks(lead + landing.shape[3:4], landing, landing, grad.at[:, c])
        flows = []
        for (order, j, nj, col, width), own in zip(routed, buffers):
            part = (pl.ds(j, nj), slice(None), pl.ds(col, width))
            flows.append(scatter_flow(
                place, sems, landing.at[(slice(None), slice(None), slice(None), *part)], own, order,
                [target.at[:, pl.ds(col, width)] for target in targets[j:j + nj]], (nj,)))
        while flows:
            flows = [flow for flow in flows if next(flow, 0) is None]
            if flows:
                yield

    groups = []
    for number, (group, places) in enumerate(zip(chunks, plan)):
        members = []
        for (which, row, height, col, width), (grad, landing, buffers) in zip(group, places):
            if grad is None:
                make, array, targets = pack, small, [outs[which]]
            else:
                make, array = makers[number], scratch[grad]
                fill = [array]
                if makers[(number + 1) % len(makers)] is None:
                    fill = [scratch[plan[number + 1][0][0]], array]
                make = make and functools.partial(make, fill)
                rows_, cols_ = array.shape[5:]
                if width == cols_:
                    targets = [outs[which].at[row + j * rows_:row + (j + 1) * rows_, :] for j in range(2)]
                else:
                    targets = [outs[which].at[:, col + j * cols_:col + (j + 1) * cols_] for j in range(2)]
            members.append(chunk_flow(
                make, array, scratch[landing], [[scratch[b] for b in own] for own in buffers],
                scatter_routes(array.shape[4], array.shape[6]), targets))
        groups.append(members)

    fill_allowed(f.allowed, segments)
    grad_tokens[...] = g_in[...]
    f.vec[...] = vec_in[...]
    greet(place)

    def chain_some(tick):
        left = CHAIN_SHARE
        while f.stage < 3 and left > 0 and (f.stage != 1 or tick >= 5):
            left -= next(chain, 9.0)
    run_schedule(groups, SCATTER_STEPS, chain_some)
    require(3)
    sems.drain()
    near_copies.pop().wait()


def scatter_all(mesh_shape, factors, first, near, near_tokens, rows, tokens, segment_ids, g, vec, vec_up, spans, owned, chunks,
                collective_id):
    dp_size, fsdp_size = mesh_shape
    size = {"y": dp_size // 2, "c": 2, "z": fsdp_size // 2, "x": 2}
    lead = tuple(size[name] for name in NAMES if name != "c")
    whole = tuple(size[name] for name in NAMES)
    T, D = tokens.shape
    count_near, length, _ = near.shape
    part = D // (dp_size * fsdp_size)
    shapes, plan, pools, count = [], [], {}, 0

    def new(shape, role, most):
        pool = pools.setdefault((shape, role), [])
        if len(pool) < most:
            shapes.append(pltpu.VMEM(shape, BF16))
            pool.append(len(shapes) - 1)
        else:
            pool.append(pool.pop(0))
        return pool[-1]

    for group in chunks:
        places = []
        for which, *_ in group:
            small = which == len(owned) - 1
            block = (1, 32, 128) if small else (2, part, D)
            grad = None if small else new(whole + block, 0, 3)
            landing = new(lead + block, 1, LANDINGS)
            buffers = []
            for number, (order, _, nj, _, width) in enumerate(scatter_routes(block[0], block[2])):
                buffers.append([
                    new(s, (2, number, i), WINDOW)
                    for i, s in enumerate(scatter_buffers(size, order, (nj, block[1], width)))])
                count += copies_of(order, size)
            places.append((grad, landing, buffers))
        plan.append(places)
    vmem, hbm = pl.BlockSpec(memory_space=pltpu.VMEM), pl.BlockSpec(memory_space=pl.ANY)
    slots = {"active": 1, "gh": 1, "gpacked": 1, "packed": 1, "h": 1}
    return pl.pallas_call(
        functools.partial(scatter_kernel, dp_size, fsdp_size, chunks, len(owned), plan, spans),
        out_shape=[jax.ShapeDtypeStruct(shape, F32) for shape in (*owned, (T, D), near.shape)],
        in_specs=[hbm] * 12 + [vmem] * 8,
        out_specs=[vmem] * (len(owned) + 1) + [hbm],
        scratch_shapes=[
            pltpu.VMEM((slots.get(name, factors[name].shape[0]),) + factors[name].shape[1:], factors[name].dtype)
            for name in FACTORS
        ] + [
            pltpu.VMEM((T, D), BF16), pltpu.VMEM((count_near * length, 2 * D), BF16), pltpu.VMEM((8, D, D), BF16),
            pltpu.VMEM((T, D), BF16), pltpu.VMEM((T, D), F32), pltpu.VMEM((24, D), F32), pltpu.VMEM((T, T), jnp.int32),
            pltpu.VMEM(whole + (1, 32, 128), BF16), pltpu.VMEM((2, length, D), F32),
        ] + shapes + [
            pltpu.SemaphoreType.DMA((len(ORDER) + len(LATER),)),
            pltpu.SemaphoreType.DMA((8,)),
            pltpu.SemaphoreType.DMA,
            pltpu.SemaphoreType.DMA((count,)),
            pltpu.SemaphoreType.DMA((count,)),
        ],
        compiler_params=pltpu.CompilerParams(
            collective_id=collective_id, has_side_effects=True, vmem_limit_bytes=VMEM_MOST),
        name="scatter_gradients",
    )(*[factors[name] for name in FACTORS], first, near, near_tokens, rows, tokens, segment_ids,
      g, vec, vec_up)


PLACES = ((0, 0), (0, 3), (0, 4), (0, 5), (0, 7), (1, 0), (2, 0), (3, 0), (3, 3), (4, 0), (5, 0))


def chunk_table(D, part, long):
    table = [((0, 0, part, i * 2 * D, 2 * D),) for i in range(4)]
    for first in (1, 3):
        if first == 3:
            table += [((3, 0, part, i * 2 * D, 2 * D),) for i in range(2)]
        table += [((first + first // 3, 0, part, i * 2 * D, 2 * D),) for i in range(2)]
        table += [((first + first // 3 + 1, i * long // 2, long // 2, 0, D),) for i in range(2)]
    table[0] += ((6, 0, 32, 0, 128),)
    return table


def local(mesh_shape, *arrays):
    (tokens, segment_ids, neighbours, neighbour_ids, neighbour_tokens, gains_one, biases_one, w_qkv_one, w_out_one,
     w_cross_q, w_cross_kv, w_cross_out, w_up_one, bias_up_one, w_down_one, gains_two, biases_two, w_qkv_two,
     w_out_two, w_up_two, bias_up_two, w_down_two, cotangent) = arrays
    row_count, D = tokens.shape
    FF = w_up_one.shape[1]
    devices = mesh_shape[0] * mesh_shape[1]
    part = D // devices
    quarter = FF // D
    vectors = [gains_one, biases_one, gains_two, biases_two]
    shards = [w_qkv_one, w_out_one, w_cross_q, w_cross_kv, w_cross_out, w_up_one, w_down_one, w_qkv_two, w_out_two,
              w_up_two, w_down_two]
    kernels = part % 8 == 0
    table = chunk_table(D, part, w_down_one.shape[0])
    store_count = neighbours.shape[0]
    spans = neighbour_ids.shape[1]
    near_index = neighbour_ids.reshape(-1) % store_count
    if kernels:
        ups = [bias_up_one.reshape(1, -1), bias_up_two.reshape(1, -1)]
        near, near_tokens = arrange(near_index, neighbours, neighbour_tokens)
        wholes, (out, h, rows), saved = gather_and_run(
            mesh_shape, shards, tuple((w, c * D) for w, c in PLACES), vectors + ups, table, tokens, segment_ids,
            near, near_tokens, spans, 1)
        wholes = [w.reshape(-1, w.shape[-1]) for w in wholes]
        (gradient, vec, vec_up), made = run_backward(cotangent, segment_ids, rows, h, saved, wholes[1:])
        owned = [(w.shape[0] // devices, w.shape[1]) for w in wholes] + [(32, 128)]
        *owned, gradient, grad_neighbours = scatter_all(
            mesh_shape, {**saved, **made, "h": h}, wholes[0], near, near_tokens, rows, tokens, segment_ids, gradient, vec, vec_up,
            spans, owned, table[::-1], 2)
    else:
        small = jnp.concatenate(vectors + [bias_up_one.reshape(-1, part), bias_up_two.reshape(-1, part)])
        small = jnp.pad(small, ((0, -small.shape[0] % 32), (0, -part % 128)))
        sides = [[] for _ in range(6)]
        for shard, (which, _) in zip(shards, PLACES):
            sides[which].append(shard)
        shards = [jnp.concatenate(side, axis=1) for side in sides] + [small]
        *wholes, smalls = [lax.all_gather(s, ("dp", "fsdp"), axis=0, tiled=True) for s in shards]
        smalls = smalls.reshape(devices, -1, smalls.shape[-1])[:, :, :part]
        rows = smalls[:, :21].transpose(1, 0, 2).reshape(21, D)
        bias_up = [smalls[:, 21 + i * quarter:21 + (i + 1) * quarter].reshape(FF) for i in range(2)]
        rows = jnp.pad(rows.astype(F32), ((0, 3), (0, 0)))
        bias_up = jnp.pad(jnp.stack(bias_up).astype(F32), ((0, 6), (0, 0)))
        out, gradient, grad_neighbours, *grads, vectors, vectors_up = run_blocks(
            tokens, cotangent, segment_ids, neighbours, near_index, neighbour_tokens, spans, rows, bias_up, wholes)
        vectors = vectors[:21].reshape(21, devices, part).transpose(1, 0, 2)
        ups = vectors_up[:2].reshape(2, devices, quarter * part).transpose(1, 0, 2)
        vectors = [jnp.pad(v, ((0, 0), (0, 0), (0, 128 - v.shape[2]))) for v in (vectors, ups)]
        vectors = jnp.pad(jnp.concatenate(vectors, axis=1), ((0, 0), (0, 9), (0, 0)))
        grads.append(vectors.reshape(-1, 128).astype(BF16))
        owned = [lax.psum_scatter(g.astype(F32), ("dp", "fsdp"), scatter_dimension=0, tiled=True) for g in grads]
        grad_neighbours = jnp.take(grad_neighbours, near_index, axis=0)
    *split, grad_neighbours = split_gradients(owned, grad_neighbours, near_index, D, quarter, part)
    split[8], split[15] = split[8].reshape(-1), split[15].reshape(-1)
    return (out, gradient, grad_neighbours, *split)


def solution(mesh):
    in_specs = (
        P(("dp", "fsdp"), None),
        P(("dp", "fsdp"), None),
        P(("dp", "fsdp"), None, None),
        P(("dp", "fsdp"), None, None),
        P(("dp", "fsdp"), None),
        P(None, ("dp", "fsdp")),
        P(None, ("dp", "fsdp")),
        P(("dp", "fsdp"), None),
        P(("dp", "fsdp"), None),
        P(("dp", "fsdp"), None),
        P(("dp", "fsdp"), None),
        P(("dp", "fsdp"), None),
        P(("dp", "fsdp"), None),
        P(("dp", "fsdp")),
        P(("dp", "fsdp"), None),
        P(None, ("dp", "fsdp")),
        P(None, ("dp", "fsdp")),
        P(("dp", "fsdp"), None),
        P(("dp", "fsdp"), None),
        P(("dp", "fsdp"), None),
        P(("dp", "fsdp")),
        P(("dp", "fsdp"), None),
        P(("dp", "fsdp"), None),
    )
    out_specs = (
        P(("dp", "fsdp"), None),
        P(("dp", "fsdp"), None),
        P(("dp", "fsdp"), None, None),
        P(None, ("dp", "fsdp")),
        P(None, ("dp", "fsdp")),
        P(("dp", "fsdp"), None),
        P(("dp", "fsdp"), None),
        P(("dp", "fsdp"), None),
        P(("dp", "fsdp"), None),
        P(("dp", "fsdp"), None),
        P(("dp", "fsdp"), None),
        P(("dp", "fsdp")),
        P(("dp", "fsdp"), None),
        P(None, ("dp", "fsdp")),
        P(None, ("dp", "fsdp")),
        P(("dp", "fsdp"), None),
        P(("dp", "fsdp"), None),
        P(("dp", "fsdp"), None),
        P(("dp", "fsdp")),
        P(("dp", "fsdp"), None),
    )
    return jax.shard_map(
        functools.partial(local, (mesh.shape["dp"], mesh.shape["fsdp"])), mesh=mesh, in_specs=in_specs, out_specs=out_specs, check_vma=False)
```

```python
import functools
import itertools
import math
import types
import jax
import jax.numpy as jnp
from jax import lax
from jax.experimental import pallas as pl
from jax.experimental.pallas import tpu as pltpu
from jax.sharding import PartitionSpec as P

HEADS = 12
HEAD_DIM = 64
MESH = pl.DeviceIdType.MESH
ROUTES = ((("z", "x", "y"), 1), (("z", "y", "x"), 1), (("x", "z", "y"), 2), (("y", "z", "x"), 2))
NAMES = ("y", "c", "z", "x")
GATHER_STEPS = (0, 1, 2, 3, 4, 6, 8)
VMEM_MOST = 63 * 2 ** 20
COMPUTE_SHARE, CHAIN_SHARE = 3.5, 3.5
SCATTER_STEPS = (0, 2, 4, 5, 6, 7, 8)
LANDINGS, WINDOW = 6, 8


class Place:
    def __init__(self, dp_size, fsdp_size):
        dp, fsdp = lax.axis_index("dp"), lax.axis_index("fsdp")
        self.size = {"y": dp_size // 2, "c": 2, "z": fsdp_size // 2, "x": 2}
        self.at = {"y": dp // 2, "c": lax.rem(dp, 2), "z": fsdp // 2, "x": lax.rem(fsdp, 2)}

    def device(self, axis, index):
        at = dict(self.at)
        at[axis] = index
        return (at["y"] * 2 + at["c"], at["z"] * 2 + at["x"])

    def partners(self):
        found = []
        for axis in ("c", "x", "y", "z"):
            n, p = self.size[axis], self.at[axis]
            if n == 2:
                found.append((self.device(axis, 1 - p), None))
            elif n > 2:
                found.append((self.device(axis, p + 1), p + 1 < n))
                found.append((self.device(axis, p - 1), p > 0))
        return found


def greet(place):
    barrier = pltpu.get_barrier_semaphore()
    expected = 0
    for device, condition in place.partners():
        if condition is None:
            pl.semaphore_signal(barrier, inc=1, device_id=device, device_id_type=MESH)
            expected = expected + 1
        else:
            @pl.when(condition)
            def _(device=device):
                pl.semaphore_signal(barrier, inc=1, device_id=device, device_id_type=MESH)
            expected = expected + condition.astype(jnp.int32)
    pl.semaphore_wait(barrier, expected)


def when(condition, action):
    if condition is None:
        action()
    else:
        pl.when(condition)(action)


class Sems:
    def __init__(self, send, recv):
        self.send, self.recv, self.used, self.sent = send, recv, 0, []

    def take(self):
        self.used += 1
        return self.used - 1

    def copy(self, slot, src, dst, device):
        return pltpu.make_async_remote_copy(
            src_ref=src, dst_ref=dst, send_sem=self.send.at[slot], recv_sem=self.recv.at[slot],
            device_id=device, device_id_type=MESH)

    def start(self, slot, src, dst, device, condition=None):
        copy = self.copy(slot, src, dst, device)
        when(condition, copy.start)
        self.sent.append((copy, condition))

    def arrived(self, slot, dst, device, condition=None):
        when(condition, self.copy(slot, dst, dst, device).wait_recv)

    def drain(self):
        for copy, condition in self.sent:
            when(condition, copy.wait_send)


def run_schedule(groups, offsets, after=None):
    for tick in range(len(groups) + offsets[-1]):
        for k, group in enumerate(groups):
            if tick - k in offsets:
                for flow in group:
                    next(flow, None)
        if after is not None:
            after(tick)


def routes(width):
    if width % 768:
        return [(ROUTES[0][0], 0, width)]
    found, start = [], 0
    for order, share in ROUTES:
        found.append((order, start, share * width // 6))
        start += share * width // 6
    return found


def copies_of(order, size):
    return 1 + sum(1 if size[d] == 2 else 2 * (size[d] - 1) for d in order)


def gather_flow(place, sems, ref, order, row, height, col, width):
    part = (pl.ds(row, height), pl.ds(col, width))

    def block(done, **fixed):
        where = []
        for name in NAMES:
            if name in fixed:
                where.append(fixed[name])
            elif name in done:
                where.append(pl.ds(0, place.size[name]))
            else:
                where.append(place.at[name])
        return ref.at[(*where, *part)]

    c = place.at["c"]
    sibling = place.device("c", 1 - c)
    done, crossed = set(), []

    def cross(**fixed):
        slot, mine = sems.take(), block(done, c=c, **fixed)
        sems.start(slot, mine, mine, sibling)
        crossed.append((slot, block(done, c=1 - c, **fixed)))

    for axis in order:
        n, p = place.size[axis], place.at[axis]
        final = axis == order[-1]
        if n == 2:
            slot, other = sems.take(), place.device(axis, 1 - p)
            mine = block(done, **{axis: p})
            sems.start(slot, mine, mine, other)
            if final:
                cross(**{axis: p})
            yield
            sems.arrived(slot, block(done, **{axis: 1 - p}), other)
            if final:
                cross(**{axis: 1 - p})
        else:
            for step in range(n - 1):
                up, down = sems.take(), sems.take()
                above, below = place.device(axis, p + 1), place.device(axis, p - 1)
                sent = block(done, **{axis: jnp.maximum(p - step, 0)})
                sems.start(up, sent, sent, above, (p - step >= 0) & (p + 1 < n))
                sent = block(done, **{axis: jnp.minimum(p + step, n - 1)})
                sems.start(down, sent, sent, below, (p + step < n) & (p > 0))
                yield
                sems.arrived(up, block(done, **{axis: jnp.maximum(p - 1 - step, 0)}), above, p - 1 - step >= 0)
                sems.arrived(down, block(done, **{axis: jnp.minimum(p + 1 + step, n - 1)}), below, p + 1 + step < n)
            done.add(axis)
            if final:
                cross()
            continue
        done.add(axis)
    yield
    for slot, theirs in crossed:
        sems.arrived(slot, theirs, sibling)


def pack_small(parts, ups):
    rows = [jnp.pad(ref[...].astype(jnp.float32), ((0, 0), (0, 128 - ref.shape[1]))) for ref in (*parts, *ups)]
    rows = jnp.concatenate(rows, axis=0)
    return jnp.pad(rows, ((0, -rows.shape[0] % 32), (0, 0))).astype(jnp.bfloat16)


def add_blocks(lead, result, *terms):
    def body(where):
        kind = F32 if isinstance(result, list) else result.dtype
        total = terms[0][where].astype(kind)
        for term in terms[1:]:
            total = total + term[where].astype(kind)
        if isinstance(result, list):
            result[where[0]][...] = total
        else:
            result[where] = total

    for index in itertools.product(*map(range, lead)):
        body((*index, slice(None), slice(None)))


def scatter_buffers(size, order, block):
    dims, found = [name for name in NAMES if name != "c"], []
    for axis in order:
        dims = [name for name in dims if name != axis]
        lead = tuple(size[name] for name in dims)
        found.append((() if size[axis] == 2 else (2 * size[axis] - 2,)) + lead + block)
    return found


def scatter_flow(place, sems, sums, buffers, order, out, parts):
    dims = [name for name in NAMES if name != "c"]
    leaving = []

    def leave(slot, src, dst, device, condition=None):
        copy = sems.copy(slot, src, dst, device)
        when(condition, copy.start)
        leaving.append((copy, condition))

    def settle():
        while leaving:
            copy, condition = leaving.pop()
            when(condition, copy.wait_send)

    for axis, buffer in zip(order, buffers):
        n, p = place.size[axis], place.at[axis]
        spot = dims.index(axis)
        rest = [name for name in dims if name != axis]
        lead = tuple(place.size[name] for name in rest) + parts
        last = not rest

        def at(index, sums=sums, spot=spot, count=len(dims)):
            where = [slice(None)] * (count + 3)
            where[spot] = index
            return sums.at[tuple(where)]

        if n == 2:
            slot, other = sems.take(), place.device(axis, 1 - p)
            leave(slot, at(1 - p), buffer, other)
            yield
            sems.arrived(slot, buffer, other)
            settle()
            add_blocks(lead, out if last else buffer, buffer, at(p))
            sums = buffer
        else:
            above, below = place.device(axis, p + 1), place.device(axis, p - 1)
            q = n - 1 - p
            ups = [sems.take() for _ in range(n - 1)]
            downs = [sems.take() for _ in range(n - 1)]

            def from_below(block):
                return buffer.at[jnp.maximum(block - 1, 0)]

            def from_above(block):
                return buffer.at[jnp.minimum(n - 1 + block, 2 * n - 3)]
            for step in range(n - 1):
                up = jnp.minimum(n - 1 - step + p, n - 1)
                down = jnp.maximum(step - q, 0)
                if step:
                    def pass_up(up=up, step=step):
                        sems.copy(ups[step - 1], from_below(up), from_below(up), above).wait_recv()
                        add_blocks(lead, at(up), at(up), from_below(up))
                    def pass_down(down=down, step=step):
                        sems.copy(downs[step - 1], from_above(down), from_above(down), below).wait_recv()
                        add_blocks(lead, at(down), at(down), from_above(down))
                    pl.when((step >= p) & (p > 0) & (p < n - 1))(pass_up)
                    pl.when((step >= q) & (q > 0) & (q < n - 1))(pass_down)
                leave(ups[step], at(up), from_below(up), above, (step >= p) & (p < n - 1))
                leave(downs[step], at(down), from_above(down), below, (step >= q) & (p > 0))
                yield
            sems.arrived(ups[n - 2], from_below(p), above, p > 0)
            sems.arrived(downs[n - 2], from_above(p), below, p < n - 1)
            settle()
            result = out if last else at(p)
            pl.when(p == 0)(lambda: add_blocks(lead, result, at(p), from_above(p)))
            pl.when(p == n - 1)(lambda: add_blocks(lead, result, at(p), from_below(p)))
            pl.when((p > 0) & (p < n - 1))(
                lambda: add_blocks(lead, result, at(p), from_below(p), from_above(p)))
            sums = at(p)
        dims = rest


def split_kernel(D, *refs):
    one, up_one, down_one, two, up_two, down_two, small, near_in, ids = refs[:9]
    (gains_a, biases_a, qkv_a, out_a, cross_q, cross_kv, cross_out, g_up_a, bias_up_a, g_down_a,
     gains_b, biases_b, qkv_b, out_b, g_up_b, bias_up_b, g_down_b, near, sems) = refs[9:]
    copies = [pltpu.make_async_copy(near_in.at[j], near.at[ids[j]], sems.at[j]) for j in range(near.shape[0])]
    for copy in copies:
        copy.start()
    for src, dst in (
            (one[:, 0:3 * D], qkv_a), (one[:, 3 * D:4 * D], out_a), (one[:, 4 * D:5 * D], cross_q),
            (one[:, 5 * D:7 * D], cross_kv), (one[:, 7 * D:8 * D], cross_out), (up_one[...], g_up_a), (down_one[...], g_down_a),
            (two[:, 0:3 * D], qkv_b), (two[:, 3 * D:4 * D], out_b), (up_two[...], g_up_b), (down_two[...], g_down_b)):
        dst[...] = src
    start = 0
    for ref in (gains_a, biases_a, gains_b, biases_b, bias_up_a, bias_up_b):
        ref[...] = small[start:start + ref.shape[0], :ref.shape[1]]
        start += ref.shape[0]
    for copy in copies:
        copy.wait()


def split_gradients(owned, near, near_index, D, quarter, part):
    rows = owned[2].shape[0]
    shapes = [(3, part), (10, part), (part, 3 * D), (part, D), (part, D), (part, 2 * D), (part, D), (part, quarter * D),
              (1, quarter * part), (rows, D), (2, part), (6, part), (part, 3 * D), (part, D), (part, quarter * D),
              (1, quarter * part), (rows, D), near.shape]
    vmem, hbm = pl.BlockSpec(memory_space=pltpu.VMEM), pl.BlockSpec(memory_space=pl.ANY)
    return pl.pallas_call(
        functools.partial(split_kernel, D),
        out_shape=[jax.ShapeDtypeStruct(shape, jnp.float32) for shape in shapes],
        in_specs=[vmem] * 8 + [pl.BlockSpec(memory_space=pltpu.SMEM)],
        out_specs=[vmem] * 17 + [hbm],
        scratch_shapes=[pltpu.SemaphoreType.DMA((near.shape[0],))],
        compiler_params=pltpu.CompilerParams(vmem_limit_bytes=VMEM_MOST),
        name="split_gradients",
    )(*owned, near, near_index)


F32, BF16 = jnp.float32, jnp.bfloat16
SCALE = HEAD_DIM ** (-0.5)
NN, NT = (((1,), (0,)), ((), ())), (((1,), (1,)), ((), ()))
GELU_ONE, GELU_TWO = (2.0 / 3.141592653589793) ** 0.5, 0.044715


def dot(left, right, dims=NN):
    return lax.dot_general(left, right, dims, preferred_element_type=F32)


def span_of(index, width):
    return pl.ds(pl.multiple_of(index * width, width), width)


def row_blocks(count, action, block=64):
    pl.loop(0, count // block)(lambda i: action(span_of(i, block)))


def normalise(h):
    centred = h - jnp.mean(h, axis=-1, keepdims=True)
    inverse = lax.rsqrt(jnp.mean(centred * centred, axis=-1, keepdims=True) + 1e-05)
    return centred * inverse, inverse


def fill_allowed(allowed, segments):
    shape = allowed.shape
    of_key = jnp.broadcast_to(segments[...].astype(F32), shape)
    above = lax.broadcasted_iota(jnp.int32, shape, 0) >= lax.broadcasted_iota(jnp.int32, shape, 1)
    allowed[...] = (above & (of_key.T == of_key)).astype(jnp.int32)


def norm_forward(h_ref, n_ref, gain, shift):
    def block(rows):
        xhat, _ = normalise(h_ref[rows, :].astype(F32))
        n_ref[rows, :] = (xhat * gain + shift).astype(BF16)
    row_blocks(h_ref.shape[0], block)


def norm_backward(h_ref, gain, gn_ref, g_ref, vec_ref, gain_row, shift_row):
    width = h_ref.shape[1]

    def block(i, sums):
        rows = span_of(i, 64)
        xhat, inverse = normalise(h_ref[rows, :].astype(F32))
        gn = gn_ref[rows, :]
        product = gn * xhat
        scaled = gn * gain
        inner = jnp.mean(scaled * xhat, axis=-1, keepdims=True)
        g_ref[rows, :] += inverse * (scaled - jnp.mean(scaled, axis=-1, keepdims=True) - xhat * inner)
        return sums[0] + jnp.sum(product, axis=0, keepdims=True), sums[1] + jnp.sum(gn, axis=0, keepdims=True)
    zero = jnp.zeros((1, width), F32)
    of_gain, of_shift = lax.fori_loop(0, h_ref.shape[0] // 64, block, (zero, zero))
    vec_ref[gain_row:gain_row + 1, :] = of_gain
    vec_ref[shift_row:shift_row + 1, :] = of_shift


def column_sum(values):
    return jnp.sum(values.astype(F32), axis=0, keepdims=True)


def weight_gradient(dst_ref, left_ref, right_ref, tile):
    wide = right_ref.shape[1]

    def block(i):
        rows = span_of(i, 256)
        turned = left_ref[:, rows].T
        for start in range(0, wide, tile):
            dst_ref[rows, start:start + tile] = dot(turned, right_ref[:, start:start + tile]).astype(BF16)
    pl.loop(0, left_ref.shape[1] // 256)(block)


def both_heads(pair, low_half):
    none = jnp.zeros_like(pair)
    return jnp.concatenate([jnp.where(low_half, pair, none), jnp.where(low_half, none, pair)], axis=0)


def of_both(stacked, low_half):
    rows = stacked.shape[0] // 2
    return jnp.where(low_half, stacked[:rows], stacked[rows:])


def lane_half(rows):
    return lax.broadcasted_iota(jnp.int32, (rows, 2 * HEAD_DIM), 1) < HEAD_DIM


def attend(q, k, v, seen):
    low = lane_half(q.shape[0])
    scores = jnp.where(seen, dot(both_heads(q, low), k, NT) * SCALE, -1e30)
    top = jnp.max(scores, axis=-1, keepdims=True)
    raised = jnp.exp(scores - top)
    total = jnp.sum(raised, axis=-1, keepdims=True)
    mixed = dot((raised / total).astype(BF16), v)
    return of_both(mixed, low), top + jnp.log(total)


def attend_back(q, k, v, seen, logsum, gm):
    low = lane_half(q.shape[0])
    q2, gm2 = both_heads(q, low), both_heads(gm, low)
    scores = jnp.where(seen, dot(q2, k, NT) * SCALE, -1e30)
    probs = jnp.exp(scores - logsum)
    grad_probs = dot(gm2, v, NT)
    grad_v = dot(probs.astype(BF16).T, gm2)
    inner = jnp.sum(probs * grad_probs, axis=-1, keepdims=True)
    grad_scores = (probs * (grad_probs - inner)).astype(BF16)
    grad_q = of_both(dot(grad_scores, k), low) * SCALE
    grad_k = dot(grad_scores.T, q2) * SCALE
    return grad_q, grad_k, grad_v


def gelu_both(x):
    square = x * x
    bent = jnp.tanh(GELU_ONE * x * (1.0 + GELU_TWO * square))
    half = 0.5 * (1.0 + bent)
    slope = half + 0.5 * x * (1.0 - bent * bent) * (GELU_ONE * (1.0 + 3.0 * GELU_TWO * square))
    return x * half, slope


def linear(out_ref, left_ref, w_ref, first, count, tile, bias=None):
    def block(j):
        value = dot(left_ref[...], w_ref[:, pl.ds(pl.multiple_of(first + j * tile, 128), tile)])
        if bias is not None:
            value = value + bias(j)
        out_ref[:, span_of(j, tile)] = value.astype(out_ref.dtype)
    pl.loop(0, count // tile)(block)


def self_forward(e, i, h_in, h_out, w, gain, shift, bq, bv, bo, norm):
    D = h_in.shape[1]
    n, packed, mixed, logsum = e.n.at[norm], e.packed.at[i], e.mixed.at[i], e.logsum.at[i]
    norm_forward(h_in, n, gain, shift)
    zero = jnp.zeros_like(bq)

    def bias(j):
        return jnp.where(j == 0, bq, jnp.where(j == 2, bv, zero))
    linear(packed, n, w, 0, 3 * D, D, bias)
    seen = e.allowed[...] != 0
    seen = jnp.concatenate([seen, seen], axis=0)
    for p in range(D // 128):
        a = p * 128
        value, sums = attend(packed[:, a:a + 128], packed[:, D + a:D + a + 128], packed[:, 2 * D + a:2 * D + a + 128], seen)
        mixed[:, a:a + 128] = value.astype(BF16)
        logsum[:, p:p + 1] = sums
    h_out[...] = h_in[...].astype(F32) + dot(mixed[...], w[:, 3 * D:4 * D]) + bo


def cross_pairs(e):
    neighbours, keys = e.near.shape[0], e.near.shape[1]
    spans = e.spans
    return spans, neighbours // spans * keys, e.queries.shape[0] // spans


def cross_seen(e, span):
    near = e.near.shape[0] // e.spans
    return jnp.concatenate([e.near_tokens[pl.ds(span * near + j, 1), :] for j in range(near)], axis=1) != 0


def cross_keys(e, w, bv):
    D = e.near.shape[2]
    near = e.near

    def rows(i):
        for j in range(2):
            value = dot(near[2 * i:2 * i + 2].reshape(-1, D) if isinstance(i, int) else near[pl.ds(2 * i, 2)].reshape(-1, D),
                        w[:, D + j * D:2 * D + j * D])
            if j == 1:
                value = value + bv
            e.kv[span_of(i, 2 * near.shape[1]), j * D:(j + 1) * D] = value.astype(BF16)
    pl.loop(0, near.shape[0] // 2)(rows)


def cross_forward(e, h_in, h_out, w, gain, shift, bq, bo):
    D = h_in.shape[1]
    n, queries, kv, mixed, logsum = e.n.at[1], e.queries, e.kv, e.mixed.at[2], e.logsum.at[2]
    norm_forward(h_in, n, gain, shift)
    linear(queries, n, w, 0, D, D, lambda j: bq)
    spans, keys, size = cross_pairs(e)

    def span(c):
        rows, krows = span_of(c, size), span_of(c, keys)
        seen = cross_seen(e, c)
        for p in range(D // 128):
            a = p * 128
            value, sums = attend(queries[rows, a:a + 128], kv[krows, a:a + 128], kv[krows, D + a:D + a + 128], seen)
            mixed[rows, a:a + 128] = value.astype(BF16)
            logsum[span_of(c, 2 * size), p:p + 1] = sums
    pl.loop(0, spans)(span)
    h_out[...] = h_in[...] + dot(mixed[...], w[:, 3 * D:4 * D]) + bo


def ffn_forward(e, i, h_in, w_up, w_down, gain, shift, b_up, bd, norm, write):
    D, FF = h_in.shape[1], w_up.shape[1]
    n, slope, active, total = e.n.at[norm], e.slope.at[i], e.active.at[i], e.gn
    norm_forward(h_in, n, gain, shift)

    def up(j):
        cols = span_of(j, D)
        value = dot(n[...], w_up[:, cols]) + b_up[:, cols]
        raised, bent = gelu_both(value)
        active[:, cols] = raised.astype(BF16)
        slope[:, cols] = bent
    pl.loop(0, FF // D)(up)
    total[...] = h_in[...] + bd

    def down(j):
        rows = span_of(j, D)
        total[...] += dot(active[:, rows], w_down[rows, :])
    pl.loop(0, FF // D)(down)
    write(total)


def ffn_backward(e, i, h_in, w_up, w_down, gain, norm, rows, b_row):
    D, FF = h_in.shape[1], w_up.shape[1]
    n, slope, active = e.n.at[norm], e.slope.at[i], e.active.at[i]
    g, gb, gh, gn, vec = e.g, e.gb, e.gh, e.gn, e.vec
    gb[...] = g[...].astype(BF16)
    vec[rows[2]:rows[2] + 1, :] = column_sum(gb[...])

    def hidden(j):
        cols = span_of(j, D)
        value = (dot(gb[...], w_down[cols, :], NT) * slope[:, cols].astype(F32)).astype(BF16)
        gh[:, cols] = value
        e.vec_up[i:i + 1, cols] = column_sum(value)
    pl.loop(0, FF // D)(hidden)
    gn[...] = jnp.zeros_like(gn)

    def back(j):
        cols = span_of(j, D)
        gn[...] += dot(gh[:, cols], w_up[:, cols], NT)
    pl.loop(0, FF // D)(back)
    weight_gradient(w_down, active, gb, D)
    e.ship(b_row)
    weight_gradient(w_up, n, gh, D)
    e.ship(b_row + 1)
    norm_backward(h_in, gain, gn, g, vec, rows[0], rows[1])


def self_backward(e, i, h_in, w, gain, norm, rows, ship):
    D = h_in.shape[1]
    n, packed, mixed, logsum = e.n.at[norm], e.packed.at[i], e.mixed.at[i], e.logsum.at[i]
    g, gb, gmix, gpacked, gn, vec = e.g, e.gb, e.gmix, e.gpacked, e.gn, e.vec
    gb[...] = g[...].astype(BF16)
    vec[rows[4]:rows[4] + 1, :] = column_sum(gb[...])
    gmix[...] = dot(gb[...], w[:, 3 * D:4 * D], NT).astype(BF16)
    seen = e.allowed[...] != 0
    seen = jnp.concatenate([seen, seen], axis=0)
    for p in range(D // 128):
        a = p * 128
        q, k, v = (slice(t * D + a, t * D + a + 128) for t in range(3))
        of_q, of_k, of_v = attend_back(
            packed[:, q], packed[:, k], packed[:, v], seen, logsum[:, p:p + 1], gmix[:, a:a + 128])
        gpacked[:, q], gpacked[:, k], gpacked[:, v] = of_q.astype(BF16), of_k.astype(BF16), of_v.astype(BF16)
    vec[rows[2]:rows[2] + 1, :] = column_sum(gpacked[:, :D])
    vec[rows[3]:rows[3] + 1, :] = column_sum(gpacked[:, 2 * D:])
    gn[...] = jnp.zeros_like(gn)

    def back(j):
        cols = span_of(j, D)
        gn[...] += dot(gpacked[:, cols], w[:, cols], NT)
    pl.loop(0, 3)(back)
    weight_gradient(w.at[:, 0:3 * D], n, gpacked, D)
    weight_gradient(w.at[:, 3 * D:4 * D], mixed, gb, D)
    e.ship(ship)
    norm_backward(h_in, gain, gn, g, vec, rows[0], rows[1])


def cross_backward(e, h_in, w, gain, rows, ship):
    D = h_in.shape[1]
    n, queries, kv, mixed, logsum = e.n.at[1], e.queries, e.kv, e.mixed.at[2], e.logsum.at[2]
    g, gb, gmix, gq, gkv, gn, vec = e.g, e.gb, e.gmix, e.gpacked, e.gkv, e.gn, e.vec
    near = e.near
    gb[...] = g[...].astype(BF16)
    vec[rows[4]:rows[4] + 1, :] = column_sum(gb[...])
    gmix[...] = dot(gb[...], w[:, 3 * D:4 * D], NT).astype(BF16)
    spans, keys, size = cross_pairs(e)

    def span(c):
        srows, krows = span_of(c, size), span_of(c, keys)
        seen = cross_seen(e, c)
        for p in range(D // 128):
            a, b = p * 128, D + p * 128
            of_q, of_k, of_v = attend_back(
                queries[srows, a:a + 128], kv[krows, a:a + 128], kv[krows, b:b + 128], seen,
                logsum[span_of(c, 2 * size), p:p + 1], gmix[srows, a:a + 128])
            gq[srows, a:a + 128] = of_q.astype(BF16)
            gkv[krows, a:a + 128], gkv[krows, b:b + 128] = of_k.astype(BF16), of_v.astype(BF16)
    pl.loop(0, spans)(span)
    vec[rows[2]:rows[2] + 1, :] = column_sum(gq[:, :D])
    vec[rows[3]:rows[3] + 1, :] = column_sum(gkv[:, D:])
    gn[...] = dot(gq[:, :D], w[:, 0:D], NT)
    length = near.shape[1]

    def near_rows(i):
        krows = span_of(i, 2 * length)
        value = dot(gkv[krows, :D], w[:, D:2 * D], NT) + dot(gkv[krows, D:], w[:, 2 * D:3 * D], NT)
        e.near_out(i, value.reshape(2, length, D))
    pl.loop(0, near.shape[0] // 2)(near_rows)
    weight_gradient(w.at[:, 0:D], n, gq.at[:, 0:D], D)

    def pair(i):
        cols = span_of(i, 256)
        turned = near[:, :, cols].reshape(-1, 256).T
        for j in range(2):
            w[cols, D + j * D:2 * D + j * D] = dot(turned, gkv[:, j * D:(j + 1) * D]).astype(BF16)
    pl.loop(0, D // 256)(pair)
    weight_gradient(w.at[:, 3 * D:4 * D], mixed, gb, D)
    e.ship(ship)
    norm_backward(h_in, gain, gn, g, vec, rows[0], rows[1])


def block_kernel(spans, *refs):
    (ids, tokens, cotangent, segments, neighbours, stored_tokens, rows, bias_up,
     first, up_a, down_a, second, up_b, down_b,
     out, grad_tokens, grad_near, g_first, g_up_a, g_down_a, g_second, g_up_b, g_down_b, vec, vec_up,
     h, n, packed, mixed, logsum, queries, kv, near, near_tokens, slope, active, allowed,
     gb, gmix, gpacked, gkv, gh, gn, wide, tall, near_stage, loads, ships, nears, near_sems) = refs
    D = tokens.shape[1]
    FF = 4 * D

    def load(number):
        src, dst = (
            (first.at[:, 0:FF], wide.at[0]), (first.at[:, FF:2 * FF], wide.at[1]), (up_a, wide.at[2]), (down_a, tall.at[0]),
            (second, wide.at[0]), (up_b, wide.at[1]), (down_b, tall.at[1]),
            (first.at[:, FF:2 * FF], wide.at[1]), (first.at[:, 0:FF], wide.at[0]))[number]
        return pltpu.make_async_copy(src, dst, loads.at[number])

    def ship_copy(number):
        src, dst = (
            (tall.at[1], g_down_b), (wide.at[1], g_up_b), (wide.at[0], g_second), (tall.at[0], g_down_a),
            (wide.at[2], g_up_a), (wide.at[1], g_first.at[:, FF:2 * FF]), (wide.at[0], g_first.at[:, 0:FF]))[number]
        return pltpu.make_async_copy(src, dst, ships.at[number])

    def near_copy(j):
        return pltpu.make_async_copy(neighbours.at[ids[j]], near.at[j], nears.at[j])

    count = near.shape[0]
    for number in (0, 1, 2, 3, 6):
        load(number).start()
    for j in range(count):
        near_copy(j).start()
    for j in range(count):
        near_tokens[j:j + 1, :] = stored_tokens[pl.ds(ids[j], 1), :]
    grad_near_stage = near_stage

    def near_write(i, half):
        return pltpu.make_async_copy(grad_near_stage.at[i % 2, half], grad_near.at[ids[2 * i + half]], near_sems.at[i % 2, half])

    def near_out(i, value):
        @pl.when(i >= 2)
        def _():
            for half in range(2):
                near_write(i, half).wait()
        grad_near_stage[i % 2] = value
        for half in range(2):
            near_write(i, half).start()

    fill_allowed(allowed, segments)
    e = types.SimpleNamespace(n=n, packed=packed, mixed=mixed, logsum=logsum, queries=queries, kv=kv, near=near, near_tokens=near_tokens,
             slope=slope, active=active, allowed=allowed, g=grad_tokens, gb=gb, gmix=gmix, gpacked=gpacked, gkv=gkv, gh=gh,
             gn=gn, vec=vec, vec_up=vec_up, spans=spans, ship=lambda number: ship_copy(number).start(), near_out=near_out)

    def row(i):
        return rows[i:i + 1, :]
    load(0).wait()
    self_forward(e, 0, tokens, h.at[0], wide.at[0], row(0), row(3), row(6), row(7), row(8), 0)
    load(4).start()
    load(1).wait()
    for j in range(count):
        near_copy(j).wait()
    cross_keys(e, wide.at[1], row(10))
    cross_forward(e, h.at[0], h.at[1], wide.at[1], row(1), row(4), row(9), row(11))
    load(5).start()
    load(2).wait()
    load(3).wait()

    def keep(total):
        h[2] = total[...]
    ffn_forward(e, 0, h.at[1], wide.at[2], tall.at[0], row(2), row(5), bias_up.at[0:1], row(12), 2, keep)
    load(4).wait()
    self_forward(e, 1, h.at[2], h.at[3], wide.at[0], row(13), row(15), row(17), row(18), row(19), 3)
    load(5).wait()
    load(6).wait()

    def finish(total):
        out[...] = total[...].astype(BF16)
    ffn_forward(e, 1, h.at[3], wide.at[1], tall.at[1], row(14), row(16), bias_up.at[1:2], row(20), 4, finish)
    grad_tokens[...] = cotangent[...].astype(F32)
    ffn_backward(e, 1, h.at[3], wide.at[1], tall.at[1], row(14), 4, (14, 16, 20), 0)
    ship_copy(1).wait()
    load(7).start()
    self_backward(e, 1, h.at[2], wide.at[0], row(13), 3, (13, 15, 17, 18, 19), 2)
    ship_copy(2).wait()
    load(8).start()
    ffn_backward(e, 0, h.at[1], wide.at[2], tall.at[0], row(2), 2, (2, 5, 12), 3)
    load(7).wait()
    cross_backward(e, h.at[0], wide.at[1], row(1), (1, 4, 9, 10, 11), 5)
    load(8).wait()
    self_backward(e, 0, tokens, wide.at[0], row(0), 0, (0, 3, 6, 7, 8), 6)
    for number in (0, 3, 4, 5, 6):
        ship_copy(number).wait()
    for i in (count // 2 - 2, count // 2 - 1):
        for half in range(2):
            near_write(i, half).wait()


def run_blocks(tokens, cotangent, segment_ids, neighbours, near_index, neighbour_tokens, spans, rows, bias_up, weights):
    T, D = tokens.shape
    FF = 4 * D
    count, length, _ = neighbours.shape
    vmem, hbm = pl.BlockSpec(memory_space=pltpu.VMEM), pl.BlockSpec(memory_space=pl.ANY)
    shape = jax.ShapeDtypeStruct
    return pl.pallas_call(
        functools.partial(block_kernel, spans),
        out_shape=[shape((T, D), BF16), shape((T, D), F32), shape(neighbours.shape, F32)]
        + [shape(w.shape, BF16) for w in weights] + [shape((24, D), F32), shape((8, FF), F32)],
        in_specs=[pl.BlockSpec(memory_space=pltpu.SMEM), vmem, vmem, vmem, hbm, vmem, vmem, vmem] + [hbm] * 6,
        out_specs=[vmem, vmem, hbm] + [hbm] * 6 + [vmem, vmem],
        scratch_shapes=[
            pltpu.VMEM((4, T, D), F32), pltpu.VMEM((5, T, D), BF16), pltpu.VMEM((2, T, 3 * D), BF16),
            pltpu.VMEM((3, T, D), BF16), pltpu.VMEM((3, 2 * T, 128), F32), pltpu.VMEM((T, D), BF16),
            pltpu.VMEM((count * length, 2 * D), BF16), pltpu.VMEM(neighbours.shape, BF16),
            pltpu.VMEM((count, length), jnp.int32), pltpu.VMEM((2, T, FF), F32), pltpu.VMEM((2, T, FF), BF16),
            pltpu.VMEM((T, T), jnp.int32), pltpu.VMEM((T, D), BF16), pltpu.VMEM((T, D), BF16),
            pltpu.VMEM((T, 3 * D), BF16), pltpu.VMEM((count * length, 2 * D), BF16), pltpu.VMEM((T, FF), BF16),
            pltpu.VMEM((T, D), F32), pltpu.VMEM((3, D, FF), BF16), pltpu.VMEM((2, FF, D), BF16),
            pltpu.VMEM((2, 2, length, D), F32),
            pltpu.SemaphoreType.DMA((9,)), pltpu.SemaphoreType.DMA((7,)), pltpu.SemaphoreType.DMA((count,)),
            pltpu.SemaphoreType.DMA((2, 2)),
        ],
        compiler_params=pltpu.CompilerParams(vmem_limit_bytes=63 * 2 ** 20, has_side_effects=True),
        name="blocks",
    )(near_index, tokens, cotangent, segment_ids, neighbours, neighbour_tokens, rows, bias_up,
      *weights)


def parameter_tile(ref, start, width):
    tile = ref[(slice(None),) * 5 + (pl.ds(start, width),)]
    rows = math.prod(tile.shape[:5])
    if tile.shape[4] % 16:
        return tile.astype(F32).reshape(rows, width).astype(BF16)
    return tile.reshape(rows, width)


def project(out_ref, out_col, lefts, w_ref, w_col, count, bias=None, action=None):
    tile = 256

    def block(j):
        for start in range(0, group, tile):
            here = j * group + start
            weights = parameter_tile(w_ref, pl.multiple_of(w_col + here, tile), tile)
            cols = pl.ds(pl.multiple_of(out_col + here, tile), tile)
            row = 0
            for left in lefts():
                value = dot(left, weights)
                if bias is not None:
                    value = value + bias[:, pl.ds(pl.multiple_of(here, tile), tile)]
                if action is not None:
                    action(cols, value)
                else:
                    out_ref[row:row + left.shape[0], cols] = value.astype(out_ref.dtype)
                row += left.shape[0]
    group = 3 * tile if count % (3 * tile) == 0 else tile
    pl.loop(0, count // group)(block)


def self_pieces(e, i, norm, h_in, h_out, w, chunk, gain, bias_rows):
    D = h_in.shape[1]
    n, packed, mixed, logsum, rows = e.n, e.packed, e.mixed, e.logsum, e.rows
    shift, bq, bv, bo = bias_rows

    def bias(row):
        return rows.at[row:row + 1, :]
    yield chunk, 3.0
    e.free("n")
    norm_forward(h_in, n, rows[gain:gain + 1, :], rows[shift:shift + 1, :])
    e.save("n", norm)
    e.free("packed")
    project(packed, 0, lambda: [n[...]], w, 0, D, bias(bq))
    project(packed, D, lambda: [n[...]], w, D, D)
    yield chunk + 1, 1.0
    project(packed, 2 * D, lambda: [n[...]], w, 2 * D, D, bias(bv))
    e.save("packed", i)
    e.free("mixed")
    e.free("logsum")
    for p in range(D // 128):
        if p % 3 == 0:
            yield chunk + 1, 2.0
        seen = e.allowed[...] != 0
        seen = jnp.concatenate([seen, seen], axis=0)
        a = p * 128
        value, sums = attend(packed[:, a:a + 128], packed[:, D + a:D + a + 128], packed[:, 2 * D + a:2 * D + a + 128], seen)
        mixed[:, a:a + 128] = value.astype(BF16)
        logsum[:, p:p + 1] = sums
    e.save("mixed", i)
    e.save("logsum", i)
    yield chunk + 1, 1.0

    def add(cols, value):
        h_out[:, cols] = h_in[:, cols].astype(F32) + value
    project(None, 0, lambda: [mixed[...]], w, 3 * D, D, bias(bo), add)
    e.save("h", 3 * i)


def cross_pieces(e, norm, h_in, h_out, w, chunk, gain, bias_rows):
    D = h_in.shape[1]
    n, queries, kv, mixed, logsum, rows = e.n, e.queries, e.kv, e.mixed, e.logsum, e.rows
    near, near_tokens, spans = e.near, e.near_tokens, e.spans
    count, length = near.shape[0], near.shape[1]
    shift, bq, bv, bo = bias_rows
    yield chunk, 2.0
    e.free("n")
    norm_forward(h_in, n, rows[gain:gain + 1, :], rows[shift:shift + 1, :])
    e.save("n", norm)
    project(queries, 0, lambda: [n[...]], w, 4 * D, D, rows.at[bq:bq + 1, :])
    e.save("queries", 0)
    flat = lambda: [near[j:j + 2].reshape(2 * length, D) for j in range(0, count, 2)]
    yield chunk, 3.0
    project(kv, 0, flat, w, 5 * D, D)
    yield chunk + 1, 3.0
    project(kv, D, flat, w, 6 * D, D, rows.at[bv:bv + 1, :])
    e.save("kv", 0)
    e.free("mixed")
    e.free("logsum")
    size, each = n.shape[0] // spans, count // spans
    for c in range(spans):
        yield chunk + 1, 1.3
        seen = jnp.concatenate([near_tokens[c * each + j:c * each + j + 1, :] for j in range(each)], axis=1) != 0

        def read(col):
            return kv[c * each * length:(c + 1) * each * length, col:col + 128]
        for p in range(D // 128):
            a = p * 128
            value, sums = attend(queries[c * size:(c + 1) * size, a:a + 128], read(a), read(D + a), seen)
            mixed[c * size:(c + 1) * size, a:a + 128] = value.astype(BF16)
            logsum[2 * c * size:2 * (c + 1) * size, p:p + 1] = sums
    e.save("mixed", 2)
    e.save("logsum", 2)
    yield chunk + 1, 1.0

    def add(cols, value):
        h_out[:, cols] = h_in[:, cols] + value
    project(None, 0, lambda: [mixed[...]], w, 7 * D, D, rows.at[bo:bo + 1, :], add)
    e.save("h", 1)


def ffn_pieces(e, i, norm, h_in, w_up, w_down, chunk, gain, bias_rows, finish):
    D = h_in.shape[1]
    n, slope, active, rows, total = e.n, e.slope, e.active, e.rows, e.total
    shift, bd = bias_rows
    FF = active.shape[1]
    yield chunk, 1.0
    e.free("n")
    norm_forward(h_in, n, rows[gain:gain + 1, :], rows[shift:shift + 1, :])
    e.save("n", norm)
    e.free("slope")
    e.free("active")

    def action(cols, value):
        raised, bent = gelu_both(value)
        active[:, cols] = raised.astype(BF16)
        slope[:, cols] = bent.astype(BF16)
    for j in range(FF // D):
        yield chunk + (2 * j * D) // FF, 1.3
        project(None, j * D, lambda: [n[...]], w_up, j * D, D, e.bias_up.at[i:i + 1, j * D:(j + 1) * D], action)
    e.save("slope", i)
    e.save("active", i)

    def add(cols, value):
        total[:, cols] = h_in[:, cols] + value
    yield chunk + 3, 3.0
    project(None, 0, lambda: [active[...]], w_down, 0, D, rows.at[bd:bd + 1, :], add)
    finish()


def forward_pieces(e, h, tokens, first, up_a, down_a, second, up_b, down_b, small):
    yield 0, 1.5
    lines = [small[index] for index in itertools.product(*map(range, small.shape[:4]))]
    part = e.rows.shape[1] // len(lines)
    wide = e.bias_up.shape[1] // len(lines)
    e.rows[...] = jnp.concatenate([line[:24, :part].astype(F32) for line in lines], axis=1)
    both = jnp.concatenate([line[16:24, :wide].astype(F32) for line in lines], axis=1)
    e.bias_up[...] = both[5:7]
    yield from self_pieces(e, 0, 0, tokens, h.at[0], first, 0, 0, (3, 6, 7, 8))
    yield from cross_pieces(e, 1, h.at[0], h.at[1], first, 2, 1, (4, 9, 10, 11))

    def keep():
        h[2] = e.total[...]
        e.save("h", 2)
    yield from ffn_pieces(e, 0, 2, h.at[1], up_a, down_a, 4, 2, (5, 12), keep)
    yield from self_pieces(e, 1, 3, h.at[2], h.at[3], second, 8, 13, (15, 17, 18, 19))

    def finish():
        e.out[...] = e.total[...].astype(BF16)
    yield from ffn_pieces(e, 1, 4, h.at[3], up_b, down_b, 10, 14, (16, 20), finish)


SAVED = ("n", "packed", "queries", "kv", "mixed", "logsum", "slope", "active")


def forward_kernel(dp_size, fsdp_size, chunks, places, count, spans, *refs):
    n = len(places)
    shards, vectors, (tokens, segments, near, near_tokens) = refs[:n], refs[n:n + 6], refs[n + 6:n + 10]
    refs = refs[n + 10:]
    wholes, (out, h_out, rows), saved = refs[:count - 1], refs[count - 1:count + 2], dict(zip(SAVED, refs[count + 2:count + 10]))
    refs = refs[count + 10:]
    landing, held, (h, allowed, total, bias_up) = refs[:count], dict(zip(SAVED, refs[count:count + 8])), refs[count + 8:count + 12]
    kept, saves, send, recv = refs[count + 12:]
    place = Place(dp_size, fsdp_size)
    here = tuple(place.at[name] for name in NAMES)
    for shard, (which, col) in zip(shards, places):
        landing[which][(*here, slice(None), slice(col, col + shard.shape[1]))] = shard[...]
    landing[count - 1][here] = pack_small(vectors[:4], vectors[4:])
    greet(place)
    sems = Sems(send, recv)
    copies, pending, used = [], {}, [0]

    def keep(slot, which, row, height, col, width):
        where = (slice(None),) * 4 + (pl.ds(row, height), pl.ds(col, width))
        copy = pltpu.make_async_copy(landing[which].at[where], wholes[which].at[where], kept.at[slot])
        copy.start()
        copies.append(copy)

    def chunk_flow(slots, group):
        flows = [
            gather_flow(place, sems, landing[which], order, row, height, start + col, width)
            for which, row, height, start, total in group
            for order, col, width in routes(total)
        ]
        while flows:
            flows = [flow for flow in flows if next(flow, 0) is None]
            if flows:
                yield
        for slot, member in zip(slots, group):
            if member[0] < count - 1:
                keep(slot, *member)

    def save(name, index):
        src, dst = (h.at[index], h_out.at[index]) if name == "h" else (held[name], saved[name].at[index])
        copy = pltpu.make_async_copy(src, dst, saves.at[used[0]])
        copy.start()
        used[0] += 1
        pending[(name, index) if name == "h" else name] = copy

    def free(name):
        if name in pending:
            pending.pop(name).wait()

    fill_allowed(allowed, segments)
    e = types.SimpleNamespace(**held, rows=rows, bias_up=bias_up, allowed=allowed, near=near, near_tokens=near_tokens, spans=spans,
             total=total, out=out, save=save, free=free)
    work = forward_pieces(e, h, tokens, *landing)
    ahead = next(work, None)
    groups, slot = [], 0
    for group in chunks:
        groups.append([chunk_flow(range(slot, slot + len(group)), group)])
        slot += len(group)

    def compute(tick, ahead=[ahead]):
        left = COMPUTE_SHARE
        last = tick == len(groups) + GATHER_STEPS[-1] - 1
        while ahead[0] is not None and ahead[0][0] + GATHER_STEPS[-1] <= tick and (left > 0 or last):
            left -= ahead[0][1]
            ahead[0] = next(work, None)
    run_schedule(groups, GATHER_STEPS, compute)
    sems.drain()
    for copy in copies + list(pending.values()):
        copy.wait()


def arrange_kernel(ids, neighbours, stored_tokens, near, near_tokens, sems):
    copies = [pltpu.make_async_copy(neighbours.at[ids[j]], near.at[j], sems.at[j]) for j in range(near.shape[0])]
    for copy in copies:
        copy.start()
    for j in range(near.shape[0]):
        near_tokens[j:j + 1, :] = stored_tokens[pl.ds(ids[j], 1), :]
    for copy in copies:
        copy.wait()


def arrange(near_index, neighbours, neighbour_tokens):
    vmem, hbm = pl.BlockSpec(memory_space=pltpu.VMEM), pl.BlockSpec(memory_space=pl.ANY)
    return pl.pallas_call(
        arrange_kernel,
        out_shape=[jax.ShapeDtypeStruct(x.shape, x.dtype) for x in (neighbours, neighbour_tokens)],
        in_specs=[pl.BlockSpec(memory_space=pltpu.SMEM), hbm, vmem],
        out_specs=[vmem, vmem],
        scratch_shapes=[pltpu.SemaphoreType.DMA((neighbours.shape[0],))],
        name="arrange_neighbours",
    )(near_index, neighbours, neighbour_tokens)


def gather_and_run(mesh_shape, shards, places, vectors, chunks, tokens, segment_ids, neighbours, neighbour_tokens,
                   spans, collective_id):
    dp_size, fsdp_size = mesh_shape
    size = {"y": dp_size // 2, "c": 2, "z": fsdp_size // 2, "x": 2}
    count = sum(copies_of(order, size) for group in chunks for *_, total in group for order, _, _ in routes(total))
    count += sum(1 for group in chunks for *_, total in group for _ in routes(total))
    lead = tuple(size[name] for name in NAMES)
    shapes = {}
    for shard, (which, col) in zip(shards, places):
        rows, width = shapes.get(which, (shard.shape[0], 0))
        shapes[which] = (rows, max(width, col + shard.shape[1]))
    shapes = [shapes[which] for which in sorted(shapes)] + [(32, 128)]
    T, D = tokens.shape
    FF = 4 * D
    near, length, _ = neighbours.shape
    shape = jax.ShapeDtypeStruct
    held = {"n": ((T, D), BF16, 5), "packed": ((T, 3 * D), BF16, 2), "queries": ((T, D), BF16, 1),
            "kv": ((near * length, 2 * D), BF16, 1), "mixed": ((T, D), BF16, 3), "logsum": ((2 * T, 128), F32, 3),
            "slope": ((T, FF), BF16, 2), "active": ((T, FF), BF16, 2)}
    n, vmem, hbm = len(shards), pl.BlockSpec(memory_space=pltpu.VMEM), pl.BlockSpec(memory_space=pl.ANY)
    results = pl.pallas_call(
        functools.partial(forward_kernel, dp_size, fsdp_size, chunks, places, len(shapes), spans),
        out_shape=[shape(lead + s, BF16) for s in shapes[:-1]]
        + [shape((T, D), BF16), shape((4, T, D), F32), shape((24, D), F32)]
        + [shape((times,) + s, kind) for s, kind, times in held.values()],
        in_specs=[vmem] * (n + 10),
        out_specs=[hbm] * (len(shapes) - 1) + [vmem, hbm, vmem] + [hbm] * 8,
        scratch_shapes=[pltpu.VMEM(lead + s, BF16) for s in shapes]
        + [pltpu.VMEM(s, kind) for s, kind, _ in held.values()]
        + [pltpu.VMEM((4, T, D), F32), pltpu.VMEM((T, T), jnp.int32), pltpu.VMEM((T, D), F32), pltpu.VMEM((2, FF), F32)]
        + [
            pltpu.SemaphoreType.DMA((sum(map(len, chunks)),)),
            pltpu.SemaphoreType.DMA((24,)),
            pltpu.SemaphoreType.DMA((count,)),
            pltpu.SemaphoreType.DMA((count,)),
        ],
        compiler_params=pltpu.CompilerParams(
            collective_id=collective_id, has_side_effects=True, vmem_limit_bytes=63 * 2 ** 20),
        name="gather_and_forward",
    )(*shards, *vectors, tokens, segment_ids, neighbours, neighbour_tokens)
    return results[:len(shapes) - 1], results[len(shapes) - 1:len(shapes) + 2], dict(zip(SAVED, results[len(shapes) + 2:]))


def ffn_chain(e, i, h_in, w_up, w_down, gain, norm, rows):
    D, FF = h_in.shape[1], w_up.shape[1]
    slope, gb, gh, g, gn, vec = e.slope.at[i], e.gb.at[norm], e.gh.at[i], e.g, e.gn, e.vec
    gb[...] = g[...].astype(BF16)
    vec[rows[2]:rows[2] + 1, :] = column_sum(gb[...])
    gn[...] = jnp.zeros_like(gn)

    def hidden(j):
        cols = span_of(j, D)
        value = (dot(gb[...], w_down[cols, :], NT) * slope[:, cols].astype(F32)).astype(BF16)
        gh[:, cols] = value
        e.vec_up[i:i + 1, cols] = column_sum(value)
        gn[...] += dot(value, w_up[:, cols], NT)
    pl.loop(0, FF // D)(hidden)
    e.save("gb", norm)
    e.save("gh", i)
    norm_backward(h_in, gain, gn, g, vec, rows[0], rows[1])


def backward_kernel(*refs):
    cotangent, rows, h_in, slope_in, up, down, g, vec, vec_up, gb_out, gh_out, slope, gb, gh, h, gn, wide, tall, brought, saves = refs
    copies = [
        pltpu.make_async_copy(src, dst, brought.at[i])
        for i, (src, dst) in enumerate(((down, tall), (slope_in.at[1], slope.at[0]), (up, wide), (h_in.at[3], h)))]
    for copy in copies:
        copy.start()
    saved = []

    def save(name, index):
        src, dst = (gb.at[4], gb_out.at[4]) if name == "gb" else (gh.at[0], gh_out.at[1])
        copy = pltpu.make_async_copy(src, dst, saves.at[len(saved)])
        copy.start()
        saved.append(copy)
    e = types.SimpleNamespace(slope=slope, gb=gb, gh=gh, g=g, gn=gn, vec=vec, vec_up=vec_up.at[1:2], save=save)
    g[...] = cotangent[...].astype(F32)
    for copy in copies:
        copy.wait()
    ffn_chain(e, 0, h, wide, tall, rows[14:15, :], 4, (14, 16, 20))
    for copy in saved:
        copy.wait()


def run_backward(cotangent, rows, h, slope, w_up, w_down):
    T, D = cotangent.shape
    FF = 4 * D
    vmem, hbm = pl.BlockSpec(memory_space=pltpu.VMEM), pl.BlockSpec(memory_space=pl.ANY)
    shape = jax.ShapeDtypeStruct
    results = pl.pallas_call(
        backward_kernel,
        out_shape=[shape((T, D), F32), shape((24, D), F32), shape((8, FF), F32), shape((5, T, D), BF16), shape((2, T, FF), BF16)],
        in_specs=[vmem] * 2 + [hbm] * 4,
        out_specs=[vmem] * 3 + [hbm] * 2,
        scratch_shapes=[
            pltpu.VMEM((1, T, FF), BF16), pltpu.VMEM((5, T, D), BF16), pltpu.VMEM((1, T, FF), BF16), pltpu.VMEM((T, D), F32),
            pltpu.VMEM((T, D), F32), pltpu.VMEM((D, FF), BF16), pltpu.VMEM((FF, D), BF16),
            pltpu.SemaphoreType.DMA((4,)), pltpu.SemaphoreType.DMA((2,)),
        ],
        compiler_params=pltpu.CompilerParams(vmem_limit_bytes=VMEM_MOST, has_side_effects=True),
        name="backward",
    )(cotangent, rows, h, slope, w_up, w_down)
    return results[:3], {"gb": results[3], "gh": results[4]}


def gradient_columns(dst, j, left, right, right_col):
    size = dst.shape
    rows = math.prod(size[1:4]) * size[5]

    def block(y):
        turned = left(pl.ds(pl.multiple_of(y * rows, 128), rows)).T
        for start in range(0, size[6], 256):
            value = dot(turned, right[:, right_col + start:right_col + start + 256])
            dst[y, :, :, :, j, :, start:start + 256] = value.reshape(size[1:4] + (size[5], 256)).astype(BF16)
    pl.loop(0, size[0])(block)


def gradient_rows(dsts, left, right):
    Y, C, Z, X, parts, rows, width = dsts[0].shape
    each = 2 * X * rows * parts * len(dsts)

    def block(i):
        y, c, z = i // (C * Z // 2), (i // (Z // 2)) % C, i % (Z // 2)
        turned = left[:, pl.ds(pl.multiple_of(i * each, 128), each)].T
        for start in range(0, width, 256):
            value = dot(turned, right[:, start:start + 256]).reshape(2, X, len(dsts), parts, rows, 256).astype(BF16)
            for half, dst in enumerate(dsts):
                dst[y, c, pl.ds(2 * z, 2), :, :, :, start:start + 256] = value[:, :, half]
    pl.loop(0, left.shape[1] // each)(block)


FACTORS = ("n", "active", "mixed", "gb", "gh", "packed", "logsum", "kv", "queries", "h", "slope")
ORDER = (("active", 1, 0), ("gb", 4, 4), ("packed", 1, 0), ("logsum", 1, 0), ("h", 2, 0), ("n", 4, 0), ("gh", 1, 0), ("n", 3, 1),
         ("mixed", 1, 0), ("slope", 0, 0), ("n", 2, 2), ("kv", 0, 0), ("queries", 0, 0), ("mixed", 2, 1))
LATER = (("active", 0, 0), ("n", 1, 0), ("packed", 0, 0), ("logsum", 2, 0), ("h", 1, 0), ("h", 0, 0), ("logsum", 0, 0), ("n", 0, 1),
         ("mixed", 0, 0))
SLOTS = {("n", 4): 0, ("n", 3): 1, ("n", 2): 2, ("n", 1): 0, ("n", 0): 1, ("mixed", 1): 0, ("mixed", 2): 1, ("mixed", 0): 0}


def chunk_makers(f, need, later, require):
    near = f.near
    D = near.shape[2]

    def rows_of(i, norm):
        def make(dsts):
            require(2 - 2 * i)
            need(("active", i), ("gb", norm))
            gradient_rows(dsts, f.active.at[0], f.gb.at[norm])
            if i:
                later(0)
        return make

    def columns(dst, j, name, index, right, right_col):
        left = getattr(f, name)
        gradient_columns(dst, j, lambda rows: left[SLOTS[name, index], :, rows], right, right_col)

    def up(i, norm, half):
        def make(dsts):
            require(2 - 2 * i)
            need(("n", norm), ("gh", i))
            for j in range(2):
                columns(dsts[0], j, "n", norm, f.gh.at[0], (2 * half + j) * D)
            if i and not half:
                later(1)
        return make

    def query_key(i, norm):
        def make(dsts):
            require(4 - 3 * i)
            need(("n", norm),)
            for j in range(2):
                columns(dsts[0], j, "n", norm, f.gpacked, j * D)
            if i:
                later(7)
        return make

    def value_out(i, norm):
        def make(dsts):
            require(4 - 3 * i)
            need(("n", norm), ("mixed", i))
            columns(dsts[0], 0, "n", norm, f.gpacked, 2 * D)
            columns(dsts[0], 1, "mixed", i, f.gb.at[norm], 0)
            if i:
                later(8)
        return make

    def near_rows(rows):
        return near[:, :, rows].reshape(-1, rows.size)

    def cross_one(dsts):
        require(3)
        need(("n", 1),)
        columns(dsts[0], 0, "n", 1, f.gq, 0)
        gradient_columns(dsts[0], 1, near_rows, f.gkv, 0)

    def cross_two(dsts):
        require(3)
        need(("mixed", 2),)
        gradient_columns(dsts[0], 0, near_rows, f.gkv, D)
        columns(dsts[0], 1, "mixed", 2, f.gb.at[1], 0)
    return (rows_of(1, 4), None, up(1, 4, 1), up(1, 4, 0), value_out(1, 3), query_key(1, 3), rows_of(0, 2), None,
            up(0, 2, 1), up(0, 2, 0), cross_two, cross_one, value_out(0, 0), query_key(0, 0))


def self_back_pieces(f, need, norm, gain, h, lines):
    g, gn, gmix, vec, gpacked, tiles = f.g, f.gn, f.gmix, f.vec, f.gpacked, f.tiles
    D = g.shape[1]
    of_gain, of_shift, of_q, of_v, of_out = (slice(line, line + 1) for line in lines)
    gb = f.gb.at[norm]
    gb[...] = g[...].astype(BF16)
    vec[of_out, :] = column_sum(gb[...])
    gmix[...] = dot(gb[...], tiles[3], NT).astype(BF16)
    packed, logsum = f.packed.at[0], f.logsum.at[0]
    for p in range(D // 128):
        if p % 3 == 0:
            yield 3.0
        seen = f.allowed[...] != 0
        seen = jnp.concatenate([seen, seen], axis=0)
        a = p * 128
        q, k, v = (slice(t * D + a, t * D + a + 128) for t in range(3))
        grad_q, grad_k, grad_v = attend_back(
            packed[:, q], packed[:, k], packed[:, v], seen, logsum[:, p:p + 1], gmix[:, a:a + 128])
        gpacked[:, q], gpacked[:, k], gpacked[:, v] = grad_q.astype(BF16), grad_k.astype(BF16), grad_v.astype(BF16)
    yield 2.0
    vec[of_q, :] = column_sum(gpacked[:, :D])
    vec[of_v, :] = column_sum(gpacked[:, 2 * D:])
    gn[...] = dot(gpacked[:, :D], tiles[0], NT) + dot(gpacked[:, D:2 * D], tiles[1], NT) + dot(gpacked[:, 2 * D:], tiles[2], NT)
    yield 1.5
    norm_backward(h, f.rows[gain:gain + 1, :], gn, g, vec, lines[0], lines[1])


def chain_pieces(f, need, later, load, near_out, spans):
    g, gn, gmix, vec, rows, gq, gkv, tiles = f.g, f.gn, f.gmix, f.vec, f.rows, f.gq, f.gkv, f.tiles
    D = g.shape[1]
    h = f.h.at[0]
    yield 1.0
    need(("g", 0), ("tiles", 0), ("packed", 1), ("logsum", 1), ("h", 2))
    yield from self_back_pieces(f, need, 3, 13, h, (13, 15, 17, 18, 19))
    for number in (2, 3, 4):
        later(number)
    load(2)
    f.stage = 1
    yield 2.0
    need(("tiles", 1), ("slope", 0))
    gb, gh, slope = f.gb.at[2], f.gh.at[0], f.slope.at[0]
    gb[...] = g[...].astype(BF16)
    vec[12:13, :] = column_sum(gb[...])
    for j in range(4):
        if j:
            yield 2.0
        if j == 2:
            load(3)
            need(("tiles", 2),)
        cols, base = slice(j * D, (j + 1) * D), (4, 5, 0, 1)[j]
        value = (dot(gb[...], tiles[base], NT) * slope[:, cols].astype(F32)).astype(BF16)
        gh[:, cols] = value
        f.vec_up[0:1, cols] = column_sum(value)
        back = dot(value, tiles[base + 2], NT)
        gn[...] = gn[...] + back if j else back
    yield 1.5
    load(4)
    need(("h", 1),)
    norm_backward(h, rows[2:3, :], gn, g, vec, 2, 5)
    later(5)
    f.stage = 2
    yield 1.5
    need(("tiles", 3), ("kv", 0), ("queries", 0), ("logsum", 2))
    gb = f.gb.at[1]
    gb[...] = g[...].astype(BF16)
    vec[11:12, :] = column_sum(gb[...])
    gmix[...] = dot(gb[...], tiles[7], NT).astype(BF16)
    near, length = f.near_tokens.shape
    each = near // spans
    keys, size = each * length, g.shape[0] // spans
    queries, kv, logsum = f.queries.at[0], f.kv.at[0], f.logsum.at[0]
    for c in range(spans):
        yield 2.5
        srows, krows = slice(c * size, (c + 1) * size), slice(c * keys, (c + 1) * keys)
        seen = jnp.concatenate([f.near_tokens[c * each + j:c * each + j + 1, :] for j in range(each)], axis=1) != 0
        for p in range(D // 128):
            a, b = p * 128, D + p * 128
            of_q, of_k, of_v = attend_back(
                queries[srows, a:a + 128], kv[krows, a:a + 128], kv[krows, b:b + 128], seen,
                logsum[2 * c * size:2 * (c + 1) * size, p:p + 1], gmix[srows, a:a + 128])
            gq[srows, a:a + 128] = of_q.astype(BF16)
            gkv[krows, a:a + 128], gkv[krows, b:b + 128] = of_k.astype(BF16), of_v.astype(BF16)
    yield 1.0
    later(6)
    vec[9:10, :] = column_sum(gq[...])
    vec[10:11, :] = column_sum(gkv[:, D:])
    gn[...] = dot(gq[...], tiles[4], NT)
    yield 1.5
    need(("h", 0),)
    norm_backward(h, rows[1:2, :], gn, g, vec, 1, 4)
    f.stage = 3
    yield 1.0
    need(("tiles", 4), ("packed", 0), ("logsum", 0))
    yield from self_back_pieces(f, need, 0, 0, f.tokens, (0, 3, 6, 7, 8))
    f.stage = 4
    for i in range(near // 2):
        yield 1.5
        krows = slice(2 * i * length, 2 * (i + 1) * length)
        value = dot(gkv[krows, :D], tiles[5], NT) + dot(gkv[krows, D:], tiles[6], NT)
        near_out(i, value.reshape(2, length, D))
    f.stage = 5


def scatter_routes(parts, width):
    if parts == 1:
        return [(ROUTES[0][0][::-1], 0, 1, 0, width)]
    third = width // 3
    cut = ((0, 1, 0), (1, 1, 0), (0, 2, third), (0, 2, 2 * third))
    return [(order[::-1], *where, third) for (order, _), where in zip(ROUTES, cut)]


def scatter_kernel(dp_size, fsdp_size, chunks, count, plan, spans, *refs):
    factors = dict(zip(FACTORS, refs[:11]))
    (first, second, up, down, g_in, near, near_tokens, rows, tokens, segments, vec_in, vec_up_in) = refs[11:23]
    outs, grad_tokens, grad_near = refs[23:23 + count], refs[23 + count], refs[24 + count]
    refs = refs[25 + count:]
    f = types.SimpleNamespace(**dict(zip(FACTORS, refs[:11])))
    (f.gq, f.gkv, f.tiles, f.gmix, f.gn, f.vec, f.vec_up, f.gpacked, f.allowed, small, near_stage), scratch = refs[11:22], refs[22:-5]
    brought, loads, near_sem, send, recv = refs[-5:]
    f.near, f.near_tokens, f.rows, f.tokens, f.g, f.stage = near, near_tokens, rows, tokens, grad_tokens, 0
    D = tokens.shape[1]
    place = Place(dp_size, fsdp_size)
    sems = Sems(send, recv)
    c = place.at["c"]
    sibling = place.device("c", 1 - c)
    arriving = {}

    def bring(number):
        name, index, slot = (ORDER + LATER)[number]
        copy = pltpu.make_async_copy(factors[name].at[index], getattr(f, name).at[slot], brought.at[number])
        copy.start()
        arriving[name, index] = [copy]

    def load(number):
        def across(array, col, slot):
            return array.at[:, col * D:(col + 1) * D], f.tiles.at[slot]

        def along(j, slot):
            return down.at[j * D:(j + 1) * D, :], f.tiles.at[slot]
        moves = (
            [across(second, j, j) for j in range(4)], [along(0, 4), along(1, 5), across(up, 0, 6), across(up, 1, 7)],
            [along(2, 0), along(3, 1), across(up, 2, 2), across(up, 3, 3)], [across(first, 4 + j, 4 + j) for j in range(4)],
            [across(first, j, j) for j in range(4)])[number]
        arriving["tiles", number] = [
            pltpu.make_async_copy(src, dst, loads.at[4 * number + i]) for i, (src, dst) in enumerate(moves)]
        for copy in arriving["tiles", number]:
            copy.start()
    for number in range(2):
        bring(number)
    arriving["g", 0] = [pltpu.make_async_copy(g_in, grad_tokens, loads.at[20])]
    arriving["g", 0][0].start()
    load(0)
    for number in range(2, len(ORDER)):
        bring(number)
    load(1)

    def need(*wanted):
        for key in wanted:
            for copy in arriving.pop(key, ()):
                copy.wait()
    near_copies = []

    def near_out(i, value):
        if near_copies:
            near_copies.pop().wait()
        near_stage[...] = value
        near_copies.append(pltpu.make_async_copy(near_stage, grad_near.at[2 * i:2 * i + 2], near_sem))
        near_copies[-1].start()

    def later(number):
        bring(len(ORDER) + number)
    chain = chain_pieces(f, need, later, load, near_out, spans)

    def require(stage):
        while f.stage < stage:
            next(chain)
    makers = chunk_makers(f, need, later, require)
    everything = pl.ds(0, place.size["y"])
    lead = tuple(place.size[name] for name in NAMES if name != "c")

    def pack():
        require(4)
        part, wide = outs[-1].shape[0], f.vec_up.shape[1]
        for index in itertools.product(*(range(place.size[name]) for name in NAMES)):
            i = ((index[0] * 2 + index[1]) * place.size["z"] + index[2]) * 2 + index[3]
            devices = dp_size * fsdp_size
            one, many = D // devices, wide // devices
            values = jnp.pad(f.vec[0:21, i * one:(i + 1) * one], ((0, 0), (0, 128 - one)))
            ups = jnp.pad(f.vec_up[0:2, i * many:(i + 1) * many], ((0, 0), (0, 128 - many)))
            blank = jnp.zeros((part - 23, 128), F32)
            small[(*index, 0)] = jnp.concatenate([values, ups, blank], axis=0).astype(BF16)

    def chunk_flow(make, grad, landing, buffers, routed, targets):
        if make is not None:
            make()
        crossing = []
        for _, j, nj, col, width in routed:
            slot, part = sems.take(), (pl.ds(j, nj), slice(None), pl.ds(col, width))
            copy = sems.copy(slot, grad.at[(everything, 1 - c, slice(None), slice(None), *part)],
                             landing.at[(slice(None), slice(None), slice(None), *part)], sibling)
            copy.start()
            crossing.append(copy)
        yield
        for copy in crossing:
            copy.wait()
        add_blocks(lead + landing.shape[3:4], landing, landing, grad.at[:, c])
        flows = []
        for (order, j, nj, col, width), own in zip(routed, buffers):
            part = (pl.ds(j, nj), slice(None), pl.ds(col, width))
            flows.append(scatter_flow(
                place, sems, landing.at[(slice(None), slice(None), slice(None), *part)], own, order,
                [target.at[:, pl.ds(col, width)] for target in targets[j:j + nj]], (nj,)))
        while flows:
            flows = [flow for flow in flows if next(flow, 0) is None]
            if flows:
                yield

    groups = []
    for number, (group, places) in enumerate(zip(chunks, plan)):
        members = []
        for (which, row, height, col, width), (grad, landing, buffers) in zip(group, places):
            if grad is None:
                make, array, targets = pack, small, [outs[which]]
            else:
                make, array = makers[number], scratch[grad]
                fill = [array]
                if makers[(number + 1) % len(makers)] is None:
                    fill = [scratch[plan[number + 1][0][0]], array]
                make = make and functools.partial(make, fill)
                rows_, cols_ = array.shape[5:]
                if width == cols_:
                    targets = [outs[which].at[row + j * rows_:row + (j + 1) * rows_, :] for j in range(2)]
                else:
                    targets = [outs[which].at[:, col + j * cols_:col + (j + 1) * cols_] for j in range(2)]
            members.append(chunk_flow(
                make, array, scratch[landing], [[scratch[b] for b in own] for own in buffers],
                scatter_routes(array.shape[4], array.shape[6]), targets))
        groups.append(members)

    fill_allowed(f.allowed, segments)
    f.vec[...] = vec_in[...]
    f.vec_up[...] = vec_up_in[...]
    greet(place)

    def chain_some(tick):
        left = CHAIN_SHARE
        while f.stage < 5 and left > 0 and tick >= {1: 3, 3: 5}.get(f.stage, 0):
            left -= next(chain, 9.0)
    run_schedule(groups, SCATTER_STEPS, chain_some)
    require(5)
    sems.drain()
    near_copies.pop().wait()


def scatter_all(mesh_shape, factors, weights, g, near, near_tokens, rows, tokens, segment_ids, vec, vec_up, spans, owned, chunks,
                collective_id):
    dp_size, fsdp_size = mesh_shape
    size = {"y": dp_size // 2, "c": 2, "z": fsdp_size // 2, "x": 2}
    lead = tuple(size[name] for name in NAMES if name != "c")
    whole = tuple(size[name] for name in NAMES)
    T, D = tokens.shape
    count_near, length, _ = near.shape
    part = D // (dp_size * fsdp_size)
    shapes, plan, pools, count = [], [], {}, 0

    def new(shape, role, most):
        pool = pools.setdefault((shape, role), [])
        if len(pool) < most:
            shapes.append(pltpu.VMEM(shape, BF16))
            pool.append(len(shapes) - 1)
        else:
            pool.append(pool.pop(0))
        return pool[-1]

    for group in chunks:
        places = []
        for which, *_ in group:
            small = which == len(owned) - 1
            block = (1, 32, 128) if small else (2, part, D)
            grad = None if small else new(whole + block, 0, 3)
            landing = new(lead + block, 1, LANDINGS)
            buffers = []
            for number, (order, _, nj, _, width) in enumerate(scatter_routes(block[0], block[2])):
                buffers.append([
                    new(s, (2, number, i), WINDOW)
                    for i, s in enumerate(scatter_buffers(size, order, (nj, block[1], width)))])
                count += copies_of(order, size)
            places.append((grad, landing, buffers))
        plan.append(places)
    vmem, hbm = pl.BlockSpec(memory_space=pltpu.VMEM), pl.BlockSpec(memory_space=pl.ANY)
    slots = {"active": 1, "gh": 1, "packed": 1, "h": 1, "slope": 1, "n": 3, "mixed": 2, "logsum": 1}
    return pl.pallas_call(
        functools.partial(scatter_kernel, dp_size, fsdp_size, chunks, len(owned), plan, spans),
        out_shape=[jax.ShapeDtypeStruct(shape, F32) for shape in (*owned, (T, D), near.shape)],
        in_specs=[hbm] * 16 + [vmem] * 7,
        out_specs=[vmem] * (len(owned) + 1) + [hbm],
        scratch_shapes=[
            pltpu.VMEM((slots.get(name, factors[name].shape[0]),) + factors[name].shape[1:], factors[name].dtype)
            for name in FACTORS
        ] + [
            pltpu.VMEM((T, D), BF16), pltpu.VMEM((count_near * length, 2 * D), BF16), pltpu.VMEM((8, D, D), BF16),
            pltpu.VMEM((T, D), BF16), pltpu.VMEM((T, D), F32), pltpu.VMEM((24, D), F32), pltpu.VMEM(vec_up.shape, F32),
            pltpu.VMEM((T, 3 * D), BF16), pltpu.VMEM((T, T), jnp.int32), pltpu.VMEM(whole + (1, 32, 128), BF16), pltpu.VMEM((2, length, D), F32),
        ] + shapes + [
            pltpu.SemaphoreType.DMA((len(ORDER) + len(LATER),)),
            pltpu.SemaphoreType.DMA((21,)),
            pltpu.SemaphoreType.DMA,
            pltpu.SemaphoreType.DMA((count,)),
            pltpu.SemaphoreType.DMA((count,)),
        ],
        compiler_params=pltpu.CompilerParams(
            collective_id=collective_id, has_side_effects=True, vmem_limit_bytes=VMEM_MOST),
        name="scatter_gradients",
    )(*[factors[name] for name in FACTORS], *weights, g, near, near_tokens, rows, tokens, segment_ids, vec, vec_up)


PLACES = ((0, 0), (0, 3), (0, 4), (0, 5), (0, 7), (1, 0), (2, 0), (3, 0), (3, 3), (4, 0), (5, 0))


def chunk_table(D, part, long):
    table = [((0, 0, part, i * 2 * D, 2 * D),) for i in range(4)]
    for first in (1, 3):
        if first == 3:
            table += [((3, 0, part, i * 2 * D, 2 * D),) for i in range(2)]
        table += [((first + first // 3, 0, part, i * 2 * D, 2 * D),) for i in range(2)]
        table += [((first + first // 3 + 1, i * long // 2, long // 2, 0, D),) for i in range(2)]
    table[0] += ((6, 0, 32, 0, 128),)
    return table


def local(mesh_shape, *arrays):
    (tokens, segment_ids, neighbours, neighbour_ids, neighbour_tokens, gains_one, biases_one, w_qkv_one, w_out_one,
     w_cross_q, w_cross_kv, w_cross_out, w_up_one, bias_up_one, w_down_one, gains_two, biases_two, w_qkv_two,
     w_out_two, w_up_two, bias_up_two, w_down_two, cotangent) = arrays
    row_count, D = tokens.shape
    FF = w_up_one.shape[1]
    devices = mesh_shape[0] * mesh_shape[1]
    part = D // devices
    quarter = FF // D
    vectors = [gains_one, biases_one, gains_two, biases_two]
    shards = [w_qkv_one, w_out_one, w_cross_q, w_cross_kv, w_cross_out, w_up_one, w_down_one, w_qkv_two, w_out_two,
              w_up_two, w_down_two]
    kernels = part % 8 == 0
    table = chunk_table(D, part, w_down_one.shape[0])
    store_count = neighbours.shape[0]
    spans = neighbour_ids.shape[1]
    near_index = neighbour_ids.reshape(-1) % store_count
    if kernels:
        ups = [bias_up_one.reshape(1, -1), bias_up_two.reshape(1, -1)]
        near, near_tokens = arrange(near_index, neighbours, neighbour_tokens)
        wholes, (out, h, rows), saved = gather_and_run(
            mesh_shape, shards, tuple((w, c * D) for w, c in PLACES), vectors + ups, table, tokens, segment_ids,
            near, near_tokens, spans, 1)
        wholes = [w.reshape(-1, w.shape[-1]) for w in wholes]
        (gradient, vec, vec_up), made = run_backward(cotangent, rows, h, saved["slope"], *wholes[4:6])
        owned = [(w.shape[0] // devices, w.shape[1]) for w in wholes] + [(32, 128)]
        *owned, gradient, grad_neighbours = scatter_all(
            mesh_shape, {**saved, **made, "h": h}, (wholes[0], wholes[3], wholes[1], wholes[2]), gradient, near, near_tokens, rows,
            tokens, segment_ids, vec, vec_up, spans, owned, table[::-1], 2)
    else:
        small = jnp.concatenate(vectors + [bias_up_one.reshape(-1, part), bias_up_two.reshape(-1, part)])
        small = jnp.pad(small, ((0, -small.shape[0] % 32), (0, -part % 128)))
        sides = [[] for _ in range(6)]
        for shard, (which, _) in zip(shards, PLACES):
            sides[which].append(shard)
        shards = [jnp.concatenate(side, axis=1) for side in sides] + [small]
        *wholes, smalls = [lax.all_gather(s, ("dp", "fsdp"), axis=0, tiled=True) for s in shards]
        smalls = smalls.reshape(devices, -1, smalls.shape[-1])[:, :, :part]
        rows = smalls[:, :21].transpose(1, 0, 2).reshape(21, D)
        bias_up = [smalls[:, 21 + i * quarter:21 + (i + 1) * quarter].reshape(FF) for i in range(2)]
        rows = jnp.pad(rows.astype(F32), ((0, 3), (0, 0)))
        bias_up = jnp.pad(jnp.stack(bias_up).astype(F32), ((0, 6), (0, 0)))
        out, gradient, grad_neighbours, *grads, vectors, vectors_up = run_blocks(
            tokens, cotangent, segment_ids, neighbours, near_index, neighbour_tokens, spans, rows, bias_up, wholes)
        vectors = vectors[:21].reshape(21, devices, part).transpose(1, 0, 2)
        ups = vectors_up[:2].reshape(2, devices, quarter * part).transpose(1, 0, 2)
        vectors = [jnp.pad(v, ((0, 0), (0, 0), (0, 128 - v.shape[2]))) for v in (vectors, ups)]
        vectors = jnp.pad(jnp.concatenate(vectors, axis=1), ((0, 0), (0, 9), (0, 0)))
        grads.append(vectors.reshape(-1, 128).astype(BF16))
        owned = [lax.psum_scatter(g.astype(F32), ("dp", "fsdp"), scatter_dimension=0, tiled=True) for g in grads]
        grad_neighbours = jnp.take(grad_neighbours, near_index, axis=0)
    *split, grad_neighbours = split_gradients(owned, grad_neighbours, near_index, D, quarter, part)
    split[8], split[15] = split[8].reshape(-1), split[15].reshape(-1)
    return (out, gradient, grad_neighbours, *split)


def solution(mesh):
    in_specs = (
        P(("dp", "fsdp"), None),
        P(("dp", "fsdp"), None),
        P(("dp", "fsdp"), None, None),
        P(("dp", "fsdp"), None, None),
        P(("dp", "fsdp"), None),
        P(None, ("dp", "fsdp")),
        P(None, ("dp", "fsdp")),
        P(("dp", "fsdp"), None),
        P(("dp", "fsdp"), None),
        P(("dp", "fsdp"), None),
        P(("dp", "fsdp"), None),
        P(("dp", "fsdp"), None),
        P(("dp", "fsdp"), None),
        P(("dp", "fsdp")),
        P(("dp", "fsdp"), None),
        P(None, ("dp", "fsdp")),
        P(None, ("dp", "fsdp")),
        P(("dp", "fsdp"), None),
        P(("dp", "fsdp"), None),
        P(("dp", "fsdp"), None),
        P(("dp", "fsdp")),
        P(("dp", "fsdp"), None),
        P(("dp", "fsdp"), None),
    )
    out_specs = (
        P(("dp", "fsdp"), None),
        P(("dp", "fsdp"), None),
        P(("dp", "fsdp"), None, None),
        P(None, ("dp", "fsdp")),
        P(None, ("dp", "fsdp")),
        P(("dp", "fsdp"), None),
        P(("dp", "fsdp"), None),
        P(("dp", "fsdp"), None),
        P(("dp", "fsdp"), None),
        P(("dp", "fsdp"), None),
        P(("dp", "fsdp"), None),
        P(("dp", "fsdp")),
        P(("dp", "fsdp"), None),
        P(None, ("dp", "fsdp")),
        P(None, ("dp", "fsdp")),
        P(("dp", "fsdp"), None),
        P(("dp", "fsdp"), None),
        P(("dp", "fsdp"), None),
        P(("dp", "fsdp")),
        P(("dp", "fsdp"), None),
    )
    return jax.shard_map(
        functools.partial(local, (mesh.shape["dp"], mesh.shape["fsdp"])), mesh=mesh, in_specs=in_specs, out_specs=out_specs, check_vma=False)
```

```python
import functools
import itertools
import math
import types
import jax
import jax.numpy as jnp
from jax import lax
from jax.experimental import pallas as pl
from jax.experimental.pallas import tpu as pltpu
from jax.sharding import PartitionSpec as P

HEADS = 12
HEAD_DIM = 64
MESH = pl.DeviceIdType.MESH
ROUTES = ((("z", "x", "y"), 1), (("z", "y", "x"), 1), (("x", "z", "y"), 2), (("y", "z", "x"), 2))
NAMES = ("y", "c", "z", "x")
GATHER_STEPS = (0, 1, 2, 3, 4, 6, 7)
VMEM_MOST = 63 * 2 ** 20
COMPUTE_SHARE, CHAIN_SHARE = 3.5, 3.5
SCATTER_STEPS = (0, 1, 3, 4, 5, 6, 7)
LANDINGS, WINDOW = 6, 8


class Place:
    def __init__(self, dp_size, fsdp_size):
        dp, fsdp = lax.axis_index("dp"), lax.axis_index("fsdp")
        self.size = {"y": dp_size // 2, "c": 2, "z": fsdp_size // 2, "x": 2}
        self.at = {"y": dp // 2, "c": lax.rem(dp, 2), "z": fsdp // 2, "x": lax.rem(fsdp, 2)}

    def device(self, axis, index):
        at = dict(self.at)
        at[axis] = index
        return (at["y"] * 2 + at["c"], at["z"] * 2 + at["x"])

    def partners(self):
        found = []
        for axis in ("c", "x", "y", "z"):
            n, p = self.size[axis], self.at[axis]
            if n == 2:
                found.append((self.device(axis, 1 - p), None))
            elif n > 2:
                found.append((self.device(axis, p + 1), p + 1 < n))
                found.append((self.device(axis, p - 1), p > 0))
        return found


def greet(place):
    barrier = pltpu.get_barrier_semaphore()
    expected = 0
    for device, condition in place.partners():
        if condition is None:
            pl.semaphore_signal(barrier, inc=1, device_id=device, device_id_type=MESH)
            expected = expected + 1
        else:
            @pl.when(condition)
            def _(device=device):
                pl.semaphore_signal(barrier, inc=1, device_id=device, device_id_type=MESH)
            expected = expected + condition.astype(jnp.int32)
    pl.semaphore_wait(barrier, expected)


def when(condition, action):
    if condition is None:
        action()
    else:
        pl.when(condition)(action)


class Sems:
    def __init__(self, send, recv):
        self.send, self.recv, self.used, self.sent = send, recv, 0, []

    def take(self):
        self.used += 1
        return self.used - 1

    def copy(self, slot, src, dst, device):
        return pltpu.make_async_remote_copy(
            src_ref=src, dst_ref=dst, send_sem=self.send.at[slot], recv_sem=self.recv.at[slot],
            device_id=device, device_id_type=MESH)

    def start(self, slot, src, dst, device, condition=None):
        copy = self.copy(slot, src, dst, device)
        when(condition, copy.start)
        self.sent.append((copy, condition))

    def arrived(self, slot, dst, device, condition=None):
        when(condition, self.copy(slot, dst, dst, device).wait_recv)

    def drain(self):
        for copy, condition in self.sent:
            when(condition, copy.wait_send)


def run_schedule(groups, offsets, after=None):
    for tick in range(len(groups) + offsets[-1]):
        for k, group in enumerate(groups):
            if tick - k in offsets:
                for flow in group:
                    next(flow, None)
        if after is not None:
            after(tick)


def routes(width):
    if width % 768:
        return [(ROUTES[0][0], 0, width)]
    found, start = [], 0
    for order, share in ROUTES:
        found.append((order, start, share * width // 6))
        start += share * width // 6
    return found


def copies_of(order, size):
    return 1 + sum(1 if size[d] == 2 else 2 * (size[d] - 1) for d in order)


def gather_flow(place, sems, ref, order, row, height, col, width):
    part = (pl.ds(row, height), pl.ds(col, width))

    def block(done, **fixed):
        where = []
        for name in NAMES:
            if name in fixed:
                where.append(fixed[name])
            elif name in done:
                where.append(pl.ds(0, place.size[name]))
            else:
                where.append(place.at[name])
        return ref.at[(*where, *part)]

    c = place.at["c"]
    sibling = place.device("c", 1 - c)
    done, crossed = set(), []

    def cross(**fixed):
        slot, mine = sems.take(), block(done, c=c, **fixed)
        sems.start(slot, mine, mine, sibling)
        crossed.append((slot, block(done, c=1 - c, **fixed)))

    for axis in order:
        n, p = place.size[axis], place.at[axis]
        final = axis == order[-1]
        if n == 2:
            slot, other = sems.take(), place.device(axis, 1 - p)
            mine = block(done, **{axis: p})
            sems.start(slot, mine, mine, other)
            if final:
                cross(**{axis: p})
            yield
            sems.arrived(slot, block(done, **{axis: 1 - p}), other)
            if final:
                cross(**{axis: 1 - p})
        else:
            for step in range(n - 1):
                up, down = sems.take(), sems.take()
                above, below = place.device(axis, p + 1), place.device(axis, p - 1)
                sent = block(done, **{axis: jnp.maximum(p - step, 0)})
                sems.start(up, sent, sent, above, (p - step >= 0) & (p + 1 < n))
                sent = block(done, **{axis: jnp.minimum(p + step, n - 1)})
                sems.start(down, sent, sent, below, (p + step < n) & (p > 0))
                yield
                sems.arrived(up, block(done, **{axis: jnp.maximum(p - 1 - step, 0)}), above, p - 1 - step >= 0)
                sems.arrived(down, block(done, **{axis: jnp.minimum(p + 1 + step, n - 1)}), below, p + 1 + step < n)
            done.add(axis)
            if final:
                cross()
            continue
        done.add(axis)
    yield
    for slot, theirs in crossed:
        sems.arrived(slot, theirs, sibling)


def pack_small(parts, ups):
    rows = [jnp.pad(ref[...].astype(jnp.float32), ((0, 0), (0, 128 - ref.shape[1]))) for ref in (*parts, *ups)]
    rows = jnp.concatenate(rows, axis=0)
    return jnp.pad(rows, ((0, -rows.shape[0] % 32), (0, 0))).astype(jnp.bfloat16)


def add_blocks(lead, result, *terms):
    def body(where):
        kind = F32 if isinstance(result, list) else result.dtype
        total = terms[0][where].astype(kind)
        for term in terms[1:]:
            total = total + term[where].astype(kind)
        if isinstance(result, list):
            result[where[0]][...] = total
        else:
            result[where] = total

    for index in itertools.product(*map(range, lead)):
        body((*index, slice(None), slice(None)))


def scatter_buffers(size, order, block):
    dims, found = [name for name in NAMES if name != "c"], []
    for axis in order:
        dims = [name for name in dims if name != axis]
        lead = tuple(size[name] for name in dims)
        found.append((() if size[axis] == 2 else (2 * size[axis] - 2,)) + lead + block)
    return found


def scatter_flow(place, sems, sums, buffers, order, out, parts):
    dims = [name for name in NAMES if name != "c"]
    leaving = []

    def leave(slot, src, dst, device, condition=None):
        copy = sems.copy(slot, src, dst, device)
        when(condition, copy.start)
        leaving.append((copy, condition))

    def settle():
        while leaving:
            copy, condition = leaving.pop()
            when(condition, copy.wait_send)

    for axis, buffer in zip(order, buffers):
        n, p = place.size[axis], place.at[axis]
        spot = dims.index(axis)
        rest = [name for name in dims if name != axis]
        lead = tuple(place.size[name] for name in rest) + parts
        last = not rest

        def at(index, sums=sums, spot=spot, count=len(dims)):
            where = [slice(None)] * (count + 3)
            where[spot] = index
            return sums.at[tuple(where)]

        if n == 2:
            slot, other = sems.take(), place.device(axis, 1 - p)
            leave(slot, at(1 - p), buffer, other)
            yield
            sems.arrived(slot, buffer, other)
            settle()
            add_blocks(lead, out if last else buffer, buffer, at(p))
            sums = buffer
        else:
            above, below = place.device(axis, p + 1), place.device(axis, p - 1)
            q = n - 1 - p
            ups = [sems.take() for _ in range(n - 1)]
            downs = [sems.take() for _ in range(n - 1)]

            def from_below(block):
                return buffer.at[jnp.maximum(block - 1, 0)]

            def from_above(block):
                return buffer.at[jnp.minimum(n - 1 + block, 2 * n - 3)]
            for step in range(n - 1):
                up = jnp.minimum(n - 1 - step + p, n - 1)
                down = jnp.maximum(step - q, 0)
                if step:
                    def pass_up(up=up, step=step):
                        sems.copy(ups[step - 1], from_below(up), from_below(up), above).wait_recv()
                        add_blocks(lead, at(up), at(up), from_below(up))
                    def pass_down(down=down, step=step):
                        sems.copy(downs[step - 1], from_above(down), from_above(down), below).wait_recv()
                        add_blocks(lead, at(down), at(down), from_above(down))
                    pl.when((step >= p) & (p > 0) & (p < n - 1))(pass_up)
                    pl.when((step >= q) & (q > 0) & (q < n - 1))(pass_down)
                leave(ups[step], at(up), from_below(up), above, (step >= p) & (p < n - 1))
                leave(downs[step], at(down), from_above(down), below, (step >= q) & (p > 0))
                yield
            sems.arrived(ups[n - 2], from_below(p), above, p > 0)
            sems.arrived(downs[n - 2], from_above(p), below, p < n - 1)
            settle()
            result = out if last else at(p)
            pl.when(p == 0)(lambda: add_blocks(lead, result, at(p), from_above(p)))
            pl.when(p == n - 1)(lambda: add_blocks(lead, result, at(p), from_below(p)))
            pl.when((p > 0) & (p < n - 1))(
                lambda: add_blocks(lead, result, at(p), from_below(p), from_above(p)))
            sums = at(p)
        dims = rest


def split_kernel(D, *refs):
    one, up_one, down_one, two, up_two, down_two, small, out_in, tokens_in, near_in, ids = refs[:11]
    (gains_a, biases_a, qkv_a, out_a, cross_q, cross_kv, cross_out, g_up_a, bias_up_a, g_down_a,
     gains_b, biases_b, qkv_b, out_b, g_up_b, bias_up_b, g_down_b, out, grad_tokens, near, stage, sems) = refs[11:]
    count = near.shape[0]
    arriving = [pltpu.make_async_copy(near_in.at[j], stage.at[j], sems.at[j]) for j in range(count)]
    leaving = [pltpu.make_async_copy(stage.at[j], near.at[ids[j]], sems.at[count + j]) for j in range(count)]
    for copy in arriving:
        copy.start()
    for src, dst in (
            (one[:, 0:3 * D], qkv_a), (one[:, 3 * D:4 * D], out_a), (one[:, 4 * D:5 * D], cross_q),
            (one[:, 5 * D:7 * D], cross_kv), (one[:, 7 * D:8 * D], cross_out), (up_one[...], g_up_a), (down_one[...], g_down_a),
            (two[:, 0:3 * D], qkv_b), (two[:, 3 * D:4 * D], out_b), (up_two[...], g_up_b), (down_two[...], g_down_b),
            (out_in[...], out), (tokens_in[...], grad_tokens)):
        dst[...] = src
    for came, goes in zip(arriving, leaving):
        came.wait()
        goes.start()
    start = 0
    for ref in (gains_a, biases_a, gains_b, biases_b, bias_up_a, bias_up_b):
        ref[...] = small[start:start + ref.shape[0], :ref.shape[1]]
        start += ref.shape[0]
    for copy in leaving:
        copy.wait()


def split_gradients(owned, out, grad_tokens, near, near_index, D, quarter, part):
    rows = owned[2].shape[0]
    shapes = [(3, part), (10, part), (part, 3 * D), (part, D), (part, D), (part, 2 * D), (part, D), (part, quarter * D),
              (1, quarter * part), (rows, D), (2, part), (6, part), (part, 3 * D), (part, D), (part, quarter * D),
              (1, quarter * part), (rows, D), out.shape, grad_tokens.shape, near.shape]
    vmem, hbm = pl.BlockSpec(memory_space=pltpu.VMEM), pl.BlockSpec(memory_space=pl.ANY)
    return pl.pallas_call(
        functools.partial(split_kernel, D),
        out_shape=[jax.ShapeDtypeStruct(shape, BF16 if i == 17 else F32) for i, shape in enumerate(shapes)],
        in_specs=[vmem] * 9 + [hbm, pl.BlockSpec(memory_space=pltpu.SMEM)],
        out_specs=[vmem] * 19 + [hbm],
        scratch_shapes=[pltpu.VMEM(near.shape, F32), pltpu.SemaphoreType.DMA((2 * near.shape[0],))],
        compiler_params=pltpu.CompilerParams(vmem_limit_bytes=VMEM_MOST),
        name="split_gradients",
    )(*owned, out, grad_tokens, near, near_index)


F32, BF16 = jnp.float32, jnp.bfloat16
SCALE = HEAD_DIM ** (-0.5)
NN, NT = (((1,), (0,)), ((), ())), (((1,), (1,)), ((), ()))
GELU_ONE, GELU_TWO = (2.0 / 3.141592653589793) ** 0.5, 0.044715


def dot(left, right, dims=NN):
    return lax.dot_general(left, right, dims, preferred_element_type=F32)


def span_of(index, width):
    return pl.ds(pl.multiple_of(index * width, width), width)


def row_blocks(count, action, block=64):
    pl.loop(0, count // block)(lambda i: action(span_of(i, block)))


def normalise(h):
    centred = h - jnp.mean(h, axis=-1, keepdims=True)
    inverse = lax.rsqrt(jnp.mean(centred * centred, axis=-1, keepdims=True) + 1e-05)
    return centred * inverse, inverse


def fill_allowed(allowed, segments):
    shape = allowed.shape
    of_key = jnp.broadcast_to(segments[...].astype(F32), shape)
    above = lax.broadcasted_iota(jnp.int32, shape, 0) >= lax.broadcasted_iota(jnp.int32, shape, 1)
    allowed[...] = (above & (of_key.T == of_key)).astype(jnp.int32)


def norm_forward(h_ref, n_ref, gain, shift):
    def block(rows):
        xhat, _ = normalise(h_ref[rows, :].astype(F32))
        n_ref[rows, :] = (xhat * gain + shift).astype(BF16)
    row_blocks(h_ref.shape[0], block)


def norm_backward(h_ref, gain, gn_ref, g_ref, vec_ref, gain_row, shift_row):
    width = h_ref.shape[1]

    def block(i, sums):
        rows = span_of(i, 64)
        xhat, inverse = normalise(h_ref[rows, :].astype(F32))
        gn = gn_ref[rows, :]
        product = gn * xhat
        scaled = gn * gain
        inner = jnp.mean(scaled * xhat, axis=-1, keepdims=True)
        g_ref[rows, :] += inverse * (scaled - jnp.mean(scaled, axis=-1, keepdims=True) - xhat * inner)
        return sums[0] + jnp.sum(product, axis=0, keepdims=True), sums[1] + jnp.sum(gn, axis=0, keepdims=True)
    zero = jnp.zeros((1, width), F32)
    of_gain, of_shift = lax.fori_loop(0, h_ref.shape[0] // 64, block, (zero, zero))
    vec_ref[gain_row:gain_row + 1, :] = of_gain
    vec_ref[shift_row:shift_row + 1, :] = of_shift


def column_sum(values):
    return jnp.sum(values.astype(F32), axis=0, keepdims=True)


def weight_gradient(dst_ref, left_ref, right_ref, tile):
    wide = right_ref.shape[1]

    def block(i):
        rows = span_of(i, 256)
        turned = left_ref[:, rows].T
        for start in range(0, wide, tile):
            dst_ref[rows, start:start + tile] = dot(turned, right_ref[:, start:start + tile]).astype(BF16)
    pl.loop(0, left_ref.shape[1] // 256)(block)


def both_heads(pair, low_half):
    none = jnp.zeros_like(pair)
    return jnp.concatenate([jnp.where(low_half, pair, none), jnp.where(low_half, none, pair)], axis=0)


def of_both(stacked, low_half):
    rows = stacked.shape[0] // 2
    return jnp.where(low_half, stacked[:rows], stacked[rows:])


def lane_half(rows):
    return lax.broadcasted_iota(jnp.int32, (rows, 2 * HEAD_DIM), 1) < HEAD_DIM


def attend(q, k, v, seen):
    low = lane_half(q.shape[0])
    scores = jnp.where(seen, dot(both_heads(q, low), k, NT) * SCALE, -1e30)
    top = jnp.max(scores, axis=-1, keepdims=True)
    raised = jnp.exp(scores - top)
    total = jnp.sum(raised, axis=-1, keepdims=True)
    mixed = dot((raised / total).astype(BF16), v)
    return of_both(mixed, low), top + jnp.log(total)


def attend_back(q, k, v, seen, logsum, gm):
    low = lane_half(q.shape[0])
    q2, gm2 = both_heads(q, low), both_heads(gm, low)
    scores = jnp.where(seen, dot(q2, k, NT) * SCALE, -1e30)
    probs = jnp.exp(scores - logsum)
    grad_probs = dot(gm2, v, NT)
    grad_v = dot(probs.astype(BF16).T, gm2)
    inner = jnp.sum(probs * grad_probs, axis=-1, keepdims=True)
    grad_scores = (probs * (grad_probs - inner)).astype(BF16)
    grad_q = of_both(dot(grad_scores, k), low) * SCALE
    grad_k = dot(grad_scores.T, q2) * SCALE
    return grad_q, grad_k, grad_v


def gelu_both(x):
    square = x * x
    bent = jnp.tanh(GELU_ONE * x * (1.0 + GELU_TWO * square))
    half = 0.5 * (1.0 + bent)
    slope = half + 0.5 * x * (1.0 - bent * bent) * (GELU_ONE * (1.0 + 3.0 * GELU_TWO * square))
    return x * half, slope


def linear(out_ref, left_ref, w_ref, first, count, tile, bias=None):
    def block(j):
        value = dot(left_ref[...], w_ref[:, pl.ds(pl.multiple_of(first + j * tile, 128), tile)])
        if bias is not None:
            value = value + bias(j)
        out_ref[:, span_of(j, tile)] = value.astype(out_ref.dtype)
    pl.loop(0, count // tile)(block)


def self_forward(e, i, h_in, h_out, w, gain, shift, bq, bv, bo, norm):
    D = h_in.shape[1]
    n, packed, mixed, logsum = e.n.at[norm], e.packed.at[i], e.mixed.at[i], e.logsum.at[i]
    norm_forward(h_in, n, gain, shift)
    zero = jnp.zeros_like(bq)

    def bias(j):
        return jnp.where(j == 0, bq, jnp.where(j == 2, bv, zero))
    linear(packed, n, w, 0, 3 * D, D, bias)
    seen = e.allowed[...] != 0
    seen = jnp.concatenate([seen, seen], axis=0)
    for p in range(D // 128):
        a = p * 128
        value, sums = attend(packed[:, a:a + 128], packed[:, D + a:D + a + 128], packed[:, 2 * D + a:2 * D + a + 128], seen)
        mixed[:, a:a + 128] = value.astype(BF16)
        logsum[:, p:p + 1] = sums
    h_out[...] = h_in[...].astype(F32) + dot(mixed[...], w[:, 3 * D:4 * D]) + bo


def cross_pairs(e):
    neighbours, keys = e.near.shape[0], e.near.shape[1]
    spans = e.spans
    return spans, neighbours // spans * keys, e.queries.shape[0] // spans


def cross_seen(e, span):
    near = e.near.shape[0] // e.spans
    return jnp.concatenate([e.near_tokens[pl.ds(span * near + j, 1), :] for j in range(near)], axis=1) != 0


def cross_keys(e, w, bv):
    D = e.near.shape[2]
    near = e.near

    def rows(i):
        for j in range(2):
            value = dot(near[2 * i:2 * i + 2].reshape(-1, D) if isinstance(i, int) else near[pl.ds(2 * i, 2)].reshape(-1, D),
                        w[:, D + j * D:2 * D + j * D])
            if j == 1:
                value = value + bv
            e.kv[span_of(i, 2 * near.shape[1]), j * D:(j + 1) * D] = value.astype(BF16)
    pl.loop(0, near.shape[0] // 2)(rows)


def cross_forward(e, h_in, h_out, w, gain, shift, bq, bo):
    D = h_in.shape[1]
    n, queries, kv, mixed, logsum = e.n.at[1], e.queries, e.kv, e.mixed.at[2], e.logsum.at[2]
    norm_forward(h_in, n, gain, shift)
    linear(queries, n, w, 0, D, D, lambda j: bq)
    spans, keys, size = cross_pairs(e)

    def span(c):
        rows, krows = span_of(c, size), span_of(c, keys)
        seen = cross_seen(e, c)
        for p in range(D // 128):
            a = p * 128
            value, sums = attend(queries[rows, a:a + 128], kv[krows, a:a + 128], kv[krows, D + a:D + a + 128], seen)
            mixed[rows, a:a + 128] = value.astype(BF16)
            logsum[span_of(c, 2 * size), p:p + 1] = sums
    pl.loop(0, spans)(span)
    h_out[...] = h_in[...] + dot(mixed[...], w[:, 3 * D:4 * D]) + bo


def ffn_forward(e, i, h_in, w_up, w_down, gain, shift, b_up, bd, norm, write):
    D, FF = h_in.shape[1], w_up.shape[1]
    n, slope, active, total = e.n.at[norm], e.slope.at[i], e.active.at[i], e.gn
    norm_forward(h_in, n, gain, shift)

    def up(j):
        cols = span_of(j, D)
        value = dot(n[...], w_up[:, cols]) + b_up[:, cols]
        raised, bent = gelu_both(value)
        active[:, cols] = raised.astype(BF16)
        slope[:, cols] = bent
    pl.loop(0, FF // D)(up)
    total[...] = h_in[...] + bd

    def down(j):
        rows = span_of(j, D)
        total[...] += dot(active[:, rows], w_down[rows, :])
    pl.loop(0, FF // D)(down)
    write(total)


def ffn_backward(e, i, h_in, w_up, w_down, gain, norm, rows, b_row):
    D, FF = h_in.shape[1], w_up.shape[1]
    n, slope, active = e.n.at[norm], e.slope.at[i], e.active.at[i]
    g, gb, gh, gn, vec = e.g, e.gb, e.gh, e.gn, e.vec
    gb[...] = g[...].astype(BF16)
    vec[rows[2]:rows[2] + 1, :] = column_sum(gb[...])

    def hidden(j):
        cols = span_of(j, D)
        value = (dot(gb[...], w_down[cols, :], NT) * slope[:, cols].astype(F32)).astype(BF16)
        gh[:, cols] = value
        e.vec_up[i:i + 1, cols] = column_sum(value)
    pl.loop(0, FF // D)(hidden)
    gn[...] = jnp.zeros_like(gn)

    def back(j):
        cols = span_of(j, D)
        gn[...] += dot(gh[:, cols], w_up[:, cols], NT)
    pl.loop(0, FF // D)(back)
    weight_gradient(w_down, active, gb, D)
    e.ship(b_row)
    weight_gradient(w_up, n, gh, D)
    e.ship(b_row + 1)
    norm_backward(h_in, gain, gn, g, vec, rows[0], rows[1])


def self_backward(e, i, h_in, w, gain, norm, rows, ship):
    D = h_in.shape[1]
    n, packed, mixed, logsum = e.n.at[norm], e.packed.at[i], e.mixed.at[i], e.logsum.at[i]
    g, gb, gmix, gpacked, gn, vec = e.g, e.gb, e.gmix, e.gpacked, e.gn, e.vec
    gb[...] = g[...].astype(BF16)
    vec[rows[4]:rows[4] + 1, :] = column_sum(gb[...])
    gmix[...] = dot(gb[...], w[:, 3 * D:4 * D], NT).astype(BF16)
    seen = e.allowed[...] != 0
    seen = jnp.concatenate([seen, seen], axis=0)
    for p in range(D // 128):
        a = p * 128
        q, k, v = (slice(t * D + a, t * D + a + 128) for t in range(3))
        of_q, of_k, of_v = attend_back(
            packed[:, q], packed[:, k], packed[:, v], seen, logsum[:, p:p + 1], gmix[:, a:a + 128])
        gpacked[:, q], gpacked[:, k], gpacked[:, v] = of_q.astype(BF16), of_k.astype(BF16), of_v.astype(BF16)
    vec[rows[2]:rows[2] + 1, :] = column_sum(gpacked[:, :D])
    vec[rows[3]:rows[3] + 1, :] = column_sum(gpacked[:, 2 * D:])
    gn[...] = jnp.zeros_like(gn)

    def back(j):
        cols = span_of(j, D)
        gn[...] += dot(gpacked[:, cols], w[:, cols], NT)
    pl.loop(0, 3)(back)
    weight_gradient(w.at[:, 0:3 * D], n, gpacked, D)
    weight_gradient(w.at[:, 3 * D:4 * D], mixed, gb, D)
    e.ship(ship)
    norm_backward(h_in, gain, gn, g, vec, rows[0], rows[1])


def cross_backward(e, h_in, w, gain, rows, ship):
    D = h_in.shape[1]
    n, queries, kv, mixed, logsum = e.n.at[1], e.queries, e.kv, e.mixed.at[2], e.logsum.at[2]
    g, gb, gmix, gq, gkv, gn, vec = e.g, e.gb, e.gmix, e.gpacked, e.gkv, e.gn, e.vec
    near = e.near
    gb[...] = g[...].astype(BF16)
    vec[rows[4]:rows[4] + 1, :] = column_sum(gb[...])
    gmix[...] = dot(gb[...], w[:, 3 * D:4 * D], NT).astype(BF16)
    spans, keys, size = cross_pairs(e)

    def span(c):
        srows, krows = span_of(c, size), span_of(c, keys)
        seen = cross_seen(e, c)
        for p in range(D // 128):
            a, b = p * 128, D + p * 128
            of_q, of_k, of_v = attend_back(
                queries[srows, a:a + 128], kv[krows, a:a + 128], kv[krows, b:b + 128], seen,
                logsum[span_of(c, 2 * size), p:p + 1], gmix[srows, a:a + 128])
            gq[srows, a:a + 128] = of_q.astype(BF16)
            gkv[krows, a:a + 128], gkv[krows, b:b + 128] = of_k.astype(BF16), of_v.astype(BF16)
    pl.loop(0, spans)(span)
    vec[rows[2]:rows[2] + 1, :] = column_sum(gq[:, :D])
    vec[rows[3]:rows[3] + 1, :] = column_sum(gkv[:, D:])
    gn[...] = dot(gq[:, :D], w[:, 0:D], NT)
    length = near.shape[1]

    def near_rows(i):
        krows = span_of(i, 2 * length)
        value = dot(gkv[krows, :D], w[:, D:2 * D], NT) + dot(gkv[krows, D:], w[:, 2 * D:3 * D], NT)
        e.near_out(i, value.reshape(2, length, D))
    pl.loop(0, near.shape[0] // 2)(near_rows)
    weight_gradient(w.at[:, 0:D], n, gq.at[:, 0:D], D)

    def pair(i):
        cols = span_of(i, 256)
        turned = near[:, :, cols].reshape(-1, 256).T
        for j in range(2):
            w[cols, D + j * D:2 * D + j * D] = dot(turned, gkv[:, j * D:(j + 1) * D]).astype(BF16)
    pl.loop(0, D // 256)(pair)
    weight_gradient(w.at[:, 3 * D:4 * D], mixed, gb, D)
    e.ship(ship)
    norm_backward(h_in, gain, gn, g, vec, rows[0], rows[1])


def block_kernel(spans, *refs):
    (ids, tokens, cotangent, segments, neighbours, stored_tokens, rows, bias_up,
     first, up_a, down_a, second, up_b, down_b,
     out, grad_tokens, grad_near, g_first, g_up_a, g_down_a, g_second, g_up_b, g_down_b, vec, vec_up,
     h, n, packed, mixed, logsum, queries, kv, near, near_tokens, slope, active, allowed,
     gb, gmix, gpacked, gkv, gh, gn, wide, tall, near_stage, loads, ships, nears, near_sems) = refs
    D = tokens.shape[1]
    FF = 4 * D

    def load(number):
        src, dst = (
            (first.at[:, 0:FF], wide.at[0]), (first.at[:, FF:2 * FF], wide.at[1]), (up_a, wide.at[2]), (down_a, tall.at[0]),
            (second, wide.at[0]), (up_b, wide.at[1]), (down_b, tall.at[1]),
            (first.at[:, FF:2 * FF], wide.at[1]), (first.at[:, 0:FF], wide.at[0]))[number]
        return pltpu.make_async_copy(src, dst, loads.at[number])

    def ship_copy(number):
        src, dst = (
            (tall.at[1], g_down_b), (wide.at[1], g_up_b), (wide.at[0], g_second), (tall.at[0], g_down_a),
            (wide.at[2], g_up_a), (wide.at[1], g_first.at[:, FF:2 * FF]), (wide.at[0], g_first.at[:, 0:FF]))[number]
        return pltpu.make_async_copy(src, dst, ships.at[number])

    def near_copy(j):
        return pltpu.make_async_copy(neighbours.at[ids[j]], near.at[j], nears.at[j])

    count = near.shape[0]
    for number in (0, 1, 2, 3, 6):
        load(number).start()
    for j in range(count):
        near_copy(j).start()
    for j in range(count):
        near_tokens[j:j + 1, :] = stored_tokens[pl.ds(ids[j], 1), :]
    grad_near_stage = near_stage

    def near_write(i, half):
        return pltpu.make_async_copy(grad_near_stage.at[i % 2, half], grad_near.at[ids[2 * i + half]], near_sems.at[i % 2, half])

    def near_out(i, value):
        @pl.when(i >= 2)
        def _():
            for half in range(2):
                near_write(i, half).wait()
        grad_near_stage[i % 2] = value
        for half in range(2):
            near_write(i, half).start()

    fill_allowed(allowed, segments)
    e = types.SimpleNamespace(n=n, packed=packed, mixed=mixed, logsum=logsum, queries=queries, kv=kv, near=near, near_tokens=near_tokens,
             slope=slope, active=active, allowed=allowed, g=grad_tokens, gb=gb, gmix=gmix, gpacked=gpacked, gkv=gkv, gh=gh,
             gn=gn, vec=vec, vec_up=vec_up, spans=spans, ship=lambda number: ship_copy(number).start(), near_out=near_out)

    def row(i):
        return rows[i:i + 1, :]
    load(0).wait()
    self_forward(e, 0, tokens, h.at[0], wide.at[0], row(0), row(3), row(6), row(7), row(8), 0)
    load(4).start()
    load(1).wait()
    for j in range(count):
        near_copy(j).wait()
    cross_keys(e, wide.at[1], row(10))
    cross_forward(e, h.at[0], h.at[1], wide.at[1], row(1), row(4), row(9), row(11))
    load(5).start()
    load(2).wait()
    load(3).wait()

    def keep(total):
        h[2] = total[...]
    ffn_forward(e, 0, h.at[1], wide.at[2], tall.at[0], row(2), row(5), bias_up.at[0:1], row(12), 2, keep)
    load(4).wait()
    self_forward(e, 1, h.at[2], h.at[3], wide.at[0], row(13), row(15), row(17), row(18), row(19), 3)
    load(5).wait()
    load(6).wait()

    def finish(total):
        out[...] = total[...].astype(BF16)
    ffn_forward(e, 1, h.at[3], wide.at[1], tall.at[1], row(14), row(16), bias_up.at[1:2], row(20), 4, finish)
    grad_tokens[...] = cotangent[...].astype(F32)
    ffn_backward(e, 1, h.at[3], wide.at[1], tall.at[1], row(14), 4, (14, 16, 20), 0)
    ship_copy(1).wait()
    load(7).start()
    self_backward(e, 1, h.at[2], wide.at[0], row(13), 3, (13, 15, 17, 18, 19), 2)
    ship_copy(2).wait()
    load(8).start()
    ffn_backward(e, 0, h.at[1], wide.at[2], tall.at[0], row(2), 2, (2, 5, 12), 3)
    load(7).wait()
    cross_backward(e, h.at[0], wide.at[1], row(1), (1, 4, 9, 10, 11), 5)
    load(8).wait()
    self_backward(e, 0, tokens, wide.at[0], row(0), 0, (0, 3, 6, 7, 8), 6)
    for number in (0, 3, 4, 5, 6):
        ship_copy(number).wait()
    for i in (count // 2 - 2, count // 2 - 1):
        for half in range(2):
            near_write(i, half).wait()


def run_blocks(tokens, cotangent, segment_ids, neighbours, near_index, neighbour_tokens, spans, rows, bias_up, weights):
    T, D = tokens.shape
    FF = 4 * D
    count, length, _ = neighbours.shape
    vmem, hbm = pl.BlockSpec(memory_space=pltpu.VMEM), pl.BlockSpec(memory_space=pl.ANY)
    shape = jax.ShapeDtypeStruct
    return pl.pallas_call(
        functools.partial(block_kernel, spans),
        out_shape=[shape((T, D), BF16), shape((T, D), F32), shape(neighbours.shape, F32)]
        + [shape(w.shape, BF16) for w in weights] + [shape((24, D), F32), shape((8, FF), F32)],
        in_specs=[pl.BlockSpec(memory_space=pltpu.SMEM), vmem, vmem, vmem, hbm, vmem, vmem, vmem] + [hbm] * 6,
        out_specs=[vmem, vmem, hbm] + [hbm] * 6 + [vmem, vmem],
        scratch_shapes=[
            pltpu.VMEM((4, T, D), F32), pltpu.VMEM((5, T, D), BF16), pltpu.VMEM((2, T, 3 * D), BF16),
            pltpu.VMEM((3, T, D), BF16), pltpu.VMEM((3, 2 * T, 128), F32), pltpu.VMEM((T, D), BF16),
            pltpu.VMEM((count * length, 2 * D), BF16), pltpu.VMEM(neighbours.shape, BF16),
            pltpu.VMEM((count, length), jnp.int32), pltpu.VMEM((2, T, FF), F32), pltpu.VMEM((2, T, FF), BF16),
            pltpu.VMEM((T, T), jnp.int32), pltpu.VMEM((T, D), BF16), pltpu.VMEM((T, D), BF16),
            pltpu.VMEM((T, 3 * D), BF16), pltpu.VMEM((count * length, 2 * D), BF16), pltpu.VMEM((T, FF), BF16),
            pltpu.VMEM((T, D), F32), pltpu.VMEM((3, D, FF), BF16), pltpu.VMEM((2, FF, D), BF16),
            pltpu.VMEM((2, 2, length, D), F32),
            pltpu.SemaphoreType.DMA((9,)), pltpu.SemaphoreType.DMA((7,)), pltpu.SemaphoreType.DMA((count,)),
            pltpu.SemaphoreType.DMA((2, 2)),
        ],
        compiler_params=pltpu.CompilerParams(vmem_limit_bytes=63 * 2 ** 20, has_side_effects=True),
        name="blocks",
    )(near_index, tokens, cotangent, segment_ids, neighbours, neighbour_tokens, rows, bias_up,
      *weights)


def parameter_tile(ref, start, width):
    tile = ref[(slice(None),) * 5 + (pl.ds(start, width),)]
    rows = math.prod(tile.shape[:5])
    if tile.shape[4] % 16:
        return tile.astype(F32).reshape(rows, width).astype(BF16)
    return tile.reshape(rows, width)


def project(out_ref, out_col, lefts, w_ref, w_col, count, bias=None, action=None):
    tile = 256

    def block(j):
        for start in range(0, group, tile):
            here = j * group + start
            weights = parameter_tile(w_ref, pl.multiple_of(w_col + here, tile), tile)
            cols = pl.ds(pl.multiple_of(out_col + here, tile), tile)
            row = 0
            for left in lefts():
                value = dot(left, weights)
                if bias is not None:
                    value = value + bias[:, pl.ds(pl.multiple_of(here, tile), tile)]
                if action is not None:
                    action(cols, value)
                else:
                    out_ref[row:row + left.shape[0], cols] = value.astype(out_ref.dtype)
                row += left.shape[0]
    group = 3 * tile if count % (3 * tile) == 0 else tile
    pl.loop(0, count // group)(block)


def self_pieces(e, i, norm, h_in, h_out, w, chunk, gain, bias_rows):
    D = h_in.shape[1]
    n, packed, mixed, logsum, rows = e.n, e.packed, e.mixed, e.logsum, e.rows
    shift, bq, bv, bo = bias_rows

    def bias(row):
        return rows.at[row:row + 1, :]
    yield chunk, 3.0
    e.free("n")
    norm_forward(h_in, n, rows[gain:gain + 1, :], rows[shift:shift + 1, :])
    e.save("n", norm)
    e.free("packed")
    project(packed, 0, lambda: [n[...]], w, 0, D, bias(bq))
    project(packed, D, lambda: [n[...]], w, D, D)
    yield chunk + 1, 1.0
    project(packed, 2 * D, lambda: [n[...]], w, 2 * D, D, bias(bv))
    e.save("packed", i)
    e.free("mixed")
    e.free("logsum")
    for p in range(D // 128):
        if p % 3 == 0:
            yield chunk + 1, 2.0
        seen = e.allowed[...] != 0
        seen = jnp.concatenate([seen, seen], axis=0)
        a = p * 128
        value, sums = attend(packed[:, a:a + 128], packed[:, D + a:D + a + 128], packed[:, 2 * D + a:2 * D + a + 128], seen)
        mixed[:, a:a + 128] = value.astype(BF16)
        logsum[:, p:p + 1] = sums
    e.save("mixed", i)
    e.save("logsum", i)
    yield chunk + 1, 1.0

    def add(cols, value):
        h_out[:, cols] = h_in[:, cols].astype(F32) + value
    project(None, 0, lambda: [mixed[...]], w, 3 * D, D, bias(bo), add)
    e.save("h", 3 * i)


def cross_pieces(e, norm, h_in, h_out, w, chunk, gain, bias_rows):
    D = h_in.shape[1]
    n, queries, kv, mixed, logsum, rows = e.n, e.queries, e.kv, e.mixed, e.logsum, e.rows
    near, near_tokens, spans = e.near, e.near_tokens, e.spans
    count, length = near.shape[0], near.shape[1]
    shift, bq, bv, bo = bias_rows
    yield chunk, 2.0
    e.free("n")
    norm_forward(h_in, n, rows[gain:gain + 1, :], rows[shift:shift + 1, :])
    e.save("n", norm)
    project(queries, 0, lambda: [n[...]], w, 4 * D, D, rows.at[bq:bq + 1, :])
    e.save("queries", 0)
    flat = lambda: [near[j:j + 2].reshape(2 * length, D) for j in range(0, count, 2)]
    yield chunk, 3.0
    project(kv, 0, flat, w, 5 * D, D)
    yield chunk + 1, 3.0
    project(kv, D, flat, w, 6 * D, D, rows.at[bv:bv + 1, :])
    e.save("kv", 0)
    e.free("mixed")
    e.free("logsum")
    size, each = n.shape[0] // spans, count // spans
    for c in range(spans):
        yield chunk + 1, 1.3
        seen = jnp.concatenate([near_tokens[c * each + j:c * each + j + 1, :] for j in range(each)], axis=1) != 0

        def read(col):
            return kv[c * each * length:(c + 1) * each * length, col:col + 128]
        for p in range(D // 128):
            a = p * 128
            value, sums = attend(queries[c * size:(c + 1) * size, a:a + 128], read(a), read(D + a), seen)
            mixed[c * size:(c + 1) * size, a:a + 128] = value.astype(BF16)
            logsum[2 * c * size:2 * (c + 1) * size, p:p + 1] = sums
    e.save("mixed", 2)
    e.save("logsum", 2)
    yield chunk + 1, 1.0

    def add(cols, value):
        h_out[:, cols] = h_in[:, cols] + value
    project(None, 0, lambda: [mixed[...]], w, 7 * D, D, rows.at[bo:bo + 1, :], add)
    e.save("h", 1)


def ffn_pieces(e, i, norm, h_in, w_up, w_down, chunk, gain, bias_rows, finish):
    D = h_in.shape[1]
    n, slope, active, rows, total = e.n, e.slope, e.active, e.rows, e.total
    shift, bd = bias_rows
    FF = active.shape[1]
    yield chunk, 1.0
    e.free("n")
    norm_forward(h_in, n, rows[gain:gain + 1, :], rows[shift:shift + 1, :])
    e.save("n", norm)
    e.free("slope")
    e.free("active")

    def action(cols, value):
        raised, bent = gelu_both(value)
        active[:, cols] = raised.astype(BF16)
        slope[:, cols] = bent.astype(BF16)
    for j in range(FF // D):
        yield chunk + (2 * j * D) // FF, 1.3
        project(None, j * D, lambda: [n[...]], w_up, j * D, D, e.bias_up.at[i:i + 1, j * D:(j + 1) * D], action)
    e.save("slope", i)
    e.save("active", i)

    def add(cols, value):
        total[:, cols] = h_in[:, cols] + value
    yield chunk + 3, 3.0
    project(None, 0, lambda: [active[...]], w_down, 0, D, rows.at[bd:bd + 1, :], add)
    finish()


def forward_pieces(e, h, tokens, first, up_a, down_a, second, up_b, down_b, small):
    yield -len(SAVED) ** 2, 2.0
    count = e.near.shape[0]
    for j in range(count):
        block, line = e.stored[0], e.stored_tokens[0:1, :]
        for i in range(1, count):
            chosen = e.chosen[j:j + 1, i:i + 1] != 0
            block = jnp.where(jnp.broadcast_to(chosen, block.shape), e.stored[i], block)
            line = jnp.where(chosen, e.stored_tokens[i:i + 1, :], line)
        e.near[j], e.near_tokens[j:j + 1, :] = block, line
    e.save("near", 0)
    yield 0, 1.5
    lines = [small[index] for index in itertools.product(*map(range, small.shape[:4]))]
    part = e.rows.shape[1] // len(lines)
    wide = e.bias_up.shape[1] // len(lines)
    e.rows[...] = jnp.concatenate([line[:24, :part].astype(F32) for line in lines], axis=1)
    both = jnp.concatenate([line[16:24, :wide].astype(F32) for line in lines], axis=1)
    e.bias_up[...] = both[5:7]
    yield from self_pieces(e, 0, 0, tokens, h.at[0], first, 0, 0, (3, 6, 7, 8))
    yield from cross_pieces(e, 1, h.at[0], h.at[1], first, 2, 1, (4, 9, 10, 11))

    def keep():
        h[2] = e.total[...]
        e.save("h", 2)
    yield from ffn_pieces(e, 0, 2, h.at[1], up_a, down_a, 4, 2, (5, 12), keep)
    yield from self_pieces(e, 1, 3, h.at[2], h.at[3], second, 8, 13, (15, 17, 18, 19))

    def finish():
        e.out[...] = e.total[...].astype(BF16)
    yield from ffn_pieces(e, 1, 4, h.at[3], up_b, down_b, 10, 14, (16, 20), finish)


SAVED = ("n", "packed", "queries", "kv", "mixed", "logsum", "slope", "active", "near")


def forward_kernel(dp_size, fsdp_size, chunks, places, count, spans, *refs):
    n = len(places)
    shards, vectors, (tokens, segments, chosen, stored, stored_tokens) = refs[:n], refs[n:n + 6], refs[n + 6:n + 11]
    refs = refs[n + 11:]
    wholes, (out, h_out, rows, near_tokens), saved = refs[:count - 1], refs[count - 1:count + 3], dict(zip(SAVED, refs[count + 3:count + 12]))
    refs = refs[count + 12:]
    landing, held, (h, allowed, total, bias_up) = refs[:count], dict(zip(SAVED, refs[count:count + 9])), refs[count + 9:count + 13]
    kept, saves, send, recv = refs[count + 13:]
    place = Place(dp_size, fsdp_size)
    here = tuple(place.at[name] for name in NAMES)
    for shard, (which, col) in zip(shards, places):
        landing[which][(*here, slice(None), slice(col, col + shard.shape[1]))] = shard[...]
    landing[count - 1][here] = pack_small(vectors[:4], vectors[4:])
    greet(place)
    sems = Sems(send, recv)
    copies, pending, used = [], {}, [0]

    def keep(slot, which, row, height, col, width):
        where = (slice(None),) * 4 + (pl.ds(row, height), pl.ds(col, width))
        copy = pltpu.make_async_copy(landing[which].at[where], wholes[which].at[where], kept.at[slot])
        copy.start()
        copies.append(copy)

    def chunk_flow(slots, group):
        flows = [
            gather_flow(place, sems, landing[which], order, row, height, start + col, width)
            for which, row, height, start, total in group
            for order, col, width in routes(total)
        ]
        while flows:
            flows = [flow for flow in flows if next(flow, 0) is None]
            if flows:
                yield
        for slot, member in zip(slots, group):
            if member[0] < count - 1:
                keep(slot, *member)

    def save(name, index):
        src, dst = (h.at[index], h_out.at[index]) if name == "h" else (held[name], saved[name].at[index])
        copy = pltpu.make_async_copy(src, dst, saves.at[used[0]])
        copy.start()
        used[0] += 1
        pending[(name, index) if name == "h" else name] = copy

    def free(name):
        if name in pending:
            pending.pop(name).wait()

    fill_allowed(allowed, segments)
    e = types.SimpleNamespace(**held, rows=rows, bias_up=bias_up, allowed=allowed, near_tokens=near_tokens, spans=spans,
             chosen=chosen, stored=stored, stored_tokens=stored_tokens, total=total, out=out, save=save, free=free)
    work = forward_pieces(e, h, tokens, *landing)
    ahead = next(work, None)
    groups, slot = [], 0
    for group in chunks:
        groups.append([chunk_flow(range(slot, slot + len(group)), group)])
        slot += len(group)

    def compute(tick, ahead=[ahead]):
        left = COMPUTE_SHARE
        last = tick == len(groups) + GATHER_STEPS[-1] - 1
        while ahead[0] is not None and ahead[0][0] + GATHER_STEPS[-1] <= tick and (left > 0 or last):
            left -= ahead[0][1]
            ahead[0] = next(work, None)
    run_schedule(groups, GATHER_STEPS, compute)
    sems.drain()
    for copy in copies + list(pending.values()):
        copy.wait()


def gather_and_run(mesh_shape, shards, places, vectors, chunks, tokens, segment_ids, near_index, neighbours, neighbour_tokens,
                   spans, collective_id):
    dp_size, fsdp_size = mesh_shape
    size = {"y": dp_size // 2, "c": 2, "z": fsdp_size // 2, "x": 2}
    count = sum(copies_of(order, size) for group in chunks for *_, total in group for order, _, _ in routes(total))
    count += sum(1 for group in chunks for *_, total in group for _ in routes(total))
    lead = tuple(size[name] for name in NAMES)
    shapes = {}
    for shard, (which, col) in zip(shards, places):
        rows, width = shapes.get(which, (shard.shape[0], 0))
        shapes[which] = (rows, max(width, col + shard.shape[1]))
    shapes = [shapes[which] for which in sorted(shapes)] + [(32, 128)]
    T, D = tokens.shape
    FF = 4 * D
    near, length, _ = neighbours.shape
    shape = jax.ShapeDtypeStruct
    held = {"n": ((T, D), BF16, 5), "packed": ((T, 3 * D), BF16, 2), "queries": ((T, D), BF16, 1),
            "kv": ((near * length, 2 * D), BF16, 1), "mixed": ((T, D), BF16, 3), "logsum": ((2 * T, 128), F32, 3),
            "slope": ((T, FF), BF16, 2), "active": ((T, FF), BF16, 2), "near": (neighbours.shape, BF16, 1)}
    chosen = (near_index[:, None] == jnp.arange(near)[None, :]).astype(jnp.int32)
    n, vmem, hbm = len(shards), pl.BlockSpec(memory_space=pltpu.VMEM), pl.BlockSpec(memory_space=pl.ANY)
    results = pl.pallas_call(
        functools.partial(forward_kernel, dp_size, fsdp_size, chunks, places, len(shapes), spans),
        out_shape=[shape(lead + s, BF16) for s in shapes[:-1]]
        + [shape((T, D), BF16), shape((4, T, D), F32), shape((24, D), F32), shape((near, length), jnp.int32)]
        + [shape((times,) + s, kind) for s, kind, times in held.values()],
        in_specs=[vmem] * (n + 11),
        out_specs=[hbm] * (len(shapes) - 1) + [vmem, hbm, vmem, vmem] + [hbm] * 9,
        scratch_shapes=[pltpu.VMEM(lead + s, BF16) for s in shapes]
        + [pltpu.VMEM(s, kind) for s, kind, _ in held.values()]
        + [pltpu.VMEM((4, T, D), F32), pltpu.VMEM((T, T), jnp.int32), pltpu.VMEM((T, D), F32), pltpu.VMEM((2, FF), F32)]
        + [
            pltpu.SemaphoreType.DMA((sum(map(len, chunks)),)),
            pltpu.SemaphoreType.DMA((24,)),
            pltpu.SemaphoreType.DMA((count,)),
            pltpu.SemaphoreType.DMA((count,)),
        ],
        compiler_params=pltpu.CompilerParams(
            collective_id=collective_id, has_side_effects=True, vmem_limit_bytes=63 * 2 ** 20),
        name="gather_and_forward",
    )(*shards, *vectors, tokens, segment_ids, chosen, neighbours, neighbour_tokens)
    return results[:len(shapes) - 1], results[len(shapes) - 1:len(shapes) + 3], dict(zip(SAVED, results[len(shapes) + 3:]))


def ffn_chain(e, i, h_in, w_up, w_down, gain, norm, rows):
    D, FF = h_in.shape[1], w_up.shape[1]
    slope, gb, gh, g, gn, vec = e.slope.at[i], e.gb.at[norm], e.gh.at[i], e.g, e.gn, e.vec
    gb[...] = g[...].astype(BF16)
    vec[rows[2]:rows[2] + 1, :] = column_sum(gb[...])
    gn[...] = jnp.zeros_like(gn)

    def hidden(j):
        cols = span_of(j, D)
        value = (dot(gb[...], w_down[cols, :], NT) * slope[:, cols].astype(F32)).astype(BF16)
        gh[:, cols] = value
        e.vec_up[i:i + 1, cols] = column_sum(value)
        gn[...] += dot(value, w_up[:, cols], NT)
    pl.loop(0, FF // D)(hidden)
    e.save("gb", norm)
    e.save("gh", i)
    norm_backward(h_in, gain, gn, g, vec, rows[0], rows[1])


def backward_kernel(*refs):
    cotangent, rows, h_in, slope_in, up, down, g, vec, vec_up, gb_out, gh_out, slope, gb, gh, h, gn, wide, tall, brought, saves = refs
    copies = [
        pltpu.make_async_copy(src, dst, brought.at[i])
        for i, (src, dst) in enumerate(((down, tall), (slope_in.at[1], slope.at[0]), (up, wide), (h_in.at[3], h)))]
    for copy in copies:
        copy.start()
    saved = []

    def save(name, index):
        src, dst = (gb.at[4], gb_out.at[4]) if name == "gb" else (gh.at[0], gh_out.at[1])
        copy = pltpu.make_async_copy(src, dst, saves.at[len(saved)])
        copy.start()
        saved.append(copy)
    e = types.SimpleNamespace(slope=slope, gb=gb, gh=gh, g=g, gn=gn, vec=vec, vec_up=vec_up.at[1:2], save=save)
    g[...] = cotangent[...].astype(F32)
    for copy in copies:
        copy.wait()
    ffn_chain(e, 0, h, wide, tall, rows[14:15, :], 4, (14, 16, 20))
    for copy in saved:
        copy.wait()


def run_backward(cotangent, rows, h, slope, w_up, w_down):
    T, D = cotangent.shape
    FF = 4 * D
    vmem, hbm = pl.BlockSpec(memory_space=pltpu.VMEM), pl.BlockSpec(memory_space=pl.ANY)
    shape = jax.ShapeDtypeStruct
    results = pl.pallas_call(
        backward_kernel,
        out_shape=[shape((T, D), F32), shape((24, D), F32), shape((8, FF), F32), shape((5, T, D), BF16), shape((2, T, FF), BF16)],
        in_specs=[vmem] * 2 + [hbm] * 4,
        out_specs=[vmem] * 3 + [hbm] * 2,
        scratch_shapes=[
            pltpu.VMEM((1, T, FF), BF16), pltpu.VMEM((5, T, D), BF16), pltpu.VMEM((1, T, FF), BF16), pltpu.VMEM((T, D), F32),
            pltpu.VMEM((T, D), F32), pltpu.VMEM((D, FF), BF16), pltpu.VMEM((FF, D), BF16),
            pltpu.SemaphoreType.DMA((4,)), pltpu.SemaphoreType.DMA((2,)),
        ],
        compiler_params=pltpu.CompilerParams(vmem_limit_bytes=VMEM_MOST, has_side_effects=True),
        name="backward",
    )(cotangent, rows, h, slope, w_up, w_down)
    return results[:3], {"gb": results[3], "gh": results[4]}


def gradient_columns(dst, j, left, right, right_col):
    size = dst.shape
    rows = math.prod(size[1:4]) * size[5]

    def block(y):
        turned = left(pl.ds(pl.multiple_of(y * rows, 128), rows)).T
        for start in range(0, size[6], 256):
            value = dot(turned, right[:, right_col + start:right_col + start + 256])
            dst[y, :, :, :, j, :, start:start + 256] = value.reshape(size[1:4] + (size[5], 256)).astype(BF16)
    pl.loop(0, size[0])(block)


def gradient_rows(dsts, left, right):
    Y, C, Z, X, parts, rows, width = dsts[0].shape
    each = 2 * X * rows * parts * len(dsts)

    def block(i):
        y, c, z = i // (C * Z // 2), (i // (Z // 2)) % C, i % (Z // 2)
        turned = left[:, pl.ds(pl.multiple_of(i * each, 128), each)].T
        for start in range(0, width, 256):
            value = dot(turned, right[:, start:start + 256]).reshape(2, X, len(dsts), parts, rows, 256).astype(BF16)
            for half, dst in enumerate(dsts):
                dst[y, c, pl.ds(2 * z, 2), :, :, :, start:start + 256] = value[:, :, half]
    pl.loop(0, left.shape[1] // each)(block)


FACTORS = ("n", "active", "mixed", "gb", "gh", "packed", "logsum", "kv", "queries", "h", "slope")
ORDER = (("active", 1, 0), ("gb", 4, 4), ("packed", 1, 0), ("logsum", 1, 0), ("h", 2, 0), ("n", 4, 0), ("gh", 1, 0), ("n", 3, 1),
         ("mixed", 1, 0), ("slope", 0, 0), ("n", 2, 2), ("kv", 0, 0), ("queries", 0, 0), ("mixed", 2, 1))
LATER = (("active", 0, 0), ("n", 1, 0), ("packed", 0, 0), ("logsum", 2, 0), ("h", 1, 0), ("h", 0, 0), ("logsum", 0, 0), ("n", 0, 1),
         ("mixed", 0, 0))
SLOTS = {("n", 4): 0, ("n", 3): 1, ("n", 2): 2, ("n", 1): 0, ("n", 0): 1, ("mixed", 1): 0, ("mixed", 2): 1, ("mixed", 0): 0}


def chunk_makers(f, need, later, require):
    near = f.near
    D = near.shape[2]

    def rows_of(i, norm):
        def make(dsts):
            require(2 - 2 * i)
            need(("active", i), ("gb", norm))
            gradient_rows(dsts, f.active.at[0], f.gb.at[norm])
            if i:
                later(0)
        return make

    def columns(dst, j, name, index, right, right_col):
        left = getattr(f, name)
        gradient_columns(dst, j, lambda rows: left[SLOTS[name, index], :, rows], right, right_col)

    def up(i, norm, half):
        def make(dsts):
            require(2 - 2 * i)
            need(("n", norm), ("gh", i))
            for j in range(2):
                columns(dsts[0], j, "n", norm, f.gh.at[0], (2 * half + j) * D)
            if i and not half:
                later(1)
        return make

    def query_key(i, norm):
        def make(dsts):
            require(4 - 3 * i)
            need(("n", norm),)
            for j in range(2):
                columns(dsts[0], j, "n", norm, f.gpacked, j * D)
            if i:
                later(7)
        return make

    def value_out(i, norm):
        def make(dsts):
            require(4 - 3 * i)
            need(("n", norm), ("mixed", i))
            columns(dsts[0], 0, "n", norm, f.gpacked, 2 * D)
            columns(dsts[0], 1, "mixed", i, f.gb.at[norm], 0)
            if i:
                later(8)
        return make

    def near_rows(rows):
        return near[:, :, rows].reshape(-1, rows.size)

    def cross_one(dsts):
        require(3)
        need(("n", 1),)
        columns(dsts[0], 0, "n", 1, f.gq, 0)
        gradient_columns(dsts[0], 1, near_rows, f.gkv, 0)

    def cross_two(dsts):
        require(3)
        need(("mixed", 2),)
        gradient_columns(dsts[0], 0, near_rows, f.gkv, D)
        columns(dsts[0], 1, "mixed", 2, f.gb.at[1], 0)
    return (rows_of(1, 4), None, up(1, 4, 1), up(1, 4, 0), value_out(1, 3), query_key(1, 3), rows_of(0, 2), None,
            up(0, 2, 1), up(0, 2, 0), cross_two, cross_one, value_out(0, 0), query_key(0, 0))


def self_back_pieces(f, need, norm, gain, h, lines):
    g, gn, gmix, vec, gpacked, tiles = f.g, f.gn, f.gmix, f.vec, f.gpacked, f.tiles
    D = g.shape[1]
    of_gain, of_shift, of_q, of_v, of_out = (slice(line, line + 1) for line in lines)
    gb = f.gb.at[norm]
    gb[...] = g[...].astype(BF16)
    vec[of_out, :] = column_sum(gb[...])
    gmix[...] = dot(gb[...], tiles[3], NT).astype(BF16)
    packed, logsum = f.packed.at[0], f.logsum.at[0]
    for p in range(D // 128):
        if p % 3 == 0:
            yield 3.0
        seen = f.allowed[...] != 0
        seen = jnp.concatenate([seen, seen], axis=0)
        a = p * 128
        q, k, v = (slice(t * D + a, t * D + a + 128) for t in range(3))
        grad_q, grad_k, grad_v = attend_back(
            packed[:, q], packed[:, k], packed[:, v], seen, logsum[:, p:p + 1], gmix[:, a:a + 128])
        gpacked[:, q], gpacked[:, k], gpacked[:, v] = grad_q.astype(BF16), grad_k.astype(BF16), grad_v.astype(BF16)
    yield 2.0
    vec[of_q, :] = column_sum(gpacked[:, :D])
    vec[of_v, :] = column_sum(gpacked[:, 2 * D:])
    gn[...] = dot(gpacked[:, :D], tiles[0], NT) + dot(gpacked[:, D:2 * D], tiles[1], NT) + dot(gpacked[:, 2 * D:], tiles[2], NT)
    yield 1.5
    norm_backward(h, f.rows[gain:gain + 1, :], gn, g, vec, lines[0], lines[1])


def chain_pieces(f, need, later, load, near_out, spans):
    g, gn, gmix, vec, rows, gq, gkv, tiles = f.g, f.gn, f.gmix, f.vec, f.rows, f.gq, f.gkv, f.tiles
    D = g.shape[1]
    h = f.h.at[0]
    yield 1.0
    need(("g", 0), ("tiles", 0), ("packed", 1), ("logsum", 1), ("h", 2))
    yield from self_back_pieces(f, need, 3, 13, h, (13, 15, 17, 18, 19))
    for number in (2, 3, 4):
        later(number)
    load(2)
    f.stage = 1
    yield 2.0
    need(("tiles", 1), ("slope", 0))
    gb, gh, slope = f.gb.at[2], f.gh.at[0], f.slope.at[0]
    gb[...] = g[...].astype(BF16)
    vec[12:13, :] = column_sum(gb[...])
    for j in range(4):
        if j:
            yield 2.0
        if j == 2:
            load(3)
            need(("tiles", 2),)
        cols, base = slice(j * D, (j + 1) * D), (4, 5, 0, 1)[j]
        value = (dot(gb[...], tiles[base], NT) * slope[:, cols].astype(F32)).astype(BF16)
        gh[:, cols] = value
        f.vec_up[0:1, cols] = column_sum(value)
        back = dot(value, tiles[base + 2], NT)
        gn[...] = gn[...] + back if j else back
    yield 1.5
    load(4)
    need(("h", 1),)
    norm_backward(h, rows[2:3, :], gn, g, vec, 2, 5)
    later(5)
    f.stage = 2
    yield 1.5
    need(("tiles", 3), ("kv", 0), ("queries", 0), ("logsum", 2))
    gb = f.gb.at[1]
    gb[...] = g[...].astype(BF16)
    vec[11:12, :] = column_sum(gb[...])
    gmix[...] = dot(gb[...], tiles[7], NT).astype(BF16)
    near, length = f.near_tokens.shape
    each = near // spans
    keys, size = each * length, g.shape[0] // spans
    queries, kv, logsum = f.queries.at[0], f.kv.at[0], f.logsum.at[0]
    for c in range(spans):
        yield 2.5
        srows, krows = slice(c * size, (c + 1) * size), slice(c * keys, (c + 1) * keys)
        seen = jnp.concatenate([f.near_tokens[c * each + j:c * each + j + 1, :] for j in range(each)], axis=1) != 0
        for p in range(D // 128):
            a, b = p * 128, D + p * 128
            of_q, of_k, of_v = attend_back(
                queries[srows, a:a + 128], kv[krows, a:a + 128], kv[krows, b:b + 128], seen,
                logsum[2 * c * size:2 * (c + 1) * size, p:p + 1], gmix[srows, a:a + 128])
            gq[srows, a:a + 128] = of_q.astype(BF16)
            gkv[krows, a:a + 128], gkv[krows, b:b + 128] = of_k.astype(BF16), of_v.astype(BF16)
    yield 1.0
    later(6)
    vec[9:10, :] = column_sum(gq[...])
    vec[10:11, :] = column_sum(gkv[:, D:])
    gn[...] = dot(gq[...], tiles[4], NT)
    yield 1.5
    need(("h", 0),)
    norm_backward(h, rows[1:2, :], gn, g, vec, 1, 4)
    f.stage = 3
    yield 1.0
    need(("tiles", 4), ("packed", 0), ("logsum", 0))
    yield from self_back_pieces(f, need, 0, 0, f.tokens, (0, 3, 6, 7, 8))
    f.stage = 4
    for i in range(near // 2):
        yield 1.5
        krows = slice(2 * i * length, 2 * (i + 1) * length)
        value = dot(gkv[krows, :D], tiles[5], NT) + dot(gkv[krows, D:], tiles[6], NT)
        near_out(i, value.reshape(2, length, D))
    f.stage = 5


def scatter_routes(parts, width):
    if parts == 1:
        return [(ROUTES[0][0][::-1], 0, 1, 0, width)]
    third = width // 3
    cut = ((0, 1, 0), (1, 1, 0), (0, 2, third), (0, 2, 2 * third))
    return [(order[::-1], *where, third) for (order, _), where in zip(ROUTES, cut)]


def scatter_kernel(dp_size, fsdp_size, chunks, count, plan, spans, *refs):
    factors = dict(zip(FACTORS, refs[:11]))
    (first, second, up, down, g_in, near, near_tokens, rows, tokens, segments, vec_in, vec_up_in) = refs[11:23]
    outs, grad_tokens, grad_near = refs[23:23 + count], refs[23 + count], refs[24 + count]
    refs = refs[25 + count:]
    f = types.SimpleNamespace(**dict(zip(FACTORS, refs[:11])))
    (f.gq, f.gkv, f.tiles, f.gmix, f.gn, f.vec, f.vec_up, f.gpacked, f.allowed, small, near_stage), scratch = refs[11:22], refs[22:-5]
    brought, loads, near_sem, send, recv = refs[-5:]
    f.near, f.near_tokens, f.rows, f.tokens, f.g, f.stage = near, near_tokens, rows, tokens, grad_tokens, 0
    D = tokens.shape[1]
    place = Place(dp_size, fsdp_size)
    sems = Sems(send, recv)
    c = place.at["c"]
    sibling = place.device("c", 1 - c)
    arriving = {}

    def bring(number):
        name, index, slot = (ORDER + LATER)[number]
        copy = pltpu.make_async_copy(factors[name].at[index], getattr(f, name).at[slot], brought.at[number])
        copy.start()
        arriving[name, index] = [copy]

    def load(number):
        def across(array, col, slot):
            return array.at[:, col * D:(col + 1) * D], f.tiles.at[slot]

        def along(j, slot):
            return down.at[j * D:(j + 1) * D, :], f.tiles.at[slot]
        moves = (
            [across(second, j, j) for j in range(4)], [along(0, 4), along(1, 5), across(up, 0, 6), across(up, 1, 7)],
            [along(2, 0), along(3, 1), across(up, 2, 2), across(up, 3, 3)], [across(first, 4 + j, 4 + j) for j in range(4)],
            [across(first, j, j) for j in range(4)])[number]
        arriving["tiles", number] = [
            pltpu.make_async_copy(src, dst, loads.at[4 * number + i]) for i, (src, dst) in enumerate(moves)]
        for copy in arriving["tiles", number]:
            copy.start()
    for number in range(2):
        bring(number)
    arriving["g", 0] = [pltpu.make_async_copy(g_in, grad_tokens, loads.at[20])]
    arriving["g", 0][0].start()
    load(0)
    for number in range(2, len(ORDER)):
        bring(number)
    load(1)

    def need(*wanted):
        for key in wanted:
            for copy in arriving.pop(key, ()):
                copy.wait()
    near_copies = []

    def near_out(i, value):
        if near_copies:
            near_copies.pop().wait()
        near_stage[...] = value
        near_copies.append(pltpu.make_async_copy(near_stage, grad_near.at[2 * i:2 * i + 2], near_sem))
        near_copies[-1].start()

    def later(number):
        bring(len(ORDER) + number)
    chain = chain_pieces(f, need, later, load, near_out, spans)

    def require(stage):
        while f.stage < stage:
            next(chain)
    makers = chunk_makers(f, need, later, require)
    everything = pl.ds(0, place.size["y"])
    lead = tuple(place.size[name] for name in NAMES if name != "c")

    def pack():
        require(4)
        part, wide = outs[-1].shape[0], f.vec_up.shape[1]
        for index in itertools.product(*(range(place.size[name]) for name in NAMES)):
            i = ((index[0] * 2 + index[1]) * place.size["z"] + index[2]) * 2 + index[3]
            devices = dp_size * fsdp_size
            one, many = D // devices, wide // devices
            values = jnp.pad(f.vec[0:21, i * one:(i + 1) * one], ((0, 0), (0, 128 - one)))
            ups = jnp.pad(f.vec_up[0:2, i * many:(i + 1) * many], ((0, 0), (0, 128 - many)))
            blank = jnp.zeros((part - 23, 128), F32)
            small[(*index, 0)] = jnp.concatenate([values, ups, blank], axis=0).astype(BF16)

    def chunk_flow(make, grad, landing, buffers, routed, targets):
        if make is not None:
            make()
        crossing = []
        for _, j, nj, col, width in routed:
            slot, part = sems.take(), (pl.ds(j, nj), slice(None), pl.ds(col, width))
            copy = sems.copy(slot, grad.at[(everything, 1 - c, slice(None), slice(None), *part)],
                             landing.at[(slice(None), slice(None), slice(None), *part)], sibling)
            copy.start()
            crossing.append(copy)
        yield
        for copy in crossing:
            copy.wait()
        add_blocks(lead + landing.shape[3:4], landing, landing, grad.at[:, c])
        flows = []
        for (order, j, nj, col, width), own in zip(routed, buffers):
            part = (pl.ds(j, nj), slice(None), pl.ds(col, width))
            flows.append(scatter_flow(
                place, sems, landing.at[(slice(None), slice(None), slice(None), *part)], own, order,
                [target.at[:, pl.ds(col, width)] for target in targets[j:j + nj]], (nj,)))
        while flows:
            flows = [flow for flow in flows if next(flow, 0) is None]
            if flows:
                yield

    groups = []
    for number, (group, places) in enumerate(zip(chunks, plan)):
        members = []
        for (which, row, height, col, width), (grad, landing, buffers) in zip(group, places):
            if grad is None:
                make, array, targets = pack, small, [outs[which]]
            else:
                make, array = makers[number], scratch[grad]
                fill = [array]
                if makers[(number + 1) % len(makers)] is None:
                    fill = [scratch[plan[number + 1][0][0]], array]
                make = make and functools.partial(make, fill)
                rows_, cols_ = array.shape[5:]
                if width == cols_:
                    targets = [outs[which].at[row + j * rows_:row + (j + 1) * rows_, :] for j in range(2)]
                else:
                    targets = [outs[which].at[:, col + j * cols_:col + (j + 1) * cols_] for j in range(2)]
            members.append(chunk_flow(
                make, array, scratch[landing], [[scratch[b] for b in own] for own in buffers],
                scatter_routes(array.shape[4], array.shape[6]), targets))
        groups.append(members)

    fill_allowed(f.allowed, segments)
    f.vec[...] = vec_in[...]
    f.vec_up[...] = vec_up_in[...]
    greet(place)

    def chain_some(tick):
        left = CHAIN_SHARE
        while f.stage < 5 and left > 0 and tick >= {1: 3, 3: 5}.get(f.stage, 0):
            left -= next(chain, 9.0)
    run_schedule(groups, SCATTER_STEPS, chain_some)
    require(5)
    sems.drain()
    near_copies.pop().wait()


def scatter_all(mesh_shape, factors, weights, g, near, near_tokens, rows, tokens, segment_ids, vec, vec_up, spans, owned, chunks,
                collective_id):
    dp_size, fsdp_size = mesh_shape
    size = {"y": dp_size // 2, "c": 2, "z": fsdp_size // 2, "x": 2}
    lead = tuple(size[name] for name in NAMES if name != "c")
    whole = tuple(size[name] for name in NAMES)
    T, D = tokens.shape
    count_near, length, _ = near.shape
    part = D // (dp_size * fsdp_size)
    shapes, plan, pools, count = [], [], {}, 0

    def new(shape, role, most):
        pool = pools.setdefault((shape, role), [])
        if len(pool) < most:
            shapes.append(pltpu.VMEM(shape, BF16))
            pool.append(len(shapes) - 1)
        else:
            pool.append(pool.pop(0))
        return pool[-1]

    for group in chunks:
        places = []
        for which, *_ in group:
            small = which == len(owned) - 1
            block = (1, 32, 128) if small else (2, part, D)
            grad = None if small else new(whole + block, 0, 3)
            landing = new(lead + block, 1, LANDINGS)
            buffers = []
            for number, (order, _, nj, _, width) in enumerate(scatter_routes(block[0], block[2])):
                buffers.append([
                    new(s, (2, number, i), WINDOW)
                    for i, s in enumerate(scatter_buffers(size, order, (nj, block[1], width)))])
                count += copies_of(order, size)
            places.append((grad, landing, buffers))
        plan.append(places)
    vmem, hbm = pl.BlockSpec(memory_space=pltpu.VMEM), pl.BlockSpec(memory_space=pl.ANY)
    slots = {"active": 1, "gh": 1, "packed": 1, "h": 1, "slope": 1, "n": 3, "mixed": 2, "logsum": 1}
    return pl.pallas_call(
        functools.partial(scatter_kernel, dp_size, fsdp_size, chunks, len(owned), plan, spans),
        out_shape=[jax.ShapeDtypeStruct(shape, F32) for shape in (*owned, (T, D), near.shape)],
        in_specs=[hbm] * 16 + [vmem] * 7,
        out_specs=[vmem] * (len(owned) + 1) + [hbm],
        scratch_shapes=[
            pltpu.VMEM((slots.get(name, factors[name].shape[0]),) + factors[name].shape[1:], factors[name].dtype)
            for name in FACTORS
        ] + [
            pltpu.VMEM((T, D), BF16), pltpu.VMEM((count_near * length, 2 * D), BF16), pltpu.VMEM((8, D, D), BF16),
            pltpu.VMEM((T, D), BF16), pltpu.VMEM((T, D), F32), pltpu.VMEM((24, D), F32), pltpu.VMEM(vec_up.shape, F32),
            pltpu.VMEM((T, 3 * D), BF16), pltpu.VMEM((T, T), jnp.int32), pltpu.VMEM(whole + (1, 32, 128), BF16), pltpu.VMEM((2, length, D), F32),
        ] + shapes + [
            pltpu.SemaphoreType.DMA((len(ORDER) + len(LATER),)),
            pltpu.SemaphoreType.DMA((21,)),
            pltpu.SemaphoreType.DMA,
            pltpu.SemaphoreType.DMA((count,)),
            pltpu.SemaphoreType.DMA((count,)),
        ],
        compiler_params=pltpu.CompilerParams(
            collective_id=collective_id, has_side_effects=True, vmem_limit_bytes=VMEM_MOST),
        name="scatter_gradients",
    )(*[factors[name] for name in FACTORS], *weights, g, near, near_tokens, rows, tokens, segment_ids, vec, vec_up)


PLACES = ((0, 0), (0, 3), (0, 4), (0, 5), (0, 7), (1, 0), (2, 0), (3, 0), (3, 3), (4, 0), (5, 0))


def chunk_table(D, part, long):
    table = [((0, 0, part, i * 2 * D, 2 * D),) for i in range(4)]
    for first in (1, 3):
        if first == 3:
            table += [((3, 0, part, i * 2 * D, 2 * D),) for i in range(2)]
        table += [((first + first // 3, 0, part, i * 2 * D, 2 * D),) for i in range(2)]
        table += [((first + first // 3 + 1, i * long // 2, long // 2, 0, D),) for i in range(2)]
    table[0] += ((6, 0, 32, 0, 128),)
    return table


def local(mesh_shape, *arrays):
    (tokens, segment_ids, neighbours, neighbour_ids, neighbour_tokens, gains_one, biases_one, w_qkv_one, w_out_one,
     w_cross_q, w_cross_kv, w_cross_out, w_up_one, bias_up_one, w_down_one, gains_two, biases_two, w_qkv_two,
     w_out_two, w_up_two, bias_up_two, w_down_two, cotangent) = arrays
    row_count, D = tokens.shape
    FF = w_up_one.shape[1]
    devices = mesh_shape[0] * mesh_shape[1]
    part = D // devices
    quarter = FF // D
    vectors = [gains_one, biases_one, gains_two, biases_two]
    shards = [w_qkv_one, w_out_one, w_cross_q, w_cross_kv, w_cross_out, w_up_one, w_down_one, w_qkv_two, w_out_two,
              w_up_two, w_down_two]
    kernels = part % 8 == 0
    table = chunk_table(D, part, w_down_one.shape[0])
    store_count = neighbours.shape[0]
    spans = neighbour_ids.shape[1]
    near_index = neighbour_ids.reshape(-1) % store_count
    if kernels:
        ups = [bias_up_one.reshape(1, -1), bias_up_two.reshape(1, -1)]
        wholes, (out, h, rows, near_tokens), saved = gather_and_run(
            mesh_shape, shards, tuple((w, c * D) for w, c in PLACES), vectors + ups, table, tokens, segment_ids,
            near_index, neighbours, neighbour_tokens, spans, 1)
        wholes = [w.reshape(-1, w.shape[-1]) for w in wholes]
        (gradient, vec, vec_up), made = run_backward(cotangent, rows, h, saved["slope"], *wholes[4:6])
        owned = [(w.shape[0] // devices, w.shape[1]) for w in wholes] + [(32, 128)]
        *owned, gradient, grad_neighbours = scatter_all(
            mesh_shape, {**saved, **made, "h": h}, (wholes[0], wholes[3], wholes[1], wholes[2]), gradient,
            saved["near"].reshape(neighbours.shape), near_tokens, rows,
            tokens, segment_ids, vec, vec_up, spans, owned, table[::-1], 2)
    else:
        small = jnp.concatenate(vectors + [bias_up_one.reshape(-1, part), bias_up_two.reshape(-1, part)])
        small = jnp.pad(small, ((0, -small.shape[0] % 32), (0, -part % 128)))
        sides = [[] for _ in range(6)]
        for shard, (which, _) in zip(shards, PLACES):
            sides[which].append(shard)
        shards = [jnp.concatenate(side, axis=1) for side in sides] + [small]
        *wholes, smalls = [lax.all_gather(s, ("dp", "fsdp"), axis=0, tiled=True) for s in shards]
        smalls = smalls.reshape(devices, -1, smalls.shape[-1])[:, :, :part]
        rows = smalls[:, :21].transpose(1, 0, 2).reshape(21, D)
        bias_up = [smalls[:, 21 + i * quarter:21 + (i + 1) * quarter].reshape(FF) for i in range(2)]
        rows = jnp.pad(rows.astype(F32), ((0, 3), (0, 0)))
        bias_up = jnp.pad(jnp.stack(bias_up).astype(F32), ((0, 6), (0, 0)))
        out, gradient, grad_neighbours, *grads, vectors, vectors_up = run_blocks(
            tokens, cotangent, segment_ids, neighbours, near_index, neighbour_tokens, spans, rows, bias_up, wholes)
        vectors = vectors[:21].reshape(21, devices, part).transpose(1, 0, 2)
        ups = vectors_up[:2].reshape(2, devices, quarter * part).transpose(1, 0, 2)
        vectors = [jnp.pad(v, ((0, 0), (0, 0), (0, 128 - v.shape[2]))) for v in (vectors, ups)]
        vectors = jnp.pad(jnp.concatenate(vectors, axis=1), ((0, 0), (0, 9), (0, 0)))
        grads.append(vectors.reshape(-1, 128).astype(BF16))
        owned = [lax.psum_scatter(g.astype(F32), ("dp", "fsdp"), scatter_dimension=0, tiled=True) for g in grads]
        grad_neighbours = jnp.take(grad_neighbours, near_index, axis=0)
    *split, out, gradient, grad_neighbours = split_gradients(
        owned, out, gradient, grad_neighbours, near_index, D, quarter, part)
    split[8], split[15] = split[8].reshape(-1), split[15].reshape(-1)
    return (out, gradient, grad_neighbours, *split)


def solution(mesh):
    in_specs = (
        P(("dp", "fsdp"), None),
        P(("dp", "fsdp"), None),
        P(("dp", "fsdp"), None, None),
        P(("dp", "fsdp"), None, None),
        P(("dp", "fsdp"), None),
        P(None, ("dp", "fsdp")),
        P(None, ("dp", "fsdp")),
        P(("dp", "fsdp"), None),
        P(("dp", "fsdp"), None),
        P(("dp", "fsdp"), None),
        P(("dp", "fsdp"), None),
        P(("dp", "fsdp"), None),
        P(("dp", "fsdp"), None),
        P(("dp", "fsdp")),
        P(("dp", "fsdp"), None),
        P(None, ("dp", "fsdp")),
        P(None, ("dp", "fsdp")),
        P(("dp", "fsdp"), None),
        P(("dp", "fsdp"), None),
        P(("dp", "fsdp"), None),
        P(("dp", "fsdp")),
        P(("dp", "fsdp"), None),
        P(("dp", "fsdp"), None),
    )
    out_specs = (
        P(("dp", "fsdp"), None),
        P(("dp", "fsdp"), None),
        P(("dp", "fsdp"), None, None),
        P(None, ("dp", "fsdp")),
        P(None, ("dp", "fsdp")),
        P(("dp", "fsdp"), None),
        P(("dp", "fsdp"), None),
        P(("dp", "fsdp"), None),
        P(("dp", "fsdp"), None),
        P(("dp", "fsdp"), None),
        P(("dp", "fsdp"), None),
        P(("dp", "fsdp")),
        P(("dp", "fsdp"), None),
        P(None, ("dp", "fsdp")),
        P(None, ("dp", "fsdp")),
        P(("dp", "fsdp"), None),
        P(("dp", "fsdp"), None),
        P(("dp", "fsdp"), None),
        P(("dp", "fsdp")),
        P(("dp", "fsdp"), None),
    )
    return jax.shard_map(
        functools.partial(local, (mesh.shape["dp"], mesh.shape["fsdp"])), mesh=mesh, in_specs=in_specs, out_specs=out_specs, check_vma=False)
```
